32 devices in a mesh: docs: 2 (over core), blk: 16 (over z, y, x).
Axes of the slice: x: 2, y: 2, z: 4, core: 2. Of those that a mesh axis runs over, the one named last changes fastest.
Arguments:
- tokens: float32 [8, 2048, 512], P('docs', 'blk'), may hold values from -6 to 6
- query_weight: bfloat16 [512, 512], replicated, may hold values from -0.25 to 0.25
- query_bias: bfloat16 [512], replicated, may hold values from -3 to 3
- key_weight: bfloat16 [512, 512], replicated, may hold values from -0.25 to 0.25
- value_weight: bfloat16 [512, 512], replicated, may hold values from -0.25 to 0.25
- value_bias: bfloat16 [512], replicated, may hold values from -0.119628906 to 0.119628906
- out_weight: bfloat16 [512, 512], replicated, may hold values from -6 to 6
- out_bias: bfloat16 [512], replicated, may hold values from -1.796875 to 1.796875
- first_gain: bfloat16 [512], replicated, may hold values from 0.5 to 1.5
- first_shift: bfloat16 [512], replicated, may hold values from -1.796875 to 1.796875
- up_weight: bfloat16 [512, 2048], replicated, may hold values from -0.25 to 0.25
- up_bias: bfloat16 [2048], replicated, may hold values from -3 to 3
- down_weight: bfloat16 [2048, 512], replicated, may hold values from -0.125 to 0.125
- down_bias: bfloat16 [512], replicated, may hold values from -1.796875 to 1.796875
- second_gain: bfloat16 [512], replicated, may hold values from 0.5 to 1.5
- second_shift: bfloat16 [512], replicated, may hold values from -1.796875 to 1.796875
- cotangent: float32 [8, 2048, 512], P('docs', 'blk'), may hold values from -6 to 6
- lengths: int32 [8], P('docs'), may hold values from 512 to 2048, as said below
Outputs:
- output: float32 [8, 2048, 512], P('docs', 'blk')
- tokens_grad: float32 [8, 2048, 512], P('docs', 'blk')
- query_dweight: float32 [512, 512], replicated
- query_dbias: float32 [512], replicated
- key_dweight: float32 [512, 512], replicated
- value_dweight: float32 [512, 512], replicated
- value_dbias: float32 [512], replicated
- out_dweight: float32 [512, 512], replicated
- out_dbias: float32 [512], replicated
- first_dgain: float32 [512], replicated
- first_dshift: float32 [512], replicated
- up_dweight: float32 [512, 2048], replicated
- up_dbias: float32 [2048], replicated
- down_dweight: float32 [2048, 512], replicated
- down_dbias: float32 [512], replicated
- second_dgain: float32 [512], replicated
- second_dshift: float32 [512], replicated
The draws below stay inside these ranges and needn't reach their ends.
Inputs may be any that keep to these rules, and one draw needn't show every extreme that they name: `lengths`: slots are taken 4 at a time as one bucket; in every bucket at least one document has length 2048.
All inputs are finite; a program needn't handle non-finite values.
Results may differ from the reference program's by a relative error of at most 0.014.
The reference program's roundings to bfloat16 on the way count: a program that leaves them out, or rounds other values in their place, can miss the bound.
Values may be sent and summed in bfloat16 or wider, within the bound.
A program may use at most 384 MiB of HBM per device.

```python
import math
import jax
import jax.numpy as jnp
from jax import lax

D = 512
H = 8
HD = 64
FF = 2048
SEQS = 4
LEN = 2048
DOCS_ALL = 8


def draw_lengths(key, part):
    key = jax.random.fold_in(key, 17)
    base_key, pick_key = jax.random.split(key)
    groups = DOCS_ALL // SEQS
    drawn = jax.random.randint(base_key, (groups, SEQS), LEN // 4, LEN + 1)
    chosen = jax.random.randint(pick_key, (groups, 1), 0, SEQS)
    slot_ids = jnp.arange(SEQS, dtype=jnp.int32)[None, :]
    return jnp.where(slot_ids == chosen, LEN, drawn).reshape(groups * SEQS).astype(jnp.int32)


def steps_of(own_key, shape, shards, low, high):
    factor_of = 1.0
    for position, blocks in shards:
        steps = jax.random.uniform(jax.random.fold_in(jax.random.fold_in(own_key, 6), position), (blocks,), jnp.float32, low / len(shards), high / len(shards))
        factor_of = factor_of * jnp.repeat(jnp.exp(steps), shape[position] // blocks).reshape((-1,) + (1,) * (len(shape) - 1 - position))
    return factor_of


def gaussian(rng, dims, width, reach, cuts=(), kind=jnp.bfloat16):
    array = jax.random.normal(rng, dims, jnp.float32) * width
    if len(cuts) > 0:
        array = steps_of(rng, dims, cuts, -0.22, 0.18) * array
    return jnp.clip(array, min=-reach, max=reach).astype(kind)


def setup_inputs(seed: int = 0) -> dict:
    streams_of = jax.random.split(jax.random.key(seed), 19)
    tokens = gaussian(streams_of[0], (DOCS_ALL, LEN, D), 1.0, 6.0, ((0, 2), (1, 16)), jnp.float32)
    query_weight = gaussian(streams_of[1], (D, D), D ** -0.5, 0.25)
    query_bias = gaussian(streams_of[2], (D,), 0.5, 3.0)
    key_weight = gaussian(streams_of[3], (D, D), D ** -0.5, 0.25)
    value_weight = gaussian(streams_of[4], (D, D), D ** -0.5, 0.25)
    value_bias = gaussian(streams_of[5], (D,), 0.02, 0.119628906)
    out_weight = gaussian(streams_of[6], (D, D), ((LEN // 4) ** 0.5 * D ** -0.5), 6.0)
    out_bias = gaussian(streams_of[7], (D,), 0.3, 1.796875)
    first_gain = jnp.clip(1.0 + 0.1 * jax.random.normal(streams_of[8], (D,), jnp.float32), 0.5, 1.5).astype(jnp.bfloat16)
    first_shift = gaussian(streams_of[9], (D,), 0.3, 1.796875)
    up_weight = gaussian(streams_of[10], (D, FF), D ** -0.5, 0.25)
    up_bias = gaussian(streams_of[11], (FF,), 0.5, 3.0)
    down_weight = gaussian(streams_of[12], (FF, D), FF ** -0.5, 0.125)
    down_bias = gaussian(streams_of[13], (D,), 0.3, 1.796875)
    second_gain = jnp.clip(1.0 + 0.1 * jax.random.normal(streams_of[14], (D,), jnp.float32), 0.5, 1.5).astype(jnp.bfloat16)
    second_shift = gaussian(streams_of[15], (D,), 0.3, 1.796875)
    cotangent = gaussian(streams_of[16], (DOCS_ALL, LEN, D), 1.0, 6.0, ((0, 2), (1, 16)), jnp.float32)
    lengths = draw_lengths(jax.random.fold_in(streams_of[18], 71), 0)
    return {"tokens": tokens, "query_weight": query_weight, "query_bias": query_bias, "key_weight": key_weight, "value_weight": value_weight, "value_bias": value_bias, "out_weight": out_weight, "out_bias": out_bias, "first_gain": first_gain, "first_shift": first_shift, "up_weight": up_weight, "up_bias": up_bias, "down_weight": down_weight, "down_bias": down_bias, "second_gain": second_gain, "second_shift": second_shift, "cotangent": cotangent, "lengths": lengths}


@jax.custom_vjp
def low(v):
    return lax.optimization_barrier(v.astype(jnp.bfloat16)).astype(jnp.float32)

@jax.custom_vjp
def low_back(v):
    return v

def low_keep(v):
    return (low(v), None)

def low_pass(kept, grad):
    return (grad,)

def back_keep(v):
    return (v, None)

def back_low(kept, grad):
    return (low(grad),)
low.defvjp(low_keep, low_pass)
low_back.defvjp(back_keep, back_low)

def matmul(left, right):
    return jnp.dot(left, right, precision=lax.Precision.HIGHEST, preferred_element_type=jnp.float32)

def layer_norm(summed, gain, shift):
    centred = summed - lax.optimization_barrier(jnp.mean(summed, axis=-1, keepdims=True))
    variance = lax.optimization_barrier(jnp.mean(centred * centred, axis=-1, keepdims=True))
    return centred * lax.rsqrt(variance + 1e-05) * gain + shift

def attend_block(query_rows, all_keys, all_values, key_mask):
    raw_scores = jnp.einsum('rhd,lhd->hrl', query_rows, all_keys, precision=lax.Precision.HIGHEST) * HD ** (-0.5)
    raw_scores = low_back(raw_scores)
    masked = jnp.where(key_mask[None, None, :], raw_scores, -1e+30)
    weights = low(jax.nn.softmax(masked, axis=-1))
    return jnp.einsum('hrl,lhd->rhd', weights, all_values, precision=lax.Precision.HIGHEST)

def document(tokens_doc, length, params):
    query_weight, query_bias, key_weight, value_weight, value_bias, out_weight, out_bias, first_gain, first_shift, up_weight, up_bias, down_weight, down_bias, second_gain, second_shift = params
    tokens_low = low(tokens_doc)
    query = low(low_back(matmul(tokens_low, query_weight) + query_bias))
    key_rows = low(low_back(matmul(tokens_low, key_weight)))
    value_rows = low(low_back(matmul(tokens_low, value_weight) + value_bias))
    key_mask = jnp.arange(LEN, dtype=jnp.int32) < length
    block_rows = math.gcd(LEN, 512)
    query_blocks = query.reshape(LEN // block_rows, block_rows, H, HD)
    all_keys = key_rows.reshape(LEN, H, HD)
    all_values = value_rows.reshape(LEN, H, HD)
    attend = jax.checkpoint(lambda block: attend_block(block, all_keys, all_values, key_mask))
    attended = lax.map(attend, query_blocks).reshape(LEN, D)
    attended = low(low_back(attended))
    branch = low_back(matmul(attended, out_weight) + out_bias)
    hidden = layer_norm(tokens_doc + branch, first_gain, first_shift)
    inner = low_back(matmul(low(hidden), up_weight) + up_bias)
    activated = low(jax.nn.gelu(inner, approximate=True))
    ffn = low_back(matmul(activated, down_weight) + down_bias)
    return layer_norm(tokens_doc + hidden + ffn, second_gain, second_shift)

def reference(tokens, query_weight, query_bias, key_weight, value_weight, value_bias, out_weight, out_bias, first_gain, first_shift, up_weight, up_bias, down_weight, down_bias, second_gain, second_shift, cotangent, lengths):
    params = tuple((weight.astype(jnp.float32) for weight in (query_weight, query_bias, key_weight, value_weight, value_bias, out_weight, out_bias, first_gain, first_shift, up_weight, up_bias, down_weight, down_bias, second_gain, second_shift)))

    def one_doc(carry, item):
        tokens_doc, cot_doc, length = item
        result, pull = jax.vjp(lambda rows, weights: document(rows, length, weights), tokens_doc, params)
        row_valid = (jnp.arange(LEN, dtype=jnp.int32) < length).astype(jnp.float32)
        grad_rows, grad_params = pull(cot_doc * row_valid[:, None])
        carry = jax.tree.map(jnp.add, carry, grad_params)
        return (carry, (result, grad_rows))
    zeros = jax.tree.map(jnp.zeros_like, params)
    grads, (output, tokens_grad) = lax.scan(one_doc, zeros, (tokens, cotangent, lengths))
    return (output, tokens_grad, grads[0], grads[1], grads[2], grads[3], grads[4], grads[5], grads[6], grads[7], grads[8], grads[9], grads[10], grads[11], grads[12], grads[13], grads[14])
```

```python
import functools

import jax
import jax.numpy as jnp
from jax import lax
from jax.experimental import pallas as pl
from jax.experimental.pallas import tpu as pltpu
from jax.sharding import PartitionSpec as P

HD = 64
LANES = 128
EPS = 1e-05
MASKED = -1e30
F32 = jnp.float32
BF16 = jnp.bfloat16
VMEM = pl.BlockSpec(memory_space=pltpu.VMEM)
SMEM = pl.BlockSpec(memory_space=pltpu.SMEM)
MESH = pl.DeviceIdType.MESH
VMEM_LIMIT = 60 * 1024 * 1024


def mm(left, right):
    return jnp.dot(left, right, preferred_element_type=F32)


def mm_nt(left, right):
    return lax.dot_general(left, right, (((1,), (1,)), ((), ())), preferred_element_type=F32)


def mm_tn(left, right):
    return lax.dot_general(left, right, (((0,), (0,)), ((), ())), preferred_element_type=F32)


def params(collective_id=None):
    if collective_id is None:
        return pltpu.CompilerParams(vmem_limit_bytes=VMEM_LIMIT)
    return pltpu.CompilerParams(
        vmem_limit_bytes=VMEM_LIMIT, collective_id=collective_id, has_side_effects=True
    )


def greet(peers):
    barrier = pltpu.get_barrier_semaphore()
    for peer in peers:
        pl.semaphore_signal(barrier, inc=1, device_id=peer, device_id_type=MESH)
    pl.semaphore_wait(barrier, len(peers))


def send_to(src, dst, send_sem, recv_sem, peer):
    return pltpu.make_async_remote_copy(
        src_ref=src, dst_ref=dst, send_sem=send_sem, recv_sem=recv_sem,
        device_id=peer, device_id_type=MESH,
    )


def gather_kernel(slots, group, tok_ref, out_ref, low, send_a, recv_a, send_b, recv_b):
    me = lax.axis_index("blk")
    plane, member = me // group, me % group
    planes = [lax.rem(plane + k, slots) for k in range(1, slots)]
    members = [lax.rem(member + k, group) for k in range(1, group)]
    greet([{"blk": p * group + member} for p in planes]
          + [{"blk": plane * group + m} for m in members])
    low[...] = tok_ref[...].astype(BF16)
    first = []
    for k in range(1, slots):
        target = planes[k - 1]
        copy = send_to(low.at[target], out_ref.at[me], send_a.at[k], recv_a.at[k],
                       {"blk": target * group + member})
        copy.start()
        first.append(copy)
    out_ref[me] = low[plane]
    second = []
    for k in range(slots):
        source = lax.rem(plane + slots - k, slots)
        block = source * group + member
        if k > 0:
            send_to(low.at[plane], out_ref.at[block], send_a.at[k], recv_a.at[k],
                    {"blk": block}).wait_recv()
        for j in range(1, group):
            copy = send_to(out_ref.at[block], out_ref.at[block], send_b.at[k, j], recv_b.at[k, j],
                           {"blk": plane * group + members[j - 1]})
            copy.start()
            second.append(copy)
    for k in range(slots):
        source = lax.rem(plane + slots - k, slots)
        for j in range(1, group):
            block = source * group + lax.rem(member + group - j, group)
            send_to(out_ref.at[block], out_ref.at[block], send_b.at[k, j], recv_b.at[k, j],
                    {"blk": plane * group + members[j - 1]}).wait_recv()
    for copy in first + second:
        copy.wait_send()


def gather_tokens(tokens, blocks, collective_id):
    slots, rows, width = tokens.shape
    group = blocks // slots
    return pl.pallas_call(
        functools.partial(gather_kernel, slots, group),
        out_shape=jax.ShapeDtypeStruct((blocks, rows, width), BF16),
        in_specs=[VMEM],
        out_specs=VMEM,
        scratch_shapes=[
            pltpu.VMEM((slots, rows, width), BF16),
            pltpu.SemaphoreType.DMA((slots,)),
            pltpu.SemaphoreType.DMA((slots,)),
            pltpu.SemaphoreType.DMA((slots, group)),
            pltpu.SemaphoreType.DMA((slots, group)),
        ],
        compiler_params=params(collective_id),
    )(tokens)


def exchange_kernel(blocks, src_ref, out_ref, send_sem, recv_sem):
    me = lax.axis_index("blk")
    peers = [lax.rem(me + k, blocks) for k in range(1, blocks)]
    greet([{"blk": p} for p in peers])
    copies = []
    for k in range(1, blocks):
        copy = send_to(src_ref.at[peers[k - 1]], out_ref.at[me], send_sem.at[k], recv_sem.at[k],
                       {"blk": peers[k - 1]})
        copy.start()
        copies.append(copy)
    out_ref[me] = src_ref[me]
    for k in range(1, blocks):
        source = lax.rem(me + blocks - k, blocks)
        send_to(src_ref.at[me], out_ref.at[source], send_sem.at[k], recv_sem.at[k],
                {"blk": source}).wait_recv()
    for copy in copies:
        copy.wait_send()


def exchange(array, collective_id):
    blocks = array.shape[0]
    return pl.pallas_call(
        functools.partial(exchange_kernel, blocks),
        out_shape=jax.ShapeDtypeStruct(array.shape, array.dtype),
        in_specs=[VMEM],
        out_specs=VMEM,
        scratch_shapes=[pltpu.SemaphoreType.DMA((blocks,)), pltpu.SemaphoreType.DMA((blocks,))],
        compiler_params=params(collective_id),
    )(array)


def forward_kernel(group, q_block, tok_ref, w_ref, b_ref, len_ref,
                   att_ref, q_ref, k_ref, v_ref, o_ref, vt):
    total, width = w_ref.shape[1] // 3, w_ref.shape[0]
    heads = total // HD
    length_all = tok_ref.shape[0]
    plane = lax.axis_index("blk") // group
    doc_len = len_ref[plane]
    chunk = min(512, length_all)

    def project(step, carry):
        rows = pl.ds(step * chunk, chunk)
        qkv = mm(tok_ref[rows, :], w_ref[...]) + b_ref[...]
        lane = lax.broadcasted_iota(jnp.int32, (chunk, LANES), 1)
        row = step * chunk + lax.broadcasted_iota(jnp.int32, (chunk, LANES), 0)
        mask = jnp.where(row < doc_len, 0.0, MASKED)
        for h in range(heads):
            def part(which):
                cols = qkv[:, which * total + h * HD:which * total + (h + 1) * HD]
                return jnp.concatenate([cols, jnp.zeros_like(cols)], axis=1)
            q_ref[h, rows, :] = jnp.where(
                lane == HD, 1.0, part(0).astype(BF16).astype(F32) * (HD ** -0.5)).astype(BF16)
            k_ref[h, rows, :] = jnp.where(
                lane == HD, mask, jnp.where((lane > HD) & (lane < HD + 4), 1.0, part(1))).astype(BF16)
            v_rows = jnp.where((lane >= HD) & (lane < HD + 4), 1.0, part(2)).astype(BF16)
            v_ref[h, rows, :] = v_rows
            vt[h, :, rows] = v_rows.T
        return carry

    lax.fori_loop(0, length_all // chunk, project, 0)

    def block(step, carry):
        rows = pl.ds(step * q_block, q_block)
        for h in range(heads):
            scores = mm_nt(k_ref[h], q_ref[h, rows, :])
            top = jnp.max(scores, axis=0, keepdims=True)
            weights = jnp.exp(scores - top).astype(BF16)
            mixed = mm(vt[h], weights)
            denom = mixed[HD:HD + 1, :]
            scaled = mixed * (1.0 / denom)
            sub = lax.broadcasted_iota(jnp.int32, scaled.shape, 0)
            o_rows = jnp.where(sub == HD, top + jnp.log(denom), scaled).T
            o_ref[h, rows, :] = o_rows
            att_ref[rows, h * HD:(h + 1) * HD] = o_rows[:, :HD].astype(BF16)
        return carry

    lax.fori_loop(0, length_all // q_block, block, 0)


def attention_forward(tok_doc, weight, bias, lengths, group, q_block=256):
    length_all = tok_doc.shape[0]
    total = weight.shape[1] // 3
    heads = total // HD
    per_head = jax.ShapeDtypeStruct((heads, length_all, LANES), BF16)
    return pl.pallas_call(
        functools.partial(forward_kernel, group, q_block),
        out_shape=(
            jax.ShapeDtypeStruct((length_all, total), BF16),
            per_head, per_head, per_head,
            jax.ShapeDtypeStruct((heads, length_all, LANES), F32),
        ),
        in_specs=[VMEM, VMEM, VMEM, SMEM],
        out_specs=(VMEM,) * 5,
        scratch_shapes=[pltpu.VMEM((heads, LANES, length_all), BF16)],
        compiler_params=params(),
    )(tok_doc, weight, bias, lengths)


def three(value):
    high = value.astype(BF16).astype(F32)
    mid = (value - high).astype(BF16).astype(F32)
    return high, mid, value - high - mid


def backward_kernel(k_block, q_tile, q_ref, k_ref, v_ref, o_ref, g_ref,
                    gq_ref, gk_ref, gv_ref, qx, gx, qt, gt, gq_acc):
    heads, length_all, _ = q_ref.shape
    chunk = min(512, length_all)

    def prepare(step, carry):
        rows = pl.ds(step * chunk, chunk)
        lane = lax.broadcasted_iota(jnp.int32, (chunk, LANES), 1)
        for h in range(heads):
            g_rows = g_ref[rows, h * HD:(h + 1) * HD].astype(F32)
            g_rows = jnp.concatenate([g_rows, jnp.zeros_like(g_rows)], axis=1)
            o_rows = o_ref[h, rows, :]
            delta = jnp.sum(g_rows * o_rows, axis=1, keepdims=True)
            parts = three(-delta)
            ext = g_rows
            for i in range(3):
                ext = jnp.where(lane == HD + i, parts[i], ext)
            gx[h, rows, :] = ext.astype(BF16)
            gt[h, :, rows] = g_rows[:, :HD].T.astype(BF16)
            parts = three(-o_rows[:, HD:HD + 1])
            q_rows = q_ref[h, rows, :].astype(F32)
            ext = q_rows
            for i in range(3):
                ext = jnp.where(lane == HD + 1 + i, parts[i], ext)
            qx[h, rows, :] = ext.astype(BF16)
            qt[h, :, rows] = q_rows[:, :HD].T.astype(BF16)
        return carry

    lax.fori_loop(0, length_all // chunk, prepare, 0)
    gq_acc[...] = jnp.zeros_like(gq_acc)

    def block(step, carry):
        rows = pl.ds(step * k_block, k_block)
        for h in range(heads):
            k_rows, v_rows = k_ref[h, rows, :], v_ref[h, rows, :]
            gk = jnp.zeros((HD, k_block), F32)
            gv = jnp.zeros((HD, k_block), F32)
            for t in range(length_all // q_tile):
                tile = slice(t * q_tile, (t + 1) * q_tile)
                weights = jnp.exp(mm_nt(qx[h, tile, :], k_rows))
                centred = mm_nt(gx[h, tile, :], v_rows)
                g_scores = (weights * centred).astype(BF16)
                gv = gv + mm(gt[h, :, tile], weights.astype(BF16))
                gk = gk + mm(qt[h, :, tile], g_scores)
                gq_acc[h, tile, :] += mm(g_scores, k_rows)
            gk_ref[rows, h * HD:(h + 1) * HD] = gk.T.astype(BF16)
            gv_ref[rows, h * HD:(h + 1) * HD] = gv.T.astype(BF16)
        return carry

    lax.fori_loop(0, length_all // k_block, block, 0)

    def finish(step, carry):
        rows = pl.ds(step * chunk, chunk)
        for h in range(heads):
            gq_ref[rows, h * HD:(h + 1) * HD] = (
                gq_acc[h, rows, :HD] * (HD ** -0.5)).astype(BF16)
        return carry

    lax.fori_loop(0, length_all // chunk, finish, 0)


def attention_backward(q, k, v, o, g, k_block=256, q_tile=512):
    heads, length_all, _ = q.shape
    out = jax.ShapeDtypeStruct((length_all, heads * HD), BF16)
    return pl.pallas_call(
        functools.partial(backward_kernel, k_block, q_tile),
        out_shape=(out,) * 3,
        in_specs=[VMEM] * 5,
        out_specs=(VMEM,) * 3,
        scratch_shapes=[
            pltpu.VMEM((heads, length_all, LANES), BF16),
            pltpu.VMEM((heads, length_all, LANES), BF16),
            pltpu.VMEM((heads, HD, length_all), BF16),
            pltpu.VMEM((heads, HD, length_all), BF16),
            pltpu.VMEM((heads, length_all, LANES), F32),
        ],
        compiler_params=params(),
    )(q, k, v, o, g)


def row_mean(value):
    return jnp.mean(value, axis=1, keepdims=True)


def col_sum(value):
    return jnp.sum(value, axis=0, keepdims=True)


def middle_kernel(group, tok_ref, att_in, cot_ref, len_ref, wo_ref, ob_ref, g1_ref, s1_ref,
                  up_ref, ub_ref, down_ref, db_ref, g2_ref, s2_ref,
                  out_ref, gz_ref, gatt_ref, dw_ref, small_ref,
                  att, act, slope, hid_t):
    slots, rows, width = tok_ref.shape
    count = slots * rows
    inner_width = up_ref.shape[1]
    part = width
    parts = inner_width // part
    me = lax.axis_index("blk")
    flat = tok_ref[...].reshape(count, width)
    cols = width // group
    for s in range(slots):
        for g in range(group):
            att[s * rows:(s + 1) * rows, g * cols:(g + 1) * cols] = att_in[s * group + g]
    gain1, gain2 = g1_ref[...], g2_ref[...]
    summed = flat + mm(att[...], wo_ref[...]) + ob_ref[...]
    centred = summed - row_mean(summed)
    rstd1 = lax.rsqrt(row_mean(centred * centred) + EPS)
    xhat1 = centred * rstd1
    hidden = xhat1 * gain1 + s1_ref[...]
    hidden_low = hidden.astype(BF16)
    hid_t[...] = hidden_low.T
    ffn = jnp.zeros((count, width), F32)
    for c in range(parts):
        span = slice(c * part, (c + 1) * part)
        inner = mm(hidden_low, up_ref[:, span]) + ub_ref[:, span]
        square = inner * inner
        slope_in = 0.7978845608 * (1.0 + (3 * 0.044715) * square)
        tanh = jnp.tanh(inner * (0.7978845608 * (1.0 + 0.044715 * square)))
        half = 0.5 * (1.0 + tanh)
        slope[:, span] = half + (0.5 * inner) * ((1.0 - tanh * tanh) * slope_in)
        low = (inner * half).astype(BF16)
        act[:, span] = low
        ffn = ffn + mm(low, down_ref[span, :])
    summed = flat + hidden + ffn + db_ref[...]
    centred = summed - row_mean(summed)
    rstd2 = lax.rsqrt(row_mean(centred * centred) + EPS)
    xhat2 = centred * rstd2
    out_ref[...] = (xhat2 * gain2 + s2_ref[...]).reshape(slots, rows, width)
    position = me * rows + lax.broadcasted_iota(jnp.int32, (rows, width), 0)
    g_out = jnp.concatenate(
        [jnp.where(position < len_ref[s], cot_ref[s], 0.0) for s in range(slots)], axis=0)
    small_ref[...] = jnp.zeros_like(small_ref)
    small_ref[0:1, :] = col_sum(g_out * xhat2)
    small_ref[1:2, :] = col_sum(g_out)
    scaled = g_out * gain2
    g_z2 = rstd2 * (scaled - row_mean(scaled) - xhat2 * row_mean(scaled * xhat2))
    g_ffn = g_z2.astype(BF16)
    small_ref[2:3, :] = col_sum(g_ffn.astype(F32))
    g_hidden = g_z2
    for c in range(parts):
        span = slice(c * part, (c + 1) * part)
        dw_ref[span, :] = mm_tn(act[:, span], g_ffn)
        g_inner32 = mm_nt(g_ffn, down_ref[span, :]) * slope[:, span]
        g_inner = g_inner32.astype(BF16)
        small_ref[6 + c:7 + c, :] = col_sum(g_inner.astype(F32))
        dw_ref[inner_width + c * part:inner_width + (c + 1) * part, :] = mm(hid_t[...], g_inner)
        g_hidden = g_hidden + mm_nt(g_inner, up_ref[:, span])
    small_ref[3:4, :] = col_sum(g_hidden * xhat1)
    small_ref[4:5, :] = col_sum(g_hidden)
    scaled = g_hidden * gain1
    g_z1 = rstd1 * (scaled - row_mean(scaled) - xhat1 * row_mean(scaled * xhat1))
    g_branch = g_z1.astype(BF16)
    small_ref[5:6, :] = col_sum(g_branch.astype(F32))
    dw_ref[2 * inner_width:, :] = mm_tn(att[...], g_branch)
    gz_ref[...] = g_z1 + g_z2
    g_att = mm_nt(g_branch, wo_ref[...]).astype(BF16)
    for s in range(slots):
        for g in range(group):
            gatt_ref[s * group + g] = g_att[s * rows:(s + 1) * rows, g * cols:(g + 1) * cols]


def middle(group, tokens, att_in, cotangent, lengths, *weights):
    slots, rows, width = tokens.shape
    count = slots * rows
    inner_width = weights[4].shape[1]
    return pl.pallas_call(
        functools.partial(middle_kernel, group),
        out_shape=(
            jax.ShapeDtypeStruct((slots, rows, width), F32),
            jax.ShapeDtypeStruct((count, width), F32),
            jax.ShapeDtypeStruct(att_in.shape, BF16),
            jax.ShapeDtypeStruct((2 * inner_width + width, width), F32),
            jax.ShapeDtypeStruct((16, width), F32),
        ),
        in_specs=[VMEM, VMEM, VMEM, SMEM] + [VMEM] * 10,
        out_specs=(VMEM,) * 5,
        scratch_shapes=[
            pltpu.VMEM((count, width), BF16),
            pltpu.VMEM((count, inner_width), BF16),
            pltpu.VMEM((count, inner_width), F32),
            pltpu.VMEM((width, count), BF16),
        ],
        compiler_params=params(),
    )(tokens, att_in, cotangent, lengths, *weights)


def final_kernel(group, tok_ref, g3_ref, gz_ref, wq_ref, wk_ref, wv_ref, grad_ref, dw_ref, small_ref,
                 low_t, part):
    slots, rows, width = tok_ref.shape
    count = slots * rows
    cols = width // group
    low_t[...] = tok_ref[...].reshape(count, width).astype(BF16).T
    total = gz_ref[...]
    small_ref[...] = jnp.zeros_like(small_ref)
    for i, w_ref in enumerate((wq_ref, wk_ref, wv_ref)):
        for s in range(slots):
            for g in range(group):
                part[s * rows:(s + 1) * rows, g * cols:(g + 1) * cols] = (
                    g3_ref[s * group + g, i * rows:(i + 1) * rows, :])
        low = part[...]
        total = total + mm_nt(low, w_ref[...])
        dw_ref[i * width:(i + 1) * width, :] = mm(low_t[...], low)
        small_ref[i:i + 1, :] = col_sum(low.astype(F32))
    grad_ref[...] = total.reshape(slots, rows, width)


def final(group, tokens, g3, gz, wq, wk, wv):
    slots, rows, width = tokens.shape
    count = slots * rows
    return pl.pallas_call(
        functools.partial(final_kernel, group),
        out_shape=(
            jax.ShapeDtypeStruct((slots, rows, width), F32),
            jax.ShapeDtypeStruct((3 * width, width), F32),
            jax.ShapeDtypeStruct((8, width), F32),
        ),
        in_specs=[VMEM] * 6,
        out_specs=(VMEM,) * 3,
        scratch_shapes=[pltpu.VMEM((width, count), BF16), pltpu.VMEM((count, width), BF16)],
        compiler_params=params(),
    )(tokens, g3, gz, wq, wk, wv)


def stages_of(order, rows):
    out = []
    for axis, bit in order:
        halved = rows % 32 == 0
        out.append((axis, bit, halved))
        rows = rows // 2 if halved else rows
    return out


def orders(docs, blocks, count):
    low = [("docs", 1)]
    ring = [("blk", 1 << i) for i in range(blocks.bit_length() - 1)]
    rest = [("docs", 1 << i) for i in range(1, docs.bit_length() - 1)]
    return [low + ring[k % len(ring):] + ring[:k % len(ring)] + rest for k in range(count)]


def reduce_kernel(docs, blocks, chunks, acc_in, small_in, out_ref, small_out, acc, sent, came, small_sent,
                  small_came, send_sem, recv_sem, small_send, small_recv):
    size = acc_in.shape[0] // chunks
    me = {"docs": lax.axis_index("docs"), "blk": lax.axis_index("blk")}
    plans = [stages_of(order, size) for order in orders(docs, blocks, chunks)]
    count = len(plans[0])

    def peer(axis, bit):
        mine = me[axis]
        on = lax.rem(mine // bit, 2)
        return {axis: mine + bit - 2 * bit * on}, on

    greet([peer(axis, bit)[0] for axis, bit, _ in plans[0]])
    tile = 16

    def rows_loop(rows, body):
        step = next(t for t in (96, 64, 48, 32, 16) if rows % t == 0)

        def run(i, carry):
            body(i * step, step)
            return carry
        lax.fori_loop(0, rows // step, run, 0)

    def at(offset, i, step):
        return pl.ds(pl.multiple_of(offset + i, tile), step)

    offsets = [c * size for c in range(chunks)]
    lengths = [size] * chunks
    kept = [[] for _ in range(chunks)]
    pending = []
    arrive = [0] * chunks
    small_sent[0] = small_in[...]
    source = [acc_in] * chunks

    for s in range(count):
        flying = []
        for c in range(chunks):
            axis, bit, halved = plans[c][s]
            to, on = peer(axis, bit)
            src = source[c]
            n = lengths[c] // 2 if halved else lengths[c]
            give = offsets[c] + (1 - on) * n if halved else offsets[c]
            keep = offsets[c] + on * n if halved else offsets[c]
            place = c * 2 * size + arrive[c]
            arrive[c] += n

            def pack(i, step, src=src, give=give, place=place):
                sent[at(place, i, step), :] = src[at(give, i, step), :].astype(BF16)
            rows_loop(n, pack)
            copy = send_to(sent.at[pl.ds(place, n)], came.at[pl.ds(place, n)],
                           send_sem.at[0, c, s], recv_sem.at[0, c, s], to)
            copy.start()
            flying.append((copy, c, n, keep, place, halved))
            pending.append(copy)
        axis, bit, _ = plans[0][s]
        tiny = send_to(small_sent.at[s], small_came.at[s], small_send.at[s], small_recv.at[s],
                       peer(axis, bit)[0])
        tiny.start()
        pending.append(tiny)
        for copy, c, n, keep, place, halved in flying:
            copy.wait_recv()
            src = source[c]

            def add(i, step, src=src, keep=keep, place=place, halved=halved):
                own = src[at(keep, i, step), :]
                if not halved:
                    own = own.astype(BF16).astype(F32)
                acc[at(keep, i, step), :] = own + came[at(place, i, step), :].astype(F32)
            rows_loop(n, add)
            source[c] = acc
            if halved:
                kept[c].append((s, offsets[c], lengths[c]))
            offsets[c], lengths[c] = keep, n
        tiny.wait_recv()
        total = small_sent[s] + small_came[s]
        if s + 1 < count:
            small_sent[s + 1] = total
        else:
            small_out[...] = total
    for c in range(chunks):
        def settle(i, step, offset=offsets[c]):
            out_ref[at(offset, i, step), :] = acc[at(offset, i, step), :].astype(BF16)
        rows_loop(lengths[c], settle)
    depth = max(len(k) for k in kept)
    for d in range(depth):
        flying = []
        for c in range(chunks):
            if not kept[c]:
                continue
            s, offset, length = kept[c].pop()
            axis, bit, _ = plans[c][s]
            to, on = peer(axis, bit)
            span = pl.ds(pl.multiple_of(offsets[c], tile), lengths[c])
            copy = send_to(out_ref.at[span], out_ref.at[span], send_sem.at[1, c, s],
                           recv_sem.at[1, c, s], to)
            copy.start()
            pending.append(copy)
            other = offset + (1 - on) * lengths[c]
            flying.append((c, s, to, other, lengths[c]))
            offsets[c], lengths[c] = offset, length
        for c, s, to, other, n in flying:
            span = pl.ds(pl.multiple_of(other, tile), n)
            send_to(out_ref.at[span], out_ref.at[span], send_sem.at[1, c, s],
                    recv_sem.at[1, c, s], to).wait_recv()
    for copy in pending:
        copy.wait_send()


def reduce_all(stacked, small, docs, blocks, chunks, collective_id):
    rows, width = stacked.shape
    count = len(orders(docs, blocks, 1)[0])
    return pl.pallas_call(
        functools.partial(reduce_kernel, docs, blocks, chunks),
        out_shape=(
            jax.ShapeDtypeStruct((rows, width), BF16),
            jax.ShapeDtypeStruct(small.shape, F32),
        ),
        in_specs=[VMEM, VMEM],
        out_specs=(VMEM, VMEM),
        scratch_shapes=[
            pltpu.VMEM((rows, width), F32),
            pltpu.VMEM((2 * rows, width), BF16),
            pltpu.VMEM((2 * rows, width), BF16),
            pltpu.VMEM((count,) + small.shape, F32),
            pltpu.VMEM((count,) + small.shape, F32),
            pltpu.SemaphoreType.DMA((2, chunks, count)),
            pltpu.SemaphoreType.DMA((2, chunks, count)),
            pltpu.SemaphoreType.DMA((count,)),
            pltpu.SemaphoreType.DMA((count,)),
        ],
        compiler_params=params(collective_id),
    )(stacked, small)


def device_program(docs, blocks, tokens, query_weight, query_bias, key_weight, value_weight, value_bias,
                   out_weight, out_bias, first_gain, first_shift, up_weight, up_bias, down_weight,
                   down_bias, second_gain, second_shift, cotangent, lengths):
    slots, rows, width = tokens.shape
    inner_width = up_weight.shape[1]
    group = blocks // slots
    cols = width // group
    length_all = rows * blocks
    member = lax.axis_index("blk") % group

    def own(weight):
        return lax.dynamic_slice_in_dim(weight, member * cols, cols, weight.ndim - 1)

    def row(vector):
        return vector.astype(F32)[None, :]

    weight = jnp.concatenate([own(query_weight), own(key_weight), own(value_weight)], axis=1)
    bias = jnp.concatenate([own(query_bias), jnp.zeros_like(query_bias[:cols]), own(value_bias)])
    tok_doc = gather_tokens(tokens, blocks, 0).reshape(length_all, width)
    att, q, k, v, o = attention_forward(tok_doc, weight, row(bias), lengths, group)
    att_in = exchange(att.reshape(blocks, rows, cols), 1)
    output, gz, g_att, dw_mid, small_mid = middle(
        group, tokens, att_in, cotangent, lengths, out_weight, row(out_bias), row(first_gain),
        row(first_shift), up_weight, row(up_bias), down_weight, row(down_bias), row(second_gain),
        row(second_shift))
    g_doc = exchange(g_att, 2).reshape(length_all, cols)
    gq, gk, gv = attention_backward(q, k, v, o, g_doc)
    g3 = jnp.concatenate([a.reshape(blocks, rows, cols) for a in (gq, gk, gv)], axis=1)
    g3 = exchange(g3, 3)
    tokens_grad, dw_qkv, small_qkv = final(group, tokens, g3, gz, query_weight, key_weight, value_weight)
    dw_mid, small_mid = reduce_all(dw_mid, small_mid, docs, blocks, 3, 4)
    dw_qkv, small_qkv = reduce_all(dw_qkv, small_qkv, docs, blocks, 1, 5)
    dw_mid, dw_qkv = dw_mid.astype(F32), dw_qkv.astype(F32)
    up_parts = [dw_mid[inner_width + i * width:inner_width + (i + 1) * width]
                for i in range(inner_width // width)]
    return (
        output,
        tokens_grad,
        dw_qkv[:width],
        small_qkv[0],
        dw_qkv[width:2 * width],
        dw_qkv[2 * width:],
        small_qkv[2],
        dw_mid[2 * inner_width:],
        small_mid[5],
        small_mid[3],
        small_mid[4],
        jnp.concatenate(up_parts, axis=1),
        small_mid[6:6 + inner_width // width].reshape(inner_width),
        dw_mid[:inner_width],
        small_mid[2],
        small_mid[0],
        small_mid[1],
    )


def solution(mesh):
    split = P("docs", "blk", None)
    return jax.shard_map(
        functools.partial(device_program, mesh.shape["docs"], mesh.shape["blk"]),
        mesh=mesh,
        in_specs=(split,) + (P(),) * 15 + (split, P("docs")),
        out_specs=(split, split) + (P(),) * 15,
        check_vma=False,
    )
```

```python
import functools

import jax
import jax.numpy as jnp
from jax import lax
from jax.experimental import pallas as pl
from jax.experimental.pallas import tpu as pltpu
from jax.sharding import PartitionSpec as P

HD = 64
LANES = 128
EPS = 1e-05
MASKED = -1e30
F32 = jnp.float32
BF16 = jnp.bfloat16
VMEM = pl.BlockSpec(memory_space=pltpu.VMEM)
SMEM = pl.BlockSpec(memory_space=pltpu.SMEM)
MESH = pl.DeviceIdType.MESH
VMEM_LIMIT = 60 * 1024 * 1024


def mm(left, right):
    return jnp.dot(left, right, preferred_element_type=F32)


def mm_nt(left, right):
    return lax.dot_general(left, right, (((1,), (1,)), ((), ())), preferred_element_type=F32)


def mm_tn(left, right):
    return lax.dot_general(left, right, (((0,), (0,)), ((), ())), preferred_element_type=F32)


def params(collective_id=None):
    if collective_id is None:
        return pltpu.CompilerParams(vmem_limit_bytes=VMEM_LIMIT)
    return pltpu.CompilerParams(
        vmem_limit_bytes=VMEM_LIMIT, collective_id=collective_id, has_side_effects=True
    )


def greet(peers):
    barrier = pltpu.get_barrier_semaphore()
    for peer in peers:
        pl.semaphore_signal(barrier, inc=1, device_id=peer, device_id_type=MESH)
    pl.semaphore_wait(barrier, len(peers))


def send_to(src, dst, send_sem, recv_sem, peer):
    return pltpu.make_async_remote_copy(
        src_ref=src, dst_ref=dst, send_sem=send_sem, recv_sem=recv_sem,
        device_id=peer, device_id_type=MESH,
    )


def gather_kernel(slots, group, tok_ref, out_ref, low, send_a, recv_a, send_b, recv_b):
    me = lax.axis_index("blk")
    plane, member = me // group, me % group
    planes = [lax.rem(plane + k, slots) for k in range(1, slots)]
    members = [lax.rem(member + k, group) for k in range(1, group)]
    greet([{"blk": p * group + member} for p in planes]
          + [{"blk": plane * group + m} for m in members])
    low[...] = tok_ref[...].astype(BF16)
    first = []
    for k in range(1, slots):
        target = planes[k - 1]
        copy = send_to(low.at[target], out_ref.at[me], send_a.at[k], recv_a.at[k],
                       {"blk": target * group + member})
        copy.start()
        first.append(copy)
    out_ref[me] = low[plane]
    second = []
    for k in range(slots):
        source = lax.rem(plane + slots - k, slots)
        block = source * group + member
        if k > 0:
            send_to(low.at[plane], out_ref.at[block], send_a.at[k], recv_a.at[k],
                    {"blk": block}).wait_recv()
        for j in range(1, group):
            copy = send_to(out_ref.at[block], out_ref.at[block], send_b.at[k, j], recv_b.at[k, j],
                           {"blk": plane * group + members[j - 1]})
            copy.start()
            second.append(copy)
    for k in range(slots):
        source = lax.rem(plane + slots - k, slots)
        for j in range(1, group):
            block = source * group + lax.rem(member + group - j, group)
            send_to(out_ref.at[block], out_ref.at[block], send_b.at[k, j], recv_b.at[k, j],
                    {"blk": plane * group + members[j - 1]}).wait_recv()
    for copy in first + second:
        copy.wait_send()


def gather_tokens(tokens, blocks, collective_id):
    slots, rows, width = tokens.shape
    group = blocks // slots
    return pl.pallas_call(
        functools.partial(gather_kernel, slots, group),
        out_shape=jax.ShapeDtypeStruct((blocks, rows, width), BF16),
        in_specs=[VMEM],
        out_specs=VMEM,
        scratch_shapes=[
            pltpu.VMEM((slots, rows, width), BF16),
            pltpu.SemaphoreType.DMA((slots,)),
            pltpu.SemaphoreType.DMA((slots,)),
            pltpu.SemaphoreType.DMA((slots, group)),
            pltpu.SemaphoreType.DMA((slots, group)),
        ],
        compiler_params=params(collective_id),
    )(tokens)


def exchange_kernel(blocks, src_ref, out_ref, send_sem, recv_sem):
    me = lax.axis_index("blk")
    peers = [lax.rem(me + k, blocks) for k in range(1, blocks)]
    greet([{"blk": p} for p in peers])
    copies = []
    for k in range(1, blocks):
        copy = send_to(src_ref.at[peers[k - 1]], out_ref.at[me], send_sem.at[k], recv_sem.at[k],
                       {"blk": peers[k - 1]})
        copy.start()
        copies.append(copy)
    out_ref[me] = src_ref[me]
    for k in range(1, blocks):
        source = lax.rem(me + blocks - k, blocks)
        send_to(src_ref.at[me], out_ref.at[source], send_sem.at[k], recv_sem.at[k],
                {"blk": source}).wait_recv()
    for copy in copies:
        copy.wait_send()


def exchange(array, collective_id):
    blocks = array.shape[0]
    return pl.pallas_call(
        functools.partial(exchange_kernel, blocks),
        out_shape=jax.ShapeDtypeStruct(array.shape, array.dtype),
        in_specs=[VMEM],
        out_specs=VMEM,
        scratch_shapes=[pltpu.SemaphoreType.DMA((blocks,)), pltpu.SemaphoreType.DMA((blocks,))],
        compiler_params=params(collective_id),
    )(array)


def row(ref):
    return ref[...].astype(F32).reshape(1, ref.shape[0])


def own_columns(ref, member, cols):
    if cols % LANES == 0:
        return ref[:, pl.ds(pl.multiple_of(member * cols, LANES), cols)]
    per = LANES // cols
    both = ref[:, pl.ds(pl.multiple_of(member // per * LANES, LANES), LANES)].astype(F32)
    return sum(jnp.where(lax.rem(member, per) == i, both[:, i * cols:(i + 1) * cols], 0.0)
               for i in range(per)).astype(BF16)


def own_entries(ref, member, cols):
    values = row(ref)
    return sum(jnp.where(member == i, values[:, i * cols:(i + 1) * cols], 0.0)
               for i in range(ref.shape[0] // cols))


def forward_kernel(group, q_block, tok_ref, wq_ref, wk_ref, wv_ref, qb_ref, vb_ref, len_ref,
                   att_ref, q_ref, k_ref, v_ref, o_ref, vt, w_ref):
    total, width = w_ref.shape[1] // 3, w_ref.shape[0]
    heads = total // HD
    length_all = tok_ref.shape[0]
    me = lax.axis_index("blk")
    plane, member = me // group, lax.rem(me, group)
    doc_len = len_ref[plane]
    chunk = min(512, length_all)
    for i, ref in enumerate((wq_ref, wk_ref, wv_ref)):
        w_ref[:, i * total:(i + 1) * total] = own_columns(ref, member, total)
    bias = jnp.concatenate(
        [own_entries(qb_ref, member, total), jnp.zeros((1, total), F32),
         own_entries(vb_ref, member, total)], axis=1)

    def project(step, carry):
        rows = pl.ds(step * chunk, chunk)
        qkv = mm(tok_ref[rows, :], w_ref[...]) + bias
        lane = lax.broadcasted_iota(jnp.int32, (chunk, LANES), 1)
        row = step * chunk + lax.broadcasted_iota(jnp.int32, (chunk, LANES), 0)
        mask = jnp.where(row < doc_len, 0.0, MASKED)
        for h in range(heads):
            def part(which):
                cols = qkv[:, which * total + h * HD:which * total + (h + 1) * HD]
                return jnp.concatenate([cols, jnp.zeros_like(cols)], axis=1)
            q_ref[h, rows, :] = jnp.where(
                lane == HD, 1.0, part(0).astype(BF16).astype(F32) * (HD ** -0.5)).astype(BF16)
            k_ref[h, rows, :] = jnp.where(
                lane == HD, mask, jnp.where((lane > HD) & (lane < HD + 4), 1.0, part(1))).astype(BF16)
            v_rows = jnp.where((lane >= HD) & (lane < HD + 4), 1.0, part(2)).astype(BF16)
            v_ref[h, rows, :] = v_rows
            vt[h, :, rows] = v_rows.T
        return carry

    lax.fori_loop(0, length_all // chunk, project, 0)

    def block(step, carry):
        rows = pl.ds(step * q_block, q_block)
        for h in range(heads):
            scores = mm_nt(k_ref[h], q_ref[h, rows, :])
            top = jnp.max(scores, axis=0, keepdims=True)
            weights = jnp.exp(scores - top).astype(BF16)
            mixed = mm(vt[h], weights)
            denom = mixed[HD:HD + 1, :]
            scaled = mixed * (1.0 / denom)
            sub = lax.broadcasted_iota(jnp.int32, scaled.shape, 0)
            o_rows = jnp.where(sub == HD, top + jnp.log(denom), scaled).T
            o_ref[h, rows, :] = o_rows
            att_ref[rows, h * HD:(h + 1) * HD] = o_rows[:, :HD].astype(BF16)
        return carry

    lax.fori_loop(0, length_all // q_block, block, 0)


def attention_forward(tok_doc, weights, biases, lengths, group, q_block=256):
    length_all, width = tok_doc.shape
    total = width // group
    heads = total // HD
    per_head = jax.ShapeDtypeStruct((heads, length_all, LANES), BF16)
    return pl.pallas_call(
        functools.partial(forward_kernel, group, q_block),
        out_shape=(
            jax.ShapeDtypeStruct((length_all, total), BF16),
            per_head, per_head, per_head,
            jax.ShapeDtypeStruct((heads, length_all, LANES), F32),
        ),
        in_specs=[VMEM] * 6 + [SMEM],
        out_specs=(VMEM,) * 5,
        scratch_shapes=[
            pltpu.VMEM((heads, LANES, length_all), BF16),
            pltpu.VMEM((width, 3 * total), BF16),
        ],
        compiler_params=params(),
    )(tok_doc, *weights, *biases, lengths)


def three(value):
    high = value.astype(BF16).astype(F32)
    mid = (value - high).astype(BF16).astype(F32)
    return high, mid, value - high - mid


def row_mean(value):
    return jnp.mean(value, axis=1, keepdims=True)


def col_sum(value):
    return jnp.sum(value, axis=0, keepdims=True)


def middle_kernel(group, tok_ref, att_in, cot_ref, len_ref, wo_ref, ob_ref, g1_ref, s1_ref,
                  up_ref, ub_ref, down_ref, db_ref, g2_ref, s2_ref,
                  out_ref, gz_ref, gatt_ref, dw_ref, small_ref,
                  att, act, slope, hid_t):
    slots, rows, width = tok_ref.shape
    count = slots * rows
    inner_width = up_ref.shape[1]
    part = width
    parts = inner_width // part
    me = lax.axis_index("blk")
    flat = tok_ref[...].reshape(count, width)
    cols = width // group
    for s in range(slots):
        for g in range(group):
            att[s * rows:(s + 1) * rows, g * cols:(g + 1) * cols] = att_in[s * group + g]
    up_bias = row(ub_ref)
    gain1, gain2 = row(g1_ref), row(g2_ref)
    summed = flat + mm(att[...], wo_ref[...]) + row(ob_ref)
    centred = summed - row_mean(summed)
    rstd1 = lax.rsqrt(row_mean(centred * centred) + EPS)
    xhat1 = centred * rstd1
    hidden = xhat1 * gain1 + row(s1_ref)
    hidden_low = hidden.astype(BF16)
    hid_t[...] = hidden_low.T
    ffn = jnp.zeros((count, width), F32)
    for c in range(parts):
        span = slice(c * part, (c + 1) * part)
        inner = mm(hidden_low, up_ref[:, span]) + up_bias[:, span]
        square = inner * inner
        slope_in = 0.7978845608 * (1.0 + (3 * 0.044715) * square)
        tanh = jnp.tanh(inner * (0.7978845608 * (1.0 + 0.044715 * square)))
        half = 0.5 * (1.0 + tanh)
        slope[:, span] = half + (0.5 * inner) * ((1.0 - tanh * tanh) * slope_in)
        low = (inner * half).astype(BF16)
        act[:, span] = low
        ffn = ffn + mm(low, down_ref[span, :])
    summed = flat + hidden + ffn + row(db_ref)
    centred = summed - row_mean(summed)
    rstd2 = lax.rsqrt(row_mean(centred * centred) + EPS)
    xhat2 = centred * rstd2
    out_ref[...] = (xhat2 * gain2 + row(s2_ref)).reshape(slots, rows, width)
    position = me * rows + lax.broadcasted_iota(jnp.int32, (rows, width), 0)
    g_out = jnp.concatenate(
        [jnp.where(position < len_ref[s], cot_ref[s], 0.0) for s in range(slots)], axis=0)
    small_ref[...] = jnp.zeros_like(small_ref)
    small_ref[0:1, :] = col_sum(g_out * xhat2)
    small_ref[1:2, :] = col_sum(g_out)
    scaled = g_out * gain2
    g_z2 = rstd2 * (scaled - row_mean(scaled) - xhat2 * row_mean(scaled * xhat2))
    g_ffn = g_z2.astype(BF16)
    small_ref[2:3, :] = col_sum(g_ffn.astype(F32))
    g_hidden = g_z2
    for c in range(parts):
        span = slice(c * part, (c + 1) * part)
        dw_ref[span, :] = mm_tn(act[:, span], g_ffn)
        g_inner32 = mm_nt(g_ffn, down_ref[span, :]) * slope[:, span]
        g_inner = g_inner32.astype(BF16)
        small_ref[6 + c:7 + c, :] = col_sum(g_inner.astype(F32))
        dw_ref[inner_width + c * part:inner_width + (c + 1) * part, :] = mm(hid_t[...], g_inner)
        g_hidden = g_hidden + mm_nt(g_inner, up_ref[:, span])
    small_ref[3:4, :] = col_sum(g_hidden * xhat1)
    small_ref[4:5, :] = col_sum(g_hidden)
    scaled = g_hidden * gain1
    g_z1 = rstd1 * (scaled - row_mean(scaled) - xhat1 * row_mean(scaled * xhat1))
    g_branch = g_z1.astype(BF16)
    small_ref[5:6, :] = col_sum(g_branch.astype(F32))
    dw_ref[2 * inner_width:, :] = mm_tn(att[...], g_branch)
    gz_ref[...] = g_z1 + g_z2
    g_att = mm_nt(g_branch, wo_ref[...]).astype(BF16)
    for s in range(slots):
        for g in range(group):
            gatt_ref[s * group + g] = g_att[s * rows:(s + 1) * rows, g * cols:(g + 1) * cols]


def middle(group, tokens, att_in, cotangent, lengths, *weights):
    slots, rows, width = tokens.shape
    count = slots * rows
    inner_width = weights[4].shape[1]
    return pl.pallas_call(
        functools.partial(middle_kernel, group),
        out_shape=(
            jax.ShapeDtypeStruct((slots, rows, width), F32),
            jax.ShapeDtypeStruct((count, width), F32),
            jax.ShapeDtypeStruct(att_in.shape, BF16),
            jax.ShapeDtypeStruct((2 * inner_width + width, width), F32),
            jax.ShapeDtypeStruct((16, width), F32),
        ),
        in_specs=[VMEM, VMEM, VMEM, SMEM] + [VMEM] * 10,
        out_specs=(VMEM,) * 5,
        scratch_shapes=[
            pltpu.VMEM((count, width), BF16),
            pltpu.VMEM((count, inner_width), BF16),
            pltpu.VMEM((count, inner_width), F32),
            pltpu.VMEM((width, count), BF16),
        ],
        compiler_params=params(),
    )(tokens, att_in, cotangent, lengths, *weights)


def row_tile(rows):
    return next(t for t in (96, 64, 48, 32, 16) if rows % t == 0)


def over_rows(rows, body):
    step = row_tile(rows)

    def run(i, carry):
        body(i * step, step)
        return carry

    lax.fori_loop(0, rows // step, run, 0)


def rows_at(offset, i, step):
    return pl.ds(pl.multiple_of(offset + i, 16), step)


class Summer:
    def __init__(self, source, acc, sent, came, out, place, offset, rows, order, partner, send_sem, recv_sem,
                 out_offset=None):
        self.source, self.acc, self.sent, self.came, self.out = source, acc, sent, came, out
        self.send_sem, self.recv_sem = send_sem, recv_sem
        self.steps = []
        out_offset = offset if out_offset is None else out_offset
        for s, (axis, bit) in enumerate(order):
            to, on = partner(axis, bit)
            halved = rows % 32 == 0
            n = rows // 2 if halved else rows
            give = offset + (1 - on) * n if halved else offset
            keep = offset + on * n if halved else offset
            out_keep = out_offset + on * n if halved else out_offset
            out_give = out_offset + (1 - on) * n if halved else out_offset
            self.steps.append((s, to, n, give, keep, place, halved, out_keep, out_give))
            place, offset, rows, out_offset = place + n, keep, n, out_keep
        self.rows, self.offset, self.out_offset = rows, offset, out_offset

    @staticmethod
    def placed(rows, count):
        total = 0
        for _ in range(count):
            halved = rows % 32 == 0
            rows = rows // 2 if halved else rows
            total += rows
        return total

    def copy(self, s):
        s, to, n, give, keep, place, halved, _, _ = self.steps[s]
        return send_to(self.sent.at[pl.ds(place, n)], self.came.at[pl.ds(place, n)],
                       self.send_sem.at[0, s], self.recv_sem.at[0, s], to)

    def send(self, s):
        _, to, n, give, keep, place, halved, _, _ = self.steps[s]
        src = self.source if s == 0 else self.acc

        def pack(i, step):
            self.sent[rows_at(place, i, step), :] = src[rows_at(give, i, step), :].astype(BF16)

        over_rows(n, pack)
        self.copy(s).start()

    def add(self, s):
        _, to, n, give, keep, place, halved, _, _ = self.steps[s]
        src = self.source if s == 0 else self.acc
        self.copy(s).wait_recv()
        last = s == len(self.steps) - 1

        def sum_up(i, step):
            own = src[rows_at(keep, i, step), :]
            if not halved:
                own = own.astype(BF16).astype(F32)
            own = own + self.came[rows_at(place, i, step), :].astype(F32)
            if last:
                self.out[rows_at(self.out_offset, i, step), :] = own.astype(BF16)
            else:
                self.acc[rows_at(keep, i, step), :] = own

        over_rows(n, sum_up)

    def halved(self):
        return [step for step in reversed(self.steps) if step[6]]

    def spread_copy(self, step, receive):
        s, to, n, _, _, _, _, out_keep, out_give = step
        span = pl.ds(pl.multiple_of(out_give if receive else out_keep, 16), n)
        return send_to(self.out.at[span], self.out.at[span], self.send_sem.at[1, s],
                       self.recv_sem.at[1, s], to)

    def drain(self):
        for s in range(len(self.steps)):
            self.copy(s).wait_send()

    def drain_spread(self, steps):
        for step in steps:
            self.spread_copy(step, False).wait_send()


def bits_of(size):
    return [1 << i for i in range(size.bit_length() - 1)]


def tail_kernel(docs, blocks, group, chunks, k_block, q_tile, q_ref, k_ref, v_ref, o_ref, tok_ref, gsrc_ref,
                dw_ref, small_ref,
                kv_ref, gq_ref, sum_ref, small_out, qkv_ref, bias_out,
                g_in, qx, gx, qt, gt, gq_acc, kv_send, gq_send, dwt, dwt_acc, bias,
                acc, sent, came, sent_w, came_w, small_sent, small_came, bias_sent, bias_came,
                g_sems, kv_sems, gq_sems, sum_sems, w_sems, small_sems, bias_sems, wide_sems, core_sems):
    heads, length_all, _ = q_ref.shape
    rows = length_all // blocks
    width = tok_ref.shape[1]
    me = lax.axis_index("blk")
    my_doc = lax.axis_index("docs")
    index = {"docs": my_doc, "blk": me}
    plane, member = me // group, lax.rem(me, group)
    chunk = min(512, length_all)

    def partner(axis, bit):
        on = lax.rem(index[axis] // bit, 2)
        return {axis: index[axis] + bit - 2 * bit * on}, on

    def peer(k):
        return lax.rem(me + k, blocks)

    def source(k):
        return lax.rem(me + blocks - k, blocks)

    doc_bits, blk_bits = bits_of(docs), bits_of(blocks)
    greet([{"blk": peer(k)} for k in range(1, blocks)] + [partner("docs", bit)[0] for bit in doc_bits])

    def g_copy(k, to, slot):
        return send_to(gsrc_ref.at[to], g_in.at[slot], g_sems.at[0, k], g_sems.at[1, k], {"blk": to})

    for k in range(1, blocks):
        g_copy(k, peer(k), me).start()
    g_in[me] = gsrc_ref[me]

    size = dw_ref.shape[0] // chunks
    ring = [("blk", bit) for bit in blk_bits]
    orders = [[("docs", 1)] + ring[c % len(ring):] + ring[:c % len(ring)] + [("docs", bit) for bit in doc_bits[1:]]
              for c in range(chunks)]
    count = len(orders[0])
    placed = Summer.placed(size, count)
    sums = [Summer(dw_ref, acc, sent, came, sum_ref, c * placed, c * size, size, orders[c], partner,
                   sum_sems.at[c, 0], sum_sems.at[c, 1]) for c in range(chunks)]
    depth = len(sums[0].halved())

    def small_copy(buffers, sems, s):
        axis, bit = orders[0][s]
        return send_to(buffers[0].at[s], buffers[1].at[s], sems.at[0, s], sems.at[1, s],
                       partner(axis, bit)[0])

    def small_step(buffers, sems, s, out):
        small_copy(buffers, sems, s).wait_recv()
        total = buffers[0][s] + buffers[1][s]
        if s + 1 < count:
            buffers[0][s + 1] = total
            small_copy(buffers, sems, s + 1).start()
        else:
            out[...] = total

    smalls = (small_sent, small_came)
    small_sent[0] = small_ref[...]

    def begin():
        for part in sums:
            part.send(0)
        small_copy(smalls, small_sems, 0).start()

    def middle_event(s):
        for part in sums:
            part.add(s)
            if s + 1 < count:
                part.send(s + 1)
            else:
                part.spread_copy(part.halved()[0], False).start()
        small_step(smalls, small_sems, s, small_out)

    def spread_event(d):
        for part in sums:
            part.spread_copy(part.halved()[d], True).wait_recv()
            if d + 1 < depth:
                part.spread_copy(part.halved()[d + 1], False).start()

    events = ([functools.partial(middle_event, s) for s in range(count)]
              + [functools.partial(spread_event, d) for d in range(depth)])
    begin()

    for k in range(1, blocks):
        g_copy(k, source(k), source(k)).wait_recv()

    per_chunk = chunk // rows

    def prepare(step, carry):
        span = pl.ds(step * chunk, chunk)
        lane = lax.broadcasted_iota(jnp.int32, (chunk, LANES), 1)
        g_block = g_in[pl.ds(step * per_chunk, per_chunk)].reshape(chunk, heads * HD)
        for h in range(heads):
            g_rows = g_block[:, h * HD:(h + 1) * HD].astype(F32)
            g_rows = jnp.concatenate([g_rows, jnp.zeros_like(g_rows)], axis=1)
            o_rows = o_ref[h, span, :]
            delta = jnp.sum(g_rows * o_rows, axis=1, keepdims=True)
            ext = g_rows
            for i, value in enumerate(three(-delta)):
                ext = jnp.where(lane == HD + i, value, ext)
            gx[h, span, :] = ext.astype(BF16)
            gt[h, :, span] = g_rows[:, :HD].T.astype(BF16)
            q_rows = q_ref[h, span, :].astype(F32)
            ext = q_rows
            for i, value in enumerate(three(-o_rows[:, HD:HD + 1])):
                ext = jnp.where(lane == HD + 1 + i, value, ext)
            qx[h, span, :] = ext.astype(BF16)
            qt[h, :, span] = q_rows[:, :HD].T.astype(BF16)
        return carry

    lax.fori_loop(0, length_all // chunk, prepare, 0)

    k_blocks = length_all // k_block
    per_block = k_block // rows
    ones = jnp.ones((8, k_block), BF16)
    dwt[...] = jnp.zeros_like(dwt)
    bias[...] = jnp.zeros_like(bias)

    def kv_copy(h, d, slot, r):
        return send_to(kv_send.at[h, d], kv_ref.at[slot, h], kv_sems.at[0, h, r], kv_sems.at[1, h, r],
                       {"blk": d})

    def gq_copy(h, d, slot, r):
        return send_to(gq_send.at[h, d], gq_ref.at[slot, h], gq_sems.at[0, h, r], gq_sems.at[1, h, r],
                       {"blk": d})

    def block(step, carry):
        h, i = step // k_blocks, lax.rem(step, k_blocks)
        which = lax.rem(i + me // per_block + 1, k_blocks)
        span = pl.ds(pl.multiple_of(which * k_block, k_block), k_block)
        k_rows, v_rows = k_ref[h, span, :], v_ref[h, span, :]

        @pl.when(i == 0)
        def _():
            gq_acc[...] = jnp.zeros_like(gq_acc)

        gk = jnp.zeros((HD, k_block), F32)
        gv = jnp.zeros((HD, k_block), F32)
        for t in range(length_all // q_tile):
            tile = slice(t * q_tile, (t + 1) * q_tile)
            weights = jnp.exp(mm_nt(qx[h, tile, :], k_rows))
            centred = mm_nt(gx[h, tile, :], v_rows)
            g_scores = (weights * centred).astype(BF16)
            gv = gv + mm(gt[h, :, tile], weights.astype(BF16))
            gk = gk + mm(qt[h, :, tile], g_scores)
            gq_acc[tile, :] += mm(g_scores, k_rows)
        kv = jnp.concatenate([gk, gv], axis=0).astype(BF16)
        dwt[pl.ds(pl.multiple_of(h * 2 * HD, 2 * HD), 2 * HD), :] += mm(kv, tok_ref[span, :])
        bias[h, 0] += mm_nt(ones, kv[HD:])
        for u in range(per_block):
            d = which * per_block + u
            kv_send[h, d] = kv[:, u * rows:(u + 1) * rows]

            @pl.when(d != me)
            def _():
                kv_copy(h, d, me, lax.rem(d + blocks - me, blocks)).start()

            @pl.when(d == me)
            def _():
                kv_ref[me, h] = kv[:, u * rows:(u + 1) * rows]

        @pl.when(i == k_blocks - 1)
        def _():
            for n in range(blocks):
                gq_send[h, n] = (gq_acc[n * rows:(n + 1) * rows, :HD] * (HD ** -0.5)).T.astype(BF16)
            for r in range(1, blocks):
                gq_copy(h, peer(r), me, r).start()
            gq_ref[me, h] = gq_send[h, me]

        for e, event in enumerate(events):
            if when[e] is not None:
                pl.when(step == when[e])(event)
        return carry

    total_steps = heads * k_blocks
    gaps = EVENT_STEPS[:len(events)] + [total_steps] * max(0, len(events) - len(EVENT_STEPS))
    when = [g if g < total_steps - 1 else None for g in gaps]
    lax.fori_loop(0, total_steps, block, 0)
    left = [event for e, event in enumerate(events) if when[e] is None]

    q_base = heads * 2 * HD
    for h in range(heads):
        part = jnp.zeros((HD, width), F32)
        q_bias = jnp.zeros((8, HD), F32)
        for n in range(blocks):
            low = gq_send[h, n]
            part = part + mm(low, tok_ref[n * rows:(n + 1) * rows, :])
            q_bias = q_bias + mm_nt(jnp.ones((8, rows), BF16), low)
        dwt[q_base + h * HD:q_base + (h + 1) * HD, :] = part
        bias[h, 1] = q_bias
    cols = heads * HD
    lane = lax.broadcasted_iota(jnp.int32, (8, width), 1)
    sub = lax.broadcasted_iota(jnp.int32, (8, width), 0)
    wide = [jnp.concatenate([bias[h, i] for h in range(heads)] * group, axis=1) for i in range(2)]
    biases = (bias_sent, bias_came)
    bias_sent[0] = jnp.where((lane // cols) == member, jnp.where(sub == 0, wide[1], jnp.where(sub == 1, wide[0], 0.0)), 0.0)
    features = 3 * cols
    half = features // 2
    plane_bits = [bit for bit in blk_bits if bit >= group]
    w_order = ([("docs", 1)] + [("blk", bit) for bit in plane_bits] + [("docs", bit) for bit in doc_bits[1:]])
    my_core = lax.rem(my_doc, 2)
    w_sum = Summer(dwt, dwt_acc, sent_w, came_w, qkv_ref, 0, 0, features, w_order, partner,
                   w_sems.at[0], w_sems.at[1],
                   out_offset=my_core * (half * group - half) + member * half)
    small_copy(biases, bias_sems, 0).start()
    w_sum.send(0)
    w_halved = w_sum.halved()[:-1]

    def w_event(s):
        w_sum.add(s)
        if s + 1 < len(w_order):
            w_sum.send(s + 1)
        elif w_halved:
            w_sum.spread_copy(w_halved[0], False).start()

    def w_spread(d):
        w_sum.spread_copy(w_halved[d], True).wait_recv()
        if d + 1 < len(w_halved):
            w_sum.spread_copy(w_halved[d + 1], False).start()

    def slab(m):
        return pl.ds(pl.multiple_of(my_core * half * group + m * half, 16), half)

    def wide_copy(k, m):
        to = plane * group + lax.rem(member + k, group)
        return send_to(qkv_ref.at[slab(m)], qkv_ref.at[slab(m)], wide_sems.at[0, k], wide_sems.at[1, k],
                       {"blk": to})

    def core_copy(core):
        span = pl.ds(pl.multiple_of(core * half * group, 16), half * group)
        return send_to(qkv_ref.at[span], qkv_ref.at[span], core_sems.at[0], core_sems.at[1],
                       partner("docs", 1)[0])

    def wide_start():
        for k in range(1, group):
            wide_copy(k, member).start()

    def wide_wait():
        for k in range(1, group):
            wide_copy(k, lax.rem(member + group - k, group)).wait_recv()
        core_copy(my_core).start()

    w_events = ([functools.partial(w_event, s) for s in range(len(w_order))]
                + [functools.partial(w_spread, d) for d in range(len(w_halved))] + [wide_start, wide_wait])
    for e in range(max(len(w_events), len(left), count)):
        if e < len(w_events):
            w_events[e]()
        if e < len(left):
            left[e]()
        if e < count:
            small_step(biases, bias_sems, e, bias_out)
    core_copy(1 - my_core).wait_recv()

    for h in range(heads):
        for r in range(1, blocks):
            kv_copy(h, source(r), source(r), r).wait_recv()
            gq_copy(h, source(r), source(r), r).wait_recv()
    for r in range(1, blocks):
        g_copy(r, peer(r), me).wait_send()
        for h in range(heads):
            kv_copy(h, peer(r), me, r).wait_send()
            gq_copy(h, peer(r), me, r).wait_send()
    for part in sums:
        part.drain()
        part.drain_spread(part.halved())
    w_sum.drain()
    w_sum.drain_spread(w_halved)
    for k in range(1, group):
        wide_copy(k, member).wait_send()
    core_copy(my_core).wait_send()
    for s in range(count):
        small_copy(smalls, small_sems, s).wait_send()
        small_copy(biases, bias_sems, s).wait_send()


EVENT_STEPS = [0, 1, 4, 6, 8, 9, 10, 11, 13]


def tail(docs, blocks, group, chunks, q, k, v, o, tok_doc, g_att, dw, small, collective_id, k_block=256, q_tile=512):
    heads, length_all, _ = q.shape
    rows = length_all // blocks
    width = tok_doc.shape[1]
    features = 3 * heads * HD
    count = len(bits_of(docs)) + len(bits_of(blocks))
    w_count = count - len(bits_of(group))
    placed = chunks * Summer.placed(dw.shape[0] // chunks, count)
    w_placed = Summer.placed(features, w_count)
    dma = pltpu.SemaphoreType.DMA
    return pl.pallas_call(
        functools.partial(tail_kernel, docs, blocks, group, chunks, k_block, q_tile),
        out_shape=(
            jax.ShapeDtypeStruct((blocks, heads, 2 * HD, rows), BF16),
            jax.ShapeDtypeStruct((blocks, heads, HD, rows), BF16),
            jax.ShapeDtypeStruct(dw.shape, BF16),
            jax.ShapeDtypeStruct(small.shape, F32),
            jax.ShapeDtypeStruct((features * group, width), BF16),
            jax.ShapeDtypeStruct((8, width), F32),
        ),
        in_specs=[VMEM] * 8,
        out_specs=(VMEM,) * 6,
        scratch_shapes=[
            pltpu.VMEM(g_att.shape, BF16),
            pltpu.VMEM((heads, length_all, LANES), BF16),
            pltpu.VMEM((heads, length_all, LANES), BF16),
            pltpu.VMEM((heads, HD, length_all), BF16),
            pltpu.VMEM((heads, HD, length_all), BF16),
            pltpu.VMEM((length_all, LANES), F32),
            pltpu.VMEM((heads, blocks, 2 * HD, rows), BF16),
            pltpu.VMEM((heads, blocks, HD, rows), BF16),
            pltpu.VMEM((features, width), F32),
            pltpu.VMEM((features, width), F32),
            pltpu.VMEM((heads, 2, 8, HD), F32),
            pltpu.VMEM(dw.shape, F32),
            pltpu.VMEM((placed, width), BF16),
            pltpu.VMEM((placed, width), BF16),
            pltpu.VMEM((w_placed, width), BF16),
            pltpu.VMEM((w_placed, width), BF16),
            pltpu.VMEM((count,) + small.shape, F32),
            pltpu.VMEM((count,) + small.shape, F32),
            pltpu.VMEM((count, 8, width), F32),
            pltpu.VMEM((count, 8, width), F32),
            dma((2, blocks)),
            dma((2, heads, blocks)),
            dma((2, heads, blocks)),
            dma((chunks, 2, 2, count)),
            dma((2, 2, w_count)),
            dma((2, count)),
            dma((2, count)),
            dma((2, group)),
            dma((2,)),
        ],
        compiler_params=params(collective_id),
    )(q, k, v, o, tok_doc, g_att, dw, small)


def last_kernel(group, kv_ref, gq_ref, gz_ref, wq_ref, wk_ref, wv_ref, sum_ref, small_ref, qkv_ref, bias_ref,
                grad_ref, qw_ref, qb_ref, kw_ref, vw_ref, vb_ref, ow_ref, ob_ref, g1_ref, s1_ref,
                uw_ref, ub_ref, dw_ref, db_ref, g2_ref, s2_ref, across, stack):
    blocks, heads, _, rows = kv_ref.shape
    slots = blocks // group
    width = wq_ref.shape[0]
    inner_width = uw_ref.shape[1]
    cols = heads * HD

    def widen(out, rows_out, cols_out, base):
        step = row_tile(rows_out)

        def run(i, carry):
            span = pl.ds(pl.multiple_of(i * step, step), step)
            out[span, cols_out] = sum_ref[pl.ds(pl.multiple_of(base + i * step, 16), step), :].astype(F32)
            return carry

        lax.fori_loop(0, rows_out // step, run, 0)

    widen(dw_ref, inner_width, slice(None), 0)
    for c in range(inner_width // width):
        widen(uw_ref, width, slice(c * width, (c + 1) * width), inner_width + c * width)
    widen(ow_ref, width, slice(None), 2 * inner_width)
    total = gz_ref[...]
    for which, w_ref in enumerate((wq_ref, wk_ref, wv_ref)):
        for s in range(slots):
            for g in range(group):
                for h in range(heads):
                    low = gq_ref[s * group + g, h] if which == 0 else (
                        kv_ref[s * group + g, h, (which - 1) * HD:which * HD, :])
                    across[g * cols + h * HD:g * cols + (h + 1) * HD, s * rows:(s + 1) * rows] = low
        total = total + mm_nt(across[...].T, w_ref[...])
    grad_ref[...] = total.reshape(grad_ref.shape)
    half = 3 * cols // 2
    unit = HD // 2
    for which, out in enumerate((qw_ref, kw_ref, vw_ref)):
        for g in range(group):
            for h in range(heads):
                first = heads * 2 * HD + h * HD if which == 0 else h * 2 * HD + (which - 1) * HD
                for u in range(2):
                    f = first + u * unit
                    at = f // half * half * group + g * half + f % half
                    to = g * cols + h * HD + u * unit
                    stack[to:to + unit, :] = qkv_ref[at:at + unit, :]
        out[...] = stack[...].T.astype(F32)

    def vector(out, ref, i):
        out[...] = ref[i:i + 1, :].reshape(out.shape)

    vector(qb_ref, bias_ref, 0)
    vector(vb_ref, bias_ref, 1)
    for i, out in enumerate((g2_ref, s2_ref, db_ref, g1_ref, s1_ref, ob_ref)):
        vector(out, small_ref, i)
    parts = inner_width // width
    ub_ref[...] = jnp.concatenate([small_ref[6 + i:7 + i, :] for i in range(parts)], axis=1).reshape(ub_ref.shape)


def last(group, shape, inner_width, *arrays):
    width = shape[-1]
    square = jax.ShapeDtypeStruct((width, width), F32)
    vector = jax.ShapeDtypeStruct((width,), F32)
    return pl.pallas_call(
        functools.partial(last_kernel, group),
        out_shape=(
            jax.ShapeDtypeStruct(shape, F32), square, vector, square, square, vector, square, vector,
            vector, vector, jax.ShapeDtypeStruct((width, inner_width), F32),
            jax.ShapeDtypeStruct((inner_width,), F32), jax.ShapeDtypeStruct((inner_width, width), F32),
            vector, vector, vector,
        ),
        in_specs=[VMEM] * len(arrays),
        out_specs=(VMEM,) * 16,
        scratch_shapes=[
            pltpu.VMEM((width, shape[0] * shape[1]), BF16),
            pltpu.VMEM((width, width), BF16),
        ],
        compiler_params=params(),
    )(*arrays)


def device_program(docs, blocks, tokens, query_weight, query_bias, key_weight, value_weight, value_bias,
                   out_weight, out_bias, first_gain, first_shift, up_weight, up_bias, down_weight,
                   down_bias, second_gain, second_shift, cotangent, lengths):
    slots, rows, width = tokens.shape
    inner_width = up_weight.shape[1]
    group = blocks // slots
    cols = width // group
    length_all = rows * blocks
    projections = (query_weight, key_weight, value_weight)
    tok_doc = gather_tokens(tokens, blocks, 0).reshape(length_all, width)
    att, q, k, v, o = attention_forward(tok_doc, projections, (query_bias, value_bias), lengths, group)
    att_in = exchange(att.reshape(blocks, rows, cols), 1)
    output, gz, g_att, dw, small = middle(
        group, tokens, att_in, cotangent, lengths, out_weight, out_bias, first_gain, first_shift,
        up_weight, up_bias, down_weight, down_bias, second_gain, second_shift)
    kv, gq, dw, small, dw_qkv, bias = tail(
        docs, blocks, group, 3, q, k, v, o, tok_doc, g_att, dw, small, 2)
    grads = last(group, tokens.shape, inner_width, kv, gq, gz, *projections, dw, small, dw_qkv, bias)
    return (output, *grads)


def solution(mesh):
    split = P("docs", "blk", None)
    return jax.shard_map(
        functools.partial(device_program, mesh.shape["docs"], mesh.shape["blk"]),
        mesh=mesh,
        in_specs=(split,) + (P(),) * 15 + (split, P("docs")),
        out_specs=(split, split) + (P(),) * 15,
        check_vma=False,
    )
```

```python
import functools

import jax
import jax.numpy as jnp
from jax import lax
from jax.experimental import pallas as pl
from jax.experimental.pallas import tpu as pltpu
from jax.sharding import PartitionSpec as P

HD = 64
LANES = 128
EPS = 1e-05
MASKED = -1e30
F32 = jnp.float32
BF16 = jnp.bfloat16
VMEM = pl.BlockSpec(memory_space=pltpu.VMEM)
ANY = pl.BlockSpec(memory_space=pl.ANY)
SMEM = pl.BlockSpec(memory_space=pltpu.SMEM)
MESH = pl.DeviceIdType.MESH
VMEM_LIMIT = 63 * 1024 * 1024


def mm(left, right):
    return jnp.dot(left, right, preferred_element_type=F32)


def mm_nt(left, right):
    return lax.dot_general(left, right, (((1,), (1,)), ((), ())), preferred_element_type=F32)


def mm_tn(left, right):
    return lax.dot_general(left, right, (((0,), (0,)), ((), ())), preferred_element_type=F32)


def params(collective_id=None):
    if collective_id is None:
        return pltpu.CompilerParams(vmem_limit_bytes=VMEM_LIMIT)
    return pltpu.CompilerParams(
        vmem_limit_bytes=VMEM_LIMIT, collective_id=collective_id, has_side_effects=True
    )


def greet(peers):
    barrier = pltpu.get_barrier_semaphore()
    for peer in peers:
        pl.semaphore_signal(barrier, inc=1, device_id=peer, device_id_type=MESH)
    pl.semaphore_wait(barrier, len(peers))


def send_to(src, dst, send_sem, recv_sem, peer):
    return pltpu.make_async_remote_copy(
        src_ref=src, dst_ref=dst, send_sem=send_sem, recv_sem=recv_sem,
        device_id=peer, device_id_type=MESH,
    )


def gather_kernel(slots, group, tok_ref, out_ref, low, send_a, recv_a, send_b, recv_b):
    me = lax.axis_index("blk")
    plane, member = me // group, me % group
    planes = [lax.rem(plane + k, slots) for k in range(1, slots)]
    members = [lax.rem(member + k, group) for k in range(1, group)]
    greet([{"blk": p * group + member} for p in planes]
          + [{"blk": plane * group + m} for m in members])
    low[...] = tok_ref[...].astype(BF16)
    first = []
    for k in range(1, slots):
        target = planes[k - 1]
        copy = send_to(low.at[target], out_ref.at[me], send_a.at[k], recv_a.at[k],
                       {"blk": target * group + member})
        copy.start()
        first.append(copy)
    out_ref[me] = low[plane]
    second = []
    for k in range(slots):
        source = lax.rem(plane + slots - k, slots)
        block = source * group + member
        if k > 0:
            send_to(low.at[plane], out_ref.at[block], send_a.at[k], recv_a.at[k],
                    {"blk": block}).wait_recv()
        for j in range(1, group):
            copy = send_to(out_ref.at[block], out_ref.at[block], send_b.at[k, j], recv_b.at[k, j],
                           {"blk": plane * group + members[j - 1]})
            copy.start()
            second.append(copy)
    for k in range(slots):
        source = lax.rem(plane + slots - k, slots)
        for j in range(1, group):
            block = source * group + lax.rem(member + group - j, group)
            send_to(out_ref.at[block], out_ref.at[block], send_b.at[k, j], recv_b.at[k, j],
                    {"blk": plane * group + members[j - 1]}).wait_recv()
    for copy in first + second:
        copy.wait_send()


def gather_tokens(tokens, blocks, collective_id):
    slots, rows, width = tokens.shape
    group = blocks // slots
    return pl.pallas_call(
        functools.partial(gather_kernel, slots, group),
        out_shape=jax.ShapeDtypeStruct((blocks, rows, width), BF16),
        in_specs=[VMEM],
        out_specs=VMEM,
        scratch_shapes=[
            pltpu.VMEM((slots, rows, width), BF16),
            pltpu.SemaphoreType.DMA((slots,)),
            pltpu.SemaphoreType.DMA((slots,)),
            pltpu.SemaphoreType.DMA((slots, group)),
            pltpu.SemaphoreType.DMA((slots, group)),
        ],
        compiler_params=params(collective_id),
    )(tokens)


def exchange_kernel(blocks, src_ref, out_ref, send_sem, recv_sem):
    me = lax.axis_index("blk")
    peers = [lax.rem(me + k, blocks) for k in range(1, blocks)]
    greet([{"blk": p} for p in peers])
    copies = []
    for k in range(1, blocks):
        copy = send_to(src_ref.at[peers[k - 1]], out_ref.at[me], send_sem.at[k], recv_sem.at[k],
                       {"blk": peers[k - 1]})
        copy.start()
        copies.append(copy)
    out_ref[me] = src_ref[me]
    for k in range(1, blocks):
        source = lax.rem(me + blocks - k, blocks)
        send_to(src_ref.at[me], out_ref.at[source], send_sem.at[k], recv_sem.at[k],
                {"blk": source}).wait_recv()
    for copy in copies:
        copy.wait_send()


def exchange(array, collective_id):
    blocks = array.shape[0]
    return pl.pallas_call(
        functools.partial(exchange_kernel, blocks),
        out_shape=jax.ShapeDtypeStruct(array.shape, array.dtype),
        in_specs=[VMEM],
        out_specs=VMEM,
        scratch_shapes=[pltpu.SemaphoreType.DMA((blocks,)), pltpu.SemaphoreType.DMA((blocks,))],
        compiler_params=params(collective_id),
    )(array)


def row(ref):
    return ref[...].astype(F32).reshape(1, ref.shape[0])


def own_columns(ref, member, cols):
    if cols % LANES == 0:
        return ref[:, pl.ds(pl.multiple_of(member * cols, LANES), cols)]
    per = LANES // cols
    both = ref[:, pl.ds(pl.multiple_of(member // per * LANES, LANES), LANES)].astype(F32)
    return sum(jnp.where(lax.rem(member, per) == i, both[:, i * cols:(i + 1) * cols], 0.0)
               for i in range(per)).astype(BF16)


def own_entries(ref, member, cols):
    values = row(ref)
    return sum(jnp.where(member == i, values[:, i * cols:(i + 1) * cols], 0.0)
               for i in range(ref.shape[0] // cols))


def forward_kernel(group, q_block, tok_ref, wq_ref, wk_ref, wv_ref, qb_ref, vb_ref, len_ref,
                   att_ref, q_ref, k_ref, v_ref, o_ref, vt, w_ref):
    total, width = w_ref.shape[1] // 3, w_ref.shape[0]
    heads = total // HD
    length_all = tok_ref.shape[0]
    me = lax.axis_index("blk")
    plane, member = me // group, lax.rem(me, group)
    doc_len = len_ref[plane]
    chunk = min(512, length_all)
    for i, ref in enumerate((wq_ref, wk_ref, wv_ref)):
        w_ref[:, i * total:(i + 1) * total] = own_columns(ref, member, total)
    bias = jnp.concatenate(
        [own_entries(qb_ref, member, total), jnp.zeros((1, total), F32),
         own_entries(vb_ref, member, total)], axis=1)

    def project(step, carry):
        rows = pl.ds(step * chunk, chunk)
        qkv = mm(tok_ref[rows, :], w_ref[...]) + bias
        lane = lax.broadcasted_iota(jnp.int32, (chunk, LANES), 1)
        row = step * chunk + lax.broadcasted_iota(jnp.int32, (chunk, LANES), 0)
        mask = jnp.where(row < doc_len, 0.0, MASKED)
        for h in range(heads):
            def part(which):
                cols = qkv[:, which * total + h * HD:which * total + (h + 1) * HD]
                return jnp.concatenate([cols, jnp.zeros_like(cols)], axis=1)
            q_ref[h, rows, :] = jnp.where(
                lane == HD, 1.0, part(0).astype(BF16).astype(F32) * (HD ** -0.5)).astype(BF16)
            k_ref[h, rows, :] = jnp.where(
                lane == HD, mask, jnp.where((lane > HD) & (lane < HD + 4), 1.0, part(1))).astype(BF16)
            v_rows = jnp.where((lane >= HD) & (lane < HD + 4), 1.0, part(2)).astype(BF16)
            v_ref[h, rows, :] = v_rows
            vt[h, :, rows] = v_rows.T
        return carry

    lax.fori_loop(0, length_all // chunk, project, 0)

    def block(step, carry):
        rows = pl.ds(step * q_block, q_block)
        for h in range(heads):
            scores = mm_nt(k_ref[h], q_ref[h, rows, :])
            top = jnp.max(scores, axis=0, keepdims=True)
            weights = jnp.exp(scores - top).astype(BF16)
            mixed = mm(vt[h], weights)
            denom = mixed[HD:HD + 1, :]
            scaled = mixed * (1.0 / denom)
            sub = lax.broadcasted_iota(jnp.int32, scaled.shape, 0)
            o_rows = jnp.where(sub == HD, top + jnp.log(denom), scaled).T
            o_ref[h, rows, :] = o_rows
            att_ref[rows, h * HD:(h + 1) * HD] = o_rows[:, :HD].astype(BF16)
        return carry

    lax.fori_loop(0, length_all // q_block, block, 0)


def attention_forward(tok_doc, weights, biases, lengths, group, q_block=256):
    length_all, width = tok_doc.shape
    total = width // group
    heads = total // HD
    per_head = jax.ShapeDtypeStruct((heads, length_all, LANES), BF16)
    return pl.pallas_call(
        functools.partial(forward_kernel, group, q_block),
        out_shape=(
            jax.ShapeDtypeStruct((length_all, total), BF16),
            per_head, per_head, per_head,
            jax.ShapeDtypeStruct((heads, length_all, LANES), F32),
        ),
        in_specs=[VMEM] * 6 + [SMEM],
        out_specs=(VMEM,) * 5,
        scratch_shapes=[
            pltpu.VMEM((heads, LANES, length_all), BF16),
            pltpu.VMEM((width, 3 * total), BF16),
        ],
        compiler_params=params(),
    )(tok_doc, *weights, *biases, lengths)


def three(value):
    high = value.astype(BF16).astype(F32)
    mid = (value - high).astype(BF16).astype(F32)
    return high, mid, value - high - mid


def row_tile(rows):
    return next(t for t in (96, 64, 48, 32, 16) if rows % t == 0)


def over_rows(rows, body):
    step = row_tile(rows)

    def run(i, carry):
        body(i * step, step)
        return carry

    lax.fori_loop(0, rows // step, run, 0)


def rows_at(offset, i, step):
    return pl.ds(pl.multiple_of(offset + i, 16), step)


def rows_of(offset, n):
    return pl.ds(pl.multiple_of(offset, 16), n)


def bits_of(size):
    return [1 << i for i in range(size.bit_length() - 1)]


class Place:
    def __init__(self, docs, blocks, group):
        self.docs, self.blocks, self.group = docs, blocks, group
        self.planes = blocks // group
        self.me, self.doc = lax.axis_index("blk"), lax.axis_index("docs")
        self.plane, self.member = self.me // group, lax.rem(self.me, group)

    def pair(self, axis, bit):
        mine = self.me if axis == "blk" else self.doc
        on = lax.rem(mine // bit, 2)
        return {axis: mine + bit - 2 * bit * on}, on

    def peer(self, k):
        return lax.rem(self.me + k, self.blocks)

    def source(self, k):
        return lax.rem(self.me + self.blocks - k, self.blocks)

    def plane_peer(self, k):
        return lax.rem(self.plane + k, self.planes)

    def plane_source(self, k):
        return lax.rem(self.plane + self.planes - k, self.planes)


class Summer:
    def __init__(self, at, acc, sent, came, out, place, offset, rows, pairs, rest, sems, out_shift=0):
        self.at, self.acc, self.sent, self.came, self.out, self.sems = at, acc, sent, came, out, sems
        self.shift = out_shift
        self.stages = []
        for axis, bit in pairs:
            to, on = at.pair(axis, bit)
            n = rows // 2
            self.stages.append(("pair", to, n, offset + (1 - on) * n, offset + on * n, place))
            offset, rows, place = offset + on * n, n, place + n
        n = rows // at.planes
        self.stages.append(("planes", None, n, offset, offset + at.plane * n, place))
        offset, rows, place = offset + at.plane * n, n, place + (at.planes - 1) * n
        for axis, bit in rest:
            self.stages.append(("full", at.pair(axis, bit)[0], rows, offset, offset, place))
            place += rows
        self.count = len(self.stages)
        self.back = [s for s in range(self.count) if self.stages[s][0] != "full"][::-1]

    @staticmethod
    def placed(rows, pairs, planes, rest):
        total = 0
        for _ in range(pairs):
            rows //= 2
            total += rows
        rows //= planes
        return total + (planes - 1 + rest) * rows

    def copies(self, s, back=False, receive=False):
        kind, to, n, give, keep, place = self.stages[s]
        at, out = self.at, self.out
        w = 1 if back else 0
        if kind == "planes":
            found = []
            for k in range(1, at.planes):
                if back:
                    which = at.plane_source(k) if receive else at.plane
                    span = rows_of(give + which * n + self.shift, n)
                    src, dst = out.at[span], out.at[span]
                else:
                    src, dst = (ref.at[rows_of(place + (k - 1) * n, n)] for ref in (self.sent, self.came))
                to = {"blk": at.plane_peer(k) * at.group + at.member}
                found.append(send_to(src, dst, self.sems.at[w, 0, s, k], self.sems.at[w, 1, s, k], to))
            return found
        if back:
            span = rows_of((give if receive else keep) + self.shift, n)
            src, dst = out.at[span], out.at[span]
        else:
            src, dst = self.sent.at[rows_of(place, n)], self.came.at[rows_of(place, n)]
        return [send_to(src, dst, self.sems.at[w, 0, s, 0], self.sems.at[w, 1, s, 0], to)]

    def pack(self, give, place, n):
        def run(i, step):
            self.sent[rows_at(place, i, step), :] = self.acc[rows_at(give, i, step), :].astype(BF16)
        over_rows(n, run)

    def start(self, s):
        kind, to, n, give, keep, place = self.stages[s]
        if kind == "planes":
            for k in range(1, self.at.planes):
                self.pack(give + self.at.plane_peer(k) * n, place + (k - 1) * n, n)
        else:
            self.pack(give, place, n)
        for copy in self.copies(s):
            copy.start()

    def finish(self, s):
        kind, to, n, give, keep, place = self.stages[s]
        for copy in self.copies(s):
            copy.wait_recv()
        parts = self.at.planes - 1 if kind == "planes" else 1
        last = s == self.count - 1

        def run(i, step):
            total = self.acc[rows_at(keep, i, step), :]
            if kind == "full":
                total = total.astype(BF16).astype(F32)
            for k in range(parts):
                total = total + self.came[rows_at(place + k * n, i, step), :].astype(F32)
            if last:
                self.out[rows_at(keep + self.shift, i, step), :] = total.astype(BF16)
            else:
                self.acc[rows_at(keep, i, step), :] = total
        over_rows(n, run)

    def start_back(self, s):
        for copy in self.copies(s, back=True):
            copy.start()

    def finish_back(self, s):
        for copy in self.copies(s, back=True, receive=True):
            copy.wait_recv()

    def events(self, back):
        def first():
            self.start(0)

        def inward(s):
            self.finish(s)
            if s + 1 < self.count:
                self.start(s + 1)
            elif back:
                self.start_back(back[0])

        def outward(d):
            self.finish_back(back[d])
            if d + 1 < len(back):
                self.start_back(back[d + 1])

        return ([first] + [functools.partial(inward, s) for s in range(self.count)]
                + [functools.partial(outward, d) for d in range(len(back))])

    def drain(self, back):
        for s in range(self.count):
            for copy in self.copies(s):
                copy.wait_send()
        for s in back:
            for copy in self.copies(s, back=True):
                copy.wait_send()


def row_mean(value):
    return jnp.mean(value, axis=1, keepdims=True)


def col_sum(value):
    return jnp.sum(value, axis=0, keepdims=True)


def main_kernel(docs, blocks, group, cuts, k_block, q_tile,
                tokens_ref, att_in, cot_ref, len_ref, wo_ref, ob_ref, g1_ref, s1_ref, up_hbm, ub_ref, down_hbm,
                db_ref, g2_ref, s2_ref, q_ref, k_ref, v_ref, o_ref, tok_ref,
                out_ref, gz_ref, kv_ref, gq_ref, sum_ref, qkv_ref, small_out,
                att, hid_t, g_att, g_in, qx, gx, qt, gt, gq_acc, kv_send, gq_send,
                acc, sent, came, dwt, sent_w, came_w, bias, small_sent, small_came,
                g_sems, kv_sems, gq_sems, sum_sems, w_sems, small_sems, wide_sems, core_sems, load_sems):
    at = Place(docs, blocks, group)
    me, member, plane = at.me, at.member, at.plane
    slots, rows, width = tokens_ref.shape
    count = slots * rows
    cols = width // group
    inner_width = up_hbm.shape[1]
    heads, length_all, _ = q_ref.shape
    parts = inner_width // width
    doc_bits, member_bits, plane_bits = bits_of(docs), bits_of(group), [b for b in bits_of(blocks) if b >= group]

    loads = [pltpu.make_async_copy(up_hbm.at[:, c * width:(c + 1) * width],
                                   sent.at[inner_width + c * width:inner_width + (c + 1) * width], load_sems.at[c])
             for c in range(parts)]
    loads.append(pltpu.make_async_copy(down_hbm, sent.at[:inner_width], load_sems.at[parts]))
    for load in loads:
        load.start()

    def up_part(c):
        return sent[inner_width + c * width:inner_width + (c + 1) * width, :]

    greet([{"blk": at.peer(k)} for k in range(1, blocks)] + [at.pair("docs", bit)[0] for bit in doc_bits])

    rest = [("docs", bit) for bit in doc_bits[1:]]
    sums, place = [], 0
    for c, (offset, size) in enumerate(cuts):
        turn = c % len(member_bits)
        pairs = [("docs", 1)] + [("blk", bit) for bit in member_bits[turn:] + member_bits[:turn]]
        sums.append(Summer(at, acc, sent, came, sum_ref, place, offset, size, pairs, rest, sum_sems.at[c]))
        place = place + Summer.placed(size, len(pairs), at.planes, len(rest))
    chains = [s.events(s.back) for s in sums]
    groups = [[c for c in range(len(cuts)) if cuts[c][0] < inner_width],
              [c for c in range(len(cuts)) if cuts[c][0] >= inner_width]]

    def advance(which, step):
        for c in groups[which]:
            chains[c][step]()

    flat = tokens_ref[...].reshape(count, width)
    for s in range(slots):
        for g in range(group):
            att[s * rows:(s + 1) * rows, g * cols:(g + 1) * cols] = att_in[s * group + g]
    up_bias = row(ub_ref)
    gain1, gain2 = row(g1_ref), row(g2_ref)
    summed = flat + mm(att[...], wo_ref[...]) + row(ob_ref)
    centred = summed - row_mean(summed)
    rstd1 = lax.rsqrt(row_mean(centred * centred) + EPS)
    xhat1 = centred * rstd1
    hidden = xhat1 * gain1 + row(s1_ref)
    hidden_low = hidden.astype(BF16)
    hid_t[...] = hidden_low.T
    for load in loads:
        load.wait()
    ffn = jnp.zeros((count, width), F32)
    for c in range(parts):
        span = slice(c * width, (c + 1) * width)
        inner = mm(hidden_low, up_part(c)) + up_bias[:, span]
        square = inner * inner
        slope_in = 0.7978845608 * (1.0 + (3 * 0.044715) * square)
        tanh = jnp.tanh(inner * (0.7978845608 * (1.0 + 0.044715 * square)))
        half = 0.5 * (1.0 + tanh)
        acc[c * count:(c + 1) * count, :] = half + (0.5 * inner) * ((1.0 - tanh * tanh) * slope_in)
        low = (inner * half).astype(BF16)
        sum_ref[c * count:(c + 1) * count, :] = low
        ffn = ffn + mm(low, sent[span, :])
    summed = flat + hidden + ffn + row(db_ref)
    centred = summed - row_mean(summed)
    rstd2 = lax.rsqrt(row_mean(centred * centred) + EPS)
    xhat2 = centred * rstd2
    out_ref[...] = (xhat2 * gain2 + row(s2_ref)).reshape(slots, rows, width)
    position = me * rows + lax.broadcasted_iota(jnp.int32, (rows, width), 0)
    g_out = jnp.concatenate(
        [jnp.where(position < len_ref[s], cot_ref[s], 0.0) for s in range(slots)], axis=0)
    small_sent[0] = jnp.zeros(small_sent.shape[1:], F32)
    small_sent[0, 0:1, :] = col_sum(g_out * xhat2)
    small_sent[0, 1:2, :] = col_sum(g_out)
    scaled = g_out * gain2
    g_z2 = rstd2 * (scaled - row_mean(scaled) - xhat2 * row_mean(scaled * xhat2))
    g_ffn = g_z2.astype(BF16)
    small_sent[0, 2:3, :] = col_sum(g_ffn.astype(F32))
    g_hidden = g_z2
    for c in range(parts):
        span = slice(c * width, (c + 1) * width)
        g_inner = (mm_nt(g_ffn, sent[span, :]) * acc[c * count:(c + 1) * count, :]).astype(BF16)
        sum_ref[inner_width + c * count:inner_width + (c + 1) * count, :] = g_inner
        g_hidden = g_hidden + mm_nt(g_inner, up_part(c))
    scaled = g_hidden * gain1
    g_z1 = rstd1 * (scaled - row_mean(scaled) - xhat1 * row_mean(scaled * xhat1))
    g_branch = g_z1.astype(BF16)
    gz_ref[...] = g_z1 + g_z2
    g_low = mm_nt(g_branch, wo_ref[...]).astype(BF16)
    for s in range(slots):
        for g in range(group):
            g_att[s * group + g] = g_low[s * rows:(s + 1) * rows, g * cols:(g + 1) * cols]

    def g_copy(k, to, slot):
        return send_to(g_att.at[to], g_in.at[slot], g_sems.at[0, k], g_sems.at[1, k], {"blk": to})

    for k in range(1, blocks):
        g_copy(k, at.peer(k), me).start()
    g_in[me] = g_att[me]

    for c in range(parts):
        span = slice(c * width, (c + 1) * width)
        acc[span, :] = mm_tn(sum_ref[c * count:(c + 1) * count, :], g_ffn)
    advance(0, 0)
    for c in range(parts):
        span = slice(c * width, (c + 1) * width)
        g_inner = sum_ref[inner_width + c * count:inner_width + (c + 1) * count, :]
        small_sent[0, 6 + c:7 + c, :] = col_sum(g_inner.astype(F32))
        acc[inner_width + c * width:inner_width + (c + 1) * width, :] = mm(hid_t[...], g_inner)
    acc[2 * inner_width:2 * inner_width + width, :] = mm_tn(att[...], g_branch)
    if acc.shape[0] > 2 * inner_width + width:
        acc[2 * inner_width + width:, :] = jnp.zeros((acc.shape[0] - 2 * inner_width - width, width), F32)
    advance(1, 0)
    small_sent[0, 3:4, :] = col_sum(g_hidden * xhat1)
    small_sent[0, 4:5, :] = col_sum(g_hidden)
    small_sent[0, 5:6, :] = col_sum(g_branch.astype(F32))
    advance(0, 1)
    chunk = min(512, length_all)
    lane = lax.broadcasted_iota(jnp.int32, (chunk, LANES), 1)

    def prepare_q(step, carry):
        span = pl.ds(step * chunk, chunk)
        for h in range(heads):
            q_rows = q_ref[h, span, :].astype(F32)
            ext = q_rows
            for i, value in enumerate(three(-o_ref[h, span, HD:HD + 1])):
                ext = jnp.where(lane == HD + 1 + i, value, ext)
            qx[h, span, :] = ext.astype(BF16)
            qt[h, :, span] = q_rows[:, :HD].T.astype(BF16)
        return carry

    lax.fori_loop(0, length_all // chunk, prepare_q, 0)
    advance(1, 1)
    for k in range(1, blocks):
        g_copy(k, at.source(k), at.source(k)).wait_recv()

    def prepare_g(step, carry):
        span = pl.ds(step * chunk, chunk)
        g_block = g_in[pl.ds(step * (chunk // rows), chunk // rows)].reshape(chunk, cols)
        for h in range(heads):
            g_rows = g_block[:, h * HD:(h + 1) * HD].astype(F32)
            g_rows = jnp.concatenate([g_rows, jnp.zeros_like(g_rows)], axis=1)
            delta = jnp.sum(g_rows * o_ref[h, span, :], axis=1, keepdims=True)
            ext = g_rows
            for i, value in enumerate(three(-delta)):
                ext = jnp.where(lane == HD + i, value, ext)
            gx[h, span, :] = ext.astype(BF16)
            gt[h, :, span] = g_rows[:, :HD].T.astype(BF16)
        return carry

    lax.fori_loop(0, length_all // chunk, prepare_g, 0)

    k_blocks = length_all // k_block
    per_block = k_block // rows
    ones = jnp.ones((8, k_block), BF16)
    dwt[...] = jnp.zeros_like(dwt)
    bias[...] = jnp.zeros_like(bias)

    def kv_copy(h, d, slot, r):
        return send_to(kv_send.at[h, d], kv_ref.at[slot, h], kv_sems.at[0, h, r], kv_sems.at[1, h, r],
                       {"blk": d})

    def gq_copy(h, d, slot, r):
        return send_to(gq_send.at[h, d], gq_ref.at[slot, h], gq_sems.at[0, h, r], gq_sems.at[1, h, r],
                       {"blk": d})

    total_steps = heads * k_blocks
    timed = [(which, step, t) for which, table in enumerate(EVENT_STEPS) for step, t in table.items()
             if t < total_steps]
    done = [2 + sum(1 for w, _, _ in timed if w == which) for which in range(2)]

    def block(step, carry):
        h, i = step // k_blocks, lax.rem(step, k_blocks)
        which = lax.rem(i + me // per_block + 1, k_blocks)
        span = pl.ds(pl.multiple_of(which * k_block, k_block), k_block)
        k_rows, v_rows = k_ref[h, span, :], v_ref[h, span, :]

        @pl.when(i == 0)
        def _():
            gq_acc[...] = jnp.zeros_like(gq_acc)

        gk = jnp.zeros((HD, k_block), F32)
        gv = jnp.zeros((HD, k_block), F32)
        for t in range(length_all // q_tile):
            tile = slice(t * q_tile, (t + 1) * q_tile)
            weights = jnp.exp(mm_nt(qx[h, tile, :], k_rows))
            centred = mm_nt(gx[h, tile, :], v_rows)
            g_scores = (weights * centred).astype(BF16)
            gv = gv + mm(gt[h, :, tile], weights.astype(BF16))
            gk = gk + mm(qt[h, :, tile], g_scores)
            gq_acc[tile, :] += mm(g_scores, k_rows)
        kv = jnp.concatenate([gk, gv], axis=0).astype(BF16)
        dwt[pl.ds(pl.multiple_of(h * 2 * HD, 2 * HD), 2 * HD), :] += mm(kv, tok_ref[span, :])
        bias[h, 0] += mm_nt(ones, kv[HD:])
        for u in range(per_block):
            d = which * per_block + u
            kv_send[h, d] = kv[:, u * rows:(u + 1) * rows]

            @pl.when(d != me)
            def _():
                kv_copy(h, d, me, lax.rem(d + blocks - me, blocks)).start()

            @pl.when(d == me)
            def _():
                kv_ref[me, h] = kv[:, u * rows:(u + 1) * rows]

        @pl.when(i == k_blocks - 1)
        def _():
            for n in range(blocks):
                gq_send[h, n] = (gq_acc[n * rows:(n + 1) * rows, :HD] * (HD ** -0.5)).T.astype(BF16)
            for r in range(1, blocks):
                gq_copy(h, at.peer(r), me, r).start()
            gq_ref[me, h] = gq_send[h, me]

        for which_group, number, t in timed:
            pl.when(step == t)(functools.partial(advance, which_group, number))
        return carry

    lax.fori_loop(0, total_steps, block, 0)

    q_base = heads * 2 * HD
    for h in range(heads):
        part = jnp.zeros((HD, width), F32)
        q_bias = jnp.zeros((8, HD), F32)
        for n in range(blocks):
            low = gq_send[h, n]
            part = part + mm(low, tok_ref[n * rows:(n + 1) * rows, :])
            q_bias = q_bias + mm_nt(jnp.ones((8, rows), BF16), low)
        dwt[q_base + h * HD:q_base + (h + 1) * HD, :] = part
        bias[h, 1] = q_bias
    half = dwt.shape[0] // 2
    my_core = lax.rem(at.doc, 2)
    w_sum = Summer(at, dwt, sent_w, came_w, qkv_ref, 0, 0, 2 * half, [("docs", 1)], rest, w_sems,
                   out_shift=my_core * (half * group - half) + member * half)
    w_back = [s for s in w_sum.back if w_sum.stages[s][0] == "planes"]
    w_chain = w_sum.events(w_back)
    w_chain[0]()
    lane = lax.broadcasted_iota(jnp.int32, (8, width), 1)
    sub = lax.broadcasted_iota(jnp.int32, (8, width), 0)
    wide = [jnp.concatenate([bias[h, i] for h in range(heads)] * group, axis=1) for i in range(2)]
    small_sent[0, 16:24, :] = jnp.where(
        (lane // cols) == member, jnp.where(sub == 0, wide[1], jnp.where(sub == 1, wide[0], 0.0)), 0.0)
    small_order = [("docs", 1)] + [("blk", bit) for bit in bits_of(blocks)] + rest

    def small_copy(s):
        return send_to(small_sent.at[s], small_came.at[s], small_sems.at[0, s], small_sems.at[1, s],
                       at.pair(*small_order[s])[0])

    def small_step(s):
        small_copy(s).wait_recv()
        total = small_sent[s] + small_came[s]
        if s + 1 < len(small_order):
            small_sent[s + 1] = total
            small_copy(s + 1).start()
        else:
            small_out[...] = total

    small_copy(0).start()

    def slab(m):
        return rows_of(my_core * half * group + m * half, half)

    def wide_copy(k, m):
        to = plane * group + lax.rem(member + k, group)
        return send_to(qkv_ref.at[slab(m)], qkv_ref.at[slab(m)], wide_sems.at[0, k], wide_sems.at[1, k],
                       {"blk": to})

    def core_copy(core):
        span = rows_of(core * half * group, half * group)
        return send_to(qkv_ref.at[span], qkv_ref.at[span], core_sems.at[0], core_sems.at[1],
                       at.pair("docs", 1)[0])

    def wide_start():
        for k in range(1, group):
            wide_copy(k, member).start()

    def wide_wait():
        for k in range(1, group):
            wide_copy(k, lax.rem(member + group - k, group)).wait_recv()
        core_copy(my_core).start()

    w_events = w_chain[1:] + [wide_start, wide_wait]
    left = [[functools.partial(advance, which, step) for step in range(done[which], len(chains[groups[which][0]]))]
            for which in range(2)]
    small_events = [functools.partial(small_step, s) for s in range(len(small_order))]
    lanes_of_work = [w_events, left[0], left[1], small_events]
    for e in range(max(len(work) for work in lanes_of_work)):
        for work in lanes_of_work:
            if e < len(work):
                work[e]()
    core_copy(1 - my_core).wait_recv()

    for h in range(heads):
        for r in range(1, blocks):
            kv_copy(h, at.source(r), at.source(r), r).wait_recv()
            gq_copy(h, at.source(r), at.source(r), r).wait_recv()
    for r in range(1, blocks):
        g_copy(r, at.peer(r), me).wait_send()
        for h in range(heads):
            kv_copy(h, at.peer(r), me, r).wait_send()
            gq_copy(h, at.peer(r), me, r).wait_send()
    for part in sums:
        part.drain(part.back)
    w_sum.drain(w_back)
    for k in range(1, group):
        wide_copy(k, member).wait_send()
    core_copy(my_core).wait_send()
    for s in range(len(small_order)):
        small_copy(s).wait_send()


EVENT_STEPS = ({2: 2, 3: 5, 4: 8, 5: 11, 6: 13}, {2: 4, 3: 7, 4: 10, 5: 14})


def main(docs, blocks, group, tokens, att_in, cotangent, lengths, weights, attention, collective_id,
         k_block=256, q_tile=512):
    q = attention[0]
    heads, length_all, _ = q.shape
    slots, rows, width = tokens.shape
    count = slots * rows
    inner_width = weights[4].shape[1]
    features = -(-3 * heads * HD // 128) * 128
    unit = 32 * blocks
    second = -(-(inner_width + width) // unit)
    first = inner_width // 2
    split = second // 2 * unit
    cuts = [(0, first), (first, first), (inner_width, split), (inner_width + split, second * unit - split)]
    total = inner_width + second * unit
    members, rest, planes = len(bits_of(group)), len(bits_of(docs)) - 1, blocks // group
    sizes = [Summer.placed(size, 1 + members, planes, rest) for _, size in cuts]
    placed = sum(sizes)
    w_placed = Summer.placed(features, 1, planes, rest)
    stages = 2 + members + rest
    steps = len(bits_of(docs)) + len(bits_of(blocks))
    dma, vmem = pltpu.SemaphoreType.DMA, pltpu.VMEM
    return pl.pallas_call(
        functools.partial(main_kernel, docs, blocks, group, cuts, k_block, q_tile),
        out_shape=(
            jax.ShapeDtypeStruct((slots, rows, width), F32),
            jax.ShapeDtypeStruct((count, width), F32),
            jax.ShapeDtypeStruct((blocks, heads, 2 * HD, rows), BF16),
            jax.ShapeDtypeStruct((blocks, heads, HD, rows), BF16),
            jax.ShapeDtypeStruct((total, width), BF16),
            jax.ShapeDtypeStruct((features * group, width), BF16),
            jax.ShapeDtypeStruct((24, width), F32),
        ),
        in_specs=[VMEM] * 3 + [SMEM] + [VMEM] * 4 + [ANY, VMEM, ANY] + [VMEM] * 8,
        out_specs=(VMEM,) * 7,
        scratch_shapes=[
            vmem((count, width), BF16),
            vmem((width, count), BF16),
            vmem(att_in.shape, BF16),
            vmem(att_in.shape, BF16),
            vmem((heads, length_all, LANES), BF16),
            vmem((heads, length_all, LANES), BF16),
            vmem((heads, HD, length_all), BF16),
            vmem((heads, HD, length_all), BF16),
            vmem((length_all, LANES), F32),
            vmem((heads, blocks, 2 * HD, rows), BF16),
            vmem((heads, blocks, HD, rows), BF16),
            vmem((total, width), F32),
            vmem((max(placed, 2 * inner_width), width), BF16),
            vmem((placed, width), BF16),
            vmem((features, width), F32),
            vmem((w_placed, width), BF16),
            vmem((w_placed, width), BF16),
            vmem((heads, 2, 8, HD), F32),
            vmem((steps, 24, width), F32),
            vmem((steps, 24, width), F32),
            dma((2, blocks)),
            dma((2, heads, blocks)),
            dma((2, heads, blocks)),
            dma((len(cuts), 2, 2, stages, planes)),
            dma((2, 2, 2 + rest, planes)),
            dma((2, steps)),
            dma((2, group)),
            dma((2,)),
            dma((inner_width // width + 1,)),
        ],
        compiler_params=params(collective_id),
    )(tokens, att_in, cotangent, lengths, *weights, *attention)


def last_kernel(group, kv_ref, gq_ref, gz_ref, wq_ref, wk_ref, wv_ref, sum_ref, small_ref, qkv_ref,
                grad_ref, qw_ref, qb_ref, kw_ref, vw_ref, vb_ref, ow_ref, ob_ref, g1_ref, s1_ref,
                uw_ref, ub_ref, dw_ref, db_ref, g2_ref, s2_ref, across, stack):
    blocks, heads, _, rows = kv_ref.shape
    slots = blocks // group
    width = wq_ref.shape[0]
    inner_width = uw_ref.shape[1]
    cols = heads * HD

    def widen(out, rows_out, cols_out, base):
        step = row_tile(rows_out)

        def run(i, carry):
            span = pl.ds(pl.multiple_of(i * step, step), step)
            out[span, cols_out] = sum_ref[pl.ds(pl.multiple_of(base + i * step, 16), step), :].astype(F32)
            return carry

        lax.fori_loop(0, rows_out // step, run, 0)

    widen(dw_ref, inner_width, slice(None), 0)
    for c in range(inner_width // width):
        widen(uw_ref, width, slice(c * width, (c + 1) * width), inner_width + c * width)
    widen(ow_ref, width, slice(None), 2 * inner_width)
    total = gz_ref[...]
    for which, w_ref in enumerate((wq_ref, wk_ref, wv_ref)):
        for s in range(slots):
            for g in range(group):
                for h in range(heads):
                    low = gq_ref[s * group + g, h] if which == 0 else (
                        kv_ref[s * group + g, h, (which - 1) * HD:which * HD, :])
                    across[g * cols + h * HD:g * cols + (h + 1) * HD, s * rows:(s + 1) * rows] = low
        total = total + mm_nt(across[...].T, w_ref[...])
    grad_ref[...] = total.reshape(grad_ref.shape)
    half = qkv_ref.shape[0] // group // 2
    unit = HD // 2
    for which, out in enumerate((qw_ref, kw_ref, vw_ref)):
        for g in range(group):
            for h in range(heads):
                first = heads * 2 * HD + h * HD if which == 0 else h * 2 * HD + (which - 1) * HD
                for u in range(2):
                    f = first + u * unit
                    at = f // half * half * group + g * half + f % half
                    to = g * cols + h * HD + u * unit
                    stack[to:to + unit, :] = qkv_ref[at:at + unit, :]
        out[...] = stack[...].T.astype(F32)

    def vector(out, ref, i):
        out[...] = ref[i:i + 1, :].reshape(out.shape)

    vector(qb_ref, small_ref, 16)
    vector(vb_ref, small_ref, 17)
    for i, out in enumerate((g2_ref, s2_ref, db_ref, g1_ref, s1_ref, ob_ref)):
        vector(out, small_ref, i)
    parts = inner_width // width
    ub_ref[...] = jnp.concatenate([small_ref[6 + i:7 + i, :] for i in range(parts)], axis=1).reshape(ub_ref.shape)


def last(group, shape, inner_width, *arrays):
    width = shape[-1]
    square = jax.ShapeDtypeStruct((width, width), F32)
    vector = jax.ShapeDtypeStruct((width,), F32)
    return pl.pallas_call(
        functools.partial(last_kernel, group),
        out_shape=(
            jax.ShapeDtypeStruct(shape, F32), square, vector, square, square, vector, square, vector,
            vector, vector, jax.ShapeDtypeStruct((width, inner_width), F32),
            jax.ShapeDtypeStruct((inner_width,), F32), jax.ShapeDtypeStruct((inner_width, width), F32),
            vector, vector, vector,
        ),
        in_specs=[VMEM] * len(arrays),
        out_specs=(VMEM,) * 16,
        scratch_shapes=[
            pltpu.VMEM((width, shape[0] * shape[1]), BF16),
            pltpu.VMEM((width, width), BF16),
        ],
        compiler_params=params(),
    )(*arrays)


def device_program(docs, blocks, tokens, query_weight, query_bias, key_weight, value_weight, value_bias,
                   out_weight, out_bias, first_gain, first_shift, up_weight, up_bias, down_weight,
                   down_bias, second_gain, second_shift, cotangent, lengths):
    slots, rows, width = tokens.shape
    inner_width = up_weight.shape[1]
    group = blocks // slots
    cols = width // group
    length_all = rows * blocks
    projections = (query_weight, key_weight, value_weight)
    tok_doc = gather_tokens(tokens, blocks, 0).reshape(length_all, width)
    att, q, k, v, o = attention_forward(tok_doc, projections, (query_bias, value_bias), lengths, group)
    att_in = exchange(att.reshape(blocks, rows, cols), 1)
    output, gz, kv, gq, dw, dw_qkv, small = main(
        docs, blocks, group, tokens, att_in, cotangent, lengths,
        (out_weight, out_bias, first_gain, first_shift, up_weight, up_bias, down_weight, down_bias,
         second_gain, second_shift), (q, k, v, o, tok_doc), 2)
    grads = last(group, tokens.shape, inner_width, kv, gq, gz, *projections, dw, small, dw_qkv)
    return (output, *grads)


def solution(mesh):
    split = P("docs", "blk", None)
    return jax.shard_map(
        functools.partial(device_program, mesh.shape["docs"], mesh.shape["blk"]),
        mesh=mesh,
        in_specs=(split,) + (P(),) * 15 + (split, P("docs")),
        out_specs=(split, split) + (P(),) * 15,
        check_vma=False,
    )
```

```python
import functools

import jax
import jax.numpy as jnp
from jax import lax
from jax.experimental import pallas as pl
from jax.experimental.pallas import tpu as pltpu
from jax.sharding import PartitionSpec as P

HD = 64
LANES = 128
EPS = 1e-05
MASKED = -1e30
F32 = jnp.float32
BF16 = jnp.bfloat16
VMEM = pl.BlockSpec(memory_space=pltpu.VMEM)
ANY = pl.BlockSpec(memory_space=pl.ANY)
SMEM = pl.BlockSpec(memory_space=pltpu.SMEM)
MESH = pl.DeviceIdType.MESH
VMEM_LIMIT = 63 * 1024 * 1024


def mm(left, right):
    return jnp.dot(left, right, preferred_element_type=F32)


def mm_nt(left, right):
    return lax.dot_general(left, right, (((1,), (1,)), ((), ())), preferred_element_type=F32)


def mm_tn(left, right):
    return lax.dot_general(left, right, (((0,), (0,)), ((), ())), preferred_element_type=F32)


def params(collective_id=None):
    if collective_id is None:
        return pltpu.CompilerParams(vmem_limit_bytes=VMEM_LIMIT)
    return pltpu.CompilerParams(
        vmem_limit_bytes=VMEM_LIMIT, collective_id=collective_id, has_side_effects=True
    )


def greet(peers):
    barrier = pltpu.get_barrier_semaphore()
    for peer in peers:
        pl.semaphore_signal(barrier, inc=1, device_id=peer, device_id_type=MESH)
    pl.semaphore_wait(barrier, len(peers))


def send_to(src, dst, send_sem, recv_sem, peer):
    return pltpu.make_async_remote_copy(
        src_ref=src, dst_ref=dst, send_sem=send_sem, recv_sem=recv_sem,
        device_id=peer, device_id_type=MESH,
    )


def gather_kernel(slots, group, tok_ref, cot_ref, out_ref, cot_out, low, cot_low, send_a, recv_a, send_b, recv_b,
                  send_c, recv_c):
    me = lax.axis_index("blk")
    plane, member = me // group, lax.rem(me, group)
    planes = [lax.rem(plane + k, slots) for k in range(1, slots)]
    members = [lax.rem(member + k, group) for k in range(1, group)]
    greet([{"blk": p * group + member} for p in planes]
          + [{"blk": plane * group + m} for m in members])
    low[...] = tok_ref[...].astype(BF16)
    first = []
    for k in range(1, slots):
        target = planes[k - 1]
        copy = send_to(low.at[target], out_ref.at[me], send_a.at[k], recv_a.at[k],
                       {"blk": target * group + member})
        copy.start()
        first.append(copy)
    out_ref[me] = low[plane]
    second = []
    for k in range(slots):
        source = lax.rem(plane + slots - k, slots)
        block = source * group + member
        if k == 1:
            cot_low[...] = cot_ref[...].astype(BF16)
            for j in range(1, slots):
                target = planes[j - 1]
                copy = send_to(cot_low.at[target], cot_out.at[plane], send_c.at[j], recv_c.at[j],
                               {"blk": target * group + member})
                copy.start()
                first.append(copy)
            cot_out[plane] = cot_low[plane]
        if k > 0:
            send_to(low.at[plane], out_ref.at[block], send_a.at[k], recv_a.at[k],
                    {"blk": block}).wait_recv()
        for j in range(1, group):
            copy = send_to(out_ref.at[block], out_ref.at[block], send_b.at[k, j], recv_b.at[k, j],
                           {"blk": plane * group + members[j - 1]})
            copy.start()
            second.append(copy)
    for k in range(slots):
        source = lax.rem(plane + slots - k, slots)
        for j in range(1, group):
            block = source * group + lax.rem(member + group - j, group)
            send_to(out_ref.at[block], out_ref.at[block], send_b.at[k, j], recv_b.at[k, j],
                    {"blk": plane * group + members[j - 1]}).wait_recv()
    for k in range(1, slots):
        source = lax.rem(plane + slots - k, slots)
        send_to(cot_low.at[plane], cot_out.at[source], send_c.at[k], recv_c.at[k],
                {"blk": source * group + member}).wait_recv()
    for copy in first + second:
        copy.wait_send()


def gather_tokens(tokens, cotangent, blocks, collective_id):
    slots, rows, width = tokens.shape
    group = blocks // slots
    dma = pltpu.SemaphoreType.DMA
    return pl.pallas_call(
        functools.partial(gather_kernel, slots, group),
        out_shape=(jax.ShapeDtypeStruct((blocks, rows, width), BF16),
                   jax.ShapeDtypeStruct((slots, rows, width), BF16)),
        in_specs=[VMEM, VMEM],
        out_specs=(VMEM, VMEM),
        scratch_shapes=[
            pltpu.VMEM((slots, rows, width), BF16),
            pltpu.VMEM((slots, rows, width), BF16),
            dma((slots,)), dma((slots,)), dma((slots, group)), dma((slots, group)), dma((slots,)), dma((slots,)),
        ],
        compiler_params=params(collective_id),
    )(tokens, cotangent)


def exchange_kernel(planes, group, src_ref, out_ref, send_sem, recv_sem):
    me = lax.axis_index("blk")
    plane, member = me // group, lax.rem(me, group)
    members = [lax.rem(member + k, group) for k in range(1, group)]
    greet([{"blk": plane * group + m} for m in members])
    copies = []
    for k in range(1, group):
        copy = send_to(src_ref.at[:, members[k - 1]], out_ref.at[member], send_sem.at[k], recv_sem.at[k],
                       {"blk": plane * group + members[k - 1]})
        copy.start()
        copies.append(copy)
    for p in range(planes):
        out_ref[member, p] = src_ref[p, member]
    for k in range(1, group):
        source = lax.rem(member + group - k, group)
        send_to(src_ref.at[:, member], out_ref.at[source], send_sem.at[k], recv_sem.at[k],
                {"blk": plane * group + source}).wait_recv()
    for copy in copies:
        copy.wait_send()


def exchange(array, collective_id):
    planes, group, rows, cols = array.shape
    return pl.pallas_call(
        functools.partial(exchange_kernel, planes, group),
        out_shape=jax.ShapeDtypeStruct((group, planes, rows, cols), array.dtype),
        in_specs=[VMEM],
        out_specs=VMEM,
        scratch_shapes=[pltpu.SemaphoreType.DMA((group,)), pltpu.SemaphoreType.DMA((group,))],
        compiler_params=params(collective_id),
    )(array)


def row(ref):
    return ref[...].astype(F32).reshape(1, ref.shape[0])


def own_columns(ref, member, cols):
    if cols % LANES == 0:
        return ref[:, pl.ds(pl.multiple_of(member * cols, LANES), cols)]
    per = LANES // cols
    both = ref[:, pl.ds(pl.multiple_of(member // per * LANES, LANES), LANES)].astype(F32)
    return sum(jnp.where(lax.rem(member, per) == i, both[:, i * cols:(i + 1) * cols], 0.0)
               for i in range(per)).astype(BF16)


def own_entries(ref, member, cols):
    values = row(ref)
    return sum(jnp.where(member == i, values[:, i * cols:(i + 1) * cols], 0.0)
               for i in range(ref.shape[0] // cols))


def forward_kernel(group, q_block, tok_ref, wq_ref, wk_ref, wv_ref, qb_ref, vb_ref, len_ref,
                   att_ref, q_ref, k_ref, v_ref, o_ref, vt, w_ref):
    total, width = w_ref.shape[1] // 3, w_ref.shape[0]
    heads = total // HD
    length_all = tok_ref.shape[0]
    me = lax.axis_index("blk")
    plane, member = me // group, lax.rem(me, group)
    doc_len = len_ref[plane]
    chunk = min(512, length_all)
    for i, ref in enumerate((wq_ref, wk_ref, wv_ref)):
        w_ref[:, i * total:(i + 1) * total] = own_columns(ref, member, total)
    bias = jnp.concatenate(
        [own_entries(qb_ref, member, total), jnp.zeros((1, total), F32),
         own_entries(vb_ref, member, total)], axis=1)

    def project(step, carry):
        rows = pl.ds(step * chunk, chunk)
        qkv = mm(tok_ref[rows, :], w_ref[...]) + bias
        lane = lax.broadcasted_iota(jnp.int32, (chunk, LANES), 1)
        row = step * chunk + lax.broadcasted_iota(jnp.int32, (chunk, LANES), 0)
        mask = jnp.where(row < doc_len, 0.0, MASKED)
        for h in range(heads):
            def part(which):
                cols = qkv[:, which * total + h * HD:which * total + (h + 1) * HD]
                return jnp.concatenate([cols, jnp.zeros_like(cols)], axis=1)
            q_ref[h, rows, :] = jnp.where(
                lane == HD, 1.0, part(0).astype(BF16).astype(F32) * (HD ** -0.5)).astype(BF16)
            k_ref[h, rows, :] = jnp.where(
                lane == HD, mask, jnp.where((lane > HD) & (lane < HD + 4), 1.0, part(1))).astype(BF16)
            v_rows = jnp.where((lane >= HD) & (lane < HD + 4), 1.0, part(2)).astype(BF16)
            v_ref[h, rows, :] = v_rows
            vt[h, :, rows] = v_rows.T
        return carry

    lax.fori_loop(0, length_all // chunk, project, 0)

    def block(step, carry):
        rows = pl.ds(step * q_block, q_block)
        for h in range(heads):
            scores = mm_nt(k_ref[h], q_ref[h, rows, :])
            top = jnp.max(scores, axis=0, keepdims=True)
            weights = jnp.exp(scores - top).astype(BF16)
            mixed = mm(vt[h], weights)
            denom = mixed[HD:HD + 1, :]
            scaled = mixed * (1.0 / denom)
            sub = lax.broadcasted_iota(jnp.int32, scaled.shape, 0)
            o_rows = jnp.where(sub == HD, top + jnp.log(denom), scaled).T
            o_ref[h, rows, :] = o_rows
            att_ref[rows, h * HD:(h + 1) * HD] = o_rows[:, :HD].astype(BF16)
        return carry

    lax.fori_loop(0, length_all // q_block, block, 0)


def attention_forward(tok_doc, weights, biases, lengths, group, q_block=256):
    length_all, width = tok_doc.shape
    total = width // group
    heads = total // HD
    per_head = jax.ShapeDtypeStruct((heads, length_all, LANES), BF16)
    return pl.pallas_call(
        functools.partial(forward_kernel, group, q_block),
        out_shape=(
            jax.ShapeDtypeStruct((length_all, total), BF16),
            per_head, per_head, per_head,
            jax.ShapeDtypeStruct((heads, length_all, LANES), F32),
        ),
        in_specs=[VMEM] * 6 + [SMEM],
        out_specs=(VMEM,) * 5,
        scratch_shapes=[
            pltpu.VMEM((heads, LANES, length_all), BF16),
            pltpu.VMEM((width, 3 * total), BF16),
        ],
        compiler_params=params(),
    )(tok_doc, *weights, *biases, lengths)


def three(value):
    high = value.astype(BF16).astype(F32)
    mid = (value - high).astype(BF16).astype(F32)
    return high, mid, value - high - mid


def row_tile(rows):
    return next(t for t in (96, 64, 48, 32, 16) if rows % t == 0)


def over_rows(rows, body):
    step = row_tile(rows)

    def run(i, carry):
        body(i * step, step)
        return carry

    lax.fori_loop(0, rows // step, run, 0)


def rows_at(offset, i, step):
    return pl.ds(pl.multiple_of(offset + i, 16), step)


def rows_of(offset, n):
    return pl.ds(pl.multiple_of(offset, 16), n)


def bits_of(size):
    return [1 << i for i in range(size.bit_length() - 1)]


class Place:
    def __init__(self, docs, blocks, group):
        self.docs, self.blocks, self.group = docs, blocks, group
        self.planes = blocks // group
        self.me, self.doc = lax.axis_index("blk"), lax.axis_index("docs")
        self.plane, self.member = self.me // group, lax.rem(self.me, group)

    def pair(self, axis, bit):
        mine = self.me if axis == "blk" else self.doc
        on = lax.rem(mine // bit, 2)
        return {axis: mine + bit - 2 * bit * on}, on

    def member_peer(self, k):
        return lax.rem(self.member + k, self.group)

    def member_source(self, k):
        return lax.rem(self.member + self.group - k, self.group)

    def in_plane(self, member):
        return {"blk": self.plane * self.group + member}

    def in_line(self, plane):
        return {"blk": plane * self.group + self.member}

    def plane_peer(self, k):
        return lax.rem(self.plane + k, self.planes)

    def plane_source(self, k):
        return lax.rem(self.plane + self.planes - k, self.planes)


class Summer:
    def __init__(self, at, acc, sent, came, out, place, offset, rows, pairs, rest, sems, out_shift=0):
        self.at, self.acc, self.sent, self.came, self.out, self.sems = at, acc, sent, came, out, sems
        self.shift = out_shift
        self.stages = []
        for axis, bit in pairs:
            to, on = at.pair(axis, bit)
            n = rows // 2
            self.stages.append(("pair", to, n, offset + (1 - on) * n, offset + on * n, place))
            offset, rows, place = offset + on * n, n, place + n
        n = rows // at.planes
        self.stages.append(("planes", None, n, offset, offset + at.plane * n, place))
        offset, rows, place = offset + at.plane * n, n, place + (at.planes - 1) * n
        for axis, bit in rest:
            self.stages.append(("full", at.pair(axis, bit)[0], rows, offset, offset, place))
            place += rows
        self.count = len(self.stages)
        self.back = [s for s in range(self.count) if self.stages[s][0] != "full"][::-1]

    @staticmethod
    def placed(rows, pairs, planes, rest):
        total = 0
        for _ in range(pairs):
            rows //= 2
            total += rows
        rows //= planes
        return total + (planes - 1 + rest) * rows

    def copies(self, s, back=False, receive=False):
        kind, to, n, give, keep, place = self.stages[s]
        at, out = self.at, self.out
        w = 1 if back else 0
        if kind == "planes":
            found = []
            for k in range(1, at.planes):
                if back:
                    which = at.plane_source(k) if receive else at.plane
                    span = rows_of(give + which * n + self.shift, n)
                    src, dst = out.at[span], out.at[span]
                else:
                    src, dst = (ref.at[rows_of(place + (k - 1) * n, n)] for ref in (self.sent, self.came))
                to = at.in_line(at.plane_peer(k))
                found.append(send_to(src, dst, self.sems.at[w, 0, s, k], self.sems.at[w, 1, s, k], to))
            return found
        if back:
            span = rows_of((give if receive else keep) + self.shift, n)
            src, dst = out.at[span], out.at[span]
        else:
            src, dst = self.sent.at[rows_of(place, n)], self.came.at[rows_of(place, n)]
        return [send_to(src, dst, self.sems.at[w, 0, s, 0], self.sems.at[w, 1, s, 0], to)]

    def pack(self, give, place, n):
        def run(i, step):
            self.sent[rows_at(place, i, step), :] = self.acc[rows_at(give, i, step), :].astype(BF16)
        over_rows(n, run)

    def start(self, s):
        kind, to, n, give, keep, place = self.stages[s]
        if kind == "planes":
            for k in range(1, self.at.planes):
                self.pack(give + self.at.plane_peer(k) * n, place + (k - 1) * n, n)
        else:
            self.pack(give, place, n)
        for copy in self.copies(s):
            copy.start()

    def finish(self, s):
        kind, to, n, give, keep, place = self.stages[s]
        for copy in self.copies(s):
            copy.wait_recv()
        parts = self.at.planes - 1 if kind == "planes" else 1
        last = s == self.count - 1

        def run(i, step):
            total = self.acc[rows_at(keep, i, step), :]
            if kind == "full":
                total = total.astype(BF16).astype(F32)
            for k in range(parts):
                total = total + self.came[rows_at(place + k * n, i, step), :].astype(F32)
            if last:
                self.out[rows_at(keep + self.shift, i, step), :] = total.astype(BF16)
            else:
                self.acc[rows_at(keep, i, step), :] = total
        over_rows(n, run)

    def start_back(self, s):
        for copy in self.copies(s, back=True):
            copy.start()

    def finish_back(self, s):
        for copy in self.copies(s, back=True, receive=True):
            copy.wait_recv()

    def events(self, back):
        def first():
            self.start(0)

        def inward(s):
            self.finish(s)
            if s + 1 < self.count:
                self.start(s + 1)
            elif back:
                self.start_back(back[0])

        def outward(d):
            self.finish_back(back[d])
            if d + 1 < len(back):
                self.start_back(back[d + 1])

        return ([first] + [functools.partial(inward, s) for s in range(self.count)]
                + [functools.partial(outward, d) for d in range(len(back))])

    def drain(self, back):
        for s in range(self.count):
            for copy in self.copies(s):
                copy.wait_send()
        for s in back:
            for copy in self.copies(s, back=True):
                copy.wait_send()


def row_mean(value):
    return jnp.mean(value, axis=1, keepdims=True)


def col_sum(value):
    return jnp.sum(value, axis=0, keepdims=True)


def main_kernel(docs, blocks, group, cuts, k_block, q_tile,
                att_in, cot_ref, len_ref, wo_ref, ob_ref, g1_ref, s1_ref, up_hbm, ub_ref, down_hbm,
                db_ref, g2_ref, s2_ref, wq_ref, wk_ref, wv_ref, q_ref, k_ref, v_ref, o_ref, tok_ref,
                out_in, grad_in, sum_ref, qkv_ref, small_out,
                att, hid_t, gz, away, kv_in, gq_in, g_att, g_in, qx, gx, qt, gt, gq_acc, kv_send, gq_send,
                acc, sent, came, dwt, sent_w, came_w, bias, small_sent, small_came,
                g_sems, kv_sems, gq_sems, sum_sems, w_sems, small_sems, wide_sems, core_sems, load_sems,
                out_sems, grad_sems):
    at = Place(docs, blocks, group)
    me, member, plane, planes = at.me, at.member, at.plane, at.planes
    _, rows, width = tok_ref.shape
    count = planes * rows
    cols = width // group
    inner_width = up_hbm.shape[1]
    heads, length_all, _ = q_ref.shape
    parts = inner_width // width
    doc_bits, member_bits = bits_of(docs), bits_of(group)

    loads = [pltpu.make_async_copy(up_hbm.at[:, c * width:(c + 1) * width],
                                   sent.at[inner_width + c * width:inner_width + (c + 1) * width], load_sems.at[c])
             for c in range(parts)]
    loads.append(pltpu.make_async_copy(down_hbm, sent.at[:inner_width], load_sems.at[parts]))
    for load in loads:
        load.start()

    def up_part(c):
        return sent[inner_width + c * width:inner_width + (c + 1) * width, :]

    greet([at.in_plane(at.member_peer(k)) for k in range(1, group)]
          + [at.in_line(at.plane_peer(k)) for k in range(1, planes)]
          + [at.pair("docs", bit)[0] for bit in doc_bits])

    rest = [("docs", bit) for bit in doc_bits[1:]]
    sums, place = [], 0
    for c, (offset, size) in enumerate(cuts):
        turn = c % len(member_bits)
        pairs = [("docs", 1)] + [("blk", bit) for bit in member_bits[turn:] + member_bits[:turn]]
        sums.append(Summer(at, acc, sent, came, sum_ref, place, offset, size, pairs, rest, sum_sems.at[c]))
        place = place + Summer.placed(size, len(pairs), planes, len(rest))
    chains = [s.events(s.back) for s in sums]
    groups = [[c for c in range(len(cuts)) if cuts[c][0] < inner_width],
              [c for c in range(len(cuts)) if cuts[c][0] >= inner_width]]

    def advance(which, step):
        for c in groups[which]:
            chains[c][step]()

    flat = jnp.concatenate([tok_ref[p * group + member].astype(F32) for p in range(planes)], axis=0)
    for p in range(planes):
        for g in range(group):
            att[p * rows:(p + 1) * rows, g * cols:(g + 1) * cols] = att_in[g, p]
    up_bias = row(ub_ref)
    gain1, gain2 = row(g1_ref), row(g2_ref)
    summed = flat + mm(att[...], wo_ref[...]) + row(ob_ref)
    centred = summed - row_mean(summed)
    rstd1 = lax.rsqrt(row_mean(centred * centred) + EPS)
    xhat1 = centred * rstd1
    hidden = xhat1 * gain1 + row(s1_ref)
    hidden_low = hidden.astype(BF16)
    hid_t[...] = hidden_low.T
    for load in loads:
        load.wait()
    ffn = jnp.zeros((count, width), F32)
    for c in range(parts):
        span = slice(c * width, (c + 1) * width)
        inner = mm(hidden_low, up_part(c)) + up_bias[:, span]
        square = inner * inner
        slope_in = 0.7978845608 * (1.0 + (3 * 0.044715) * square)
        tanh = jnp.tanh(inner * (0.7978845608 * (1.0 + 0.044715 * square)))
        half = 0.5 * (1.0 + tanh)
        acc[c * count:(c + 1) * count, :] = half + (0.5 * inner) * ((1.0 - tanh * tanh) * slope_in)
        low = (inner * half).astype(BF16)
        sum_ref[c * count:(c + 1) * count, :] = low
        ffn = ffn + mm(low, sent[span, :])
    summed = flat + hidden + ffn + row(db_ref)
    centred = summed - row_mean(summed)
    rstd2 = lax.rsqrt(row_mean(centred * centred) + EPS)
    xhat2 = centred * rstd2
    away[...] = (xhat2 * gain2 + row(s2_ref)).astype(BF16).reshape(planes, rows, width)

    def line_copies(dst, sems, receive=False):
        return [send_to(away.at[at.plane_peer(k)], dst.at[at.plane_source(k) if receive else plane],
                        sems.at[0, k], sems.at[1, k], at.in_line(at.plane_peer(k))) for k in range(1, planes)]

    for copy in line_copies(out_in, out_sems):
        copy.start()
    out_in[plane] = away[plane]
    lane_r = lax.broadcasted_iota(jnp.int32, (rows, width), 0)
    g_out = jnp.concatenate(
        [jnp.where((p * group + member) * rows + lane_r < len_ref[plane], cot_ref[p].astype(F32), 0.0)
         for p in range(planes)], axis=0)
    small_sent[0] = jnp.zeros(small_sent.shape[1:], F32)
    small_sent[0, 0:1, :] = col_sum(g_out * xhat2)
    small_sent[0, 1:2, :] = col_sum(g_out)
    scaled = g_out * gain2
    g_z2 = rstd2 * (scaled - row_mean(scaled) - xhat2 * row_mean(scaled * xhat2))
    g_ffn = g_z2.astype(BF16)
    small_sent[0, 2:3, :] = col_sum(g_ffn.astype(F32))
    g_hidden = g_z2
    for c in range(parts):
        span = slice(c * width, (c + 1) * width)
        g_inner = (mm_nt(g_ffn, sent[span, :]) * acc[c * count:(c + 1) * count, :]).astype(BF16)
        sum_ref[inner_width + c * count:inner_width + (c + 1) * count, :] = g_inner
        g_hidden = g_hidden + mm_nt(g_inner, up_part(c))
    scaled = g_hidden * gain1
    g_z1 = rstd1 * (scaled - row_mean(scaled) - xhat1 * row_mean(scaled * xhat1))
    g_branch = g_z1.astype(BF16)
    gz[...] = g_z1 + g_z2
    g_low = mm_nt(g_branch, wo_ref[...]).astype(BF16)
    for p in range(planes):
        for g in range(group):
            g_att[g, p] = g_low[p * rows:(p + 1) * rows, g * cols:(g + 1) * cols]

    def g_copy(k, receive=False):
        slot = at.member_source(k) if receive else member
        return send_to(g_att.at[at.member_peer(k)], g_in.at[:, slot], g_sems.at[0, k], g_sems.at[1, k],
                       at.in_plane(at.member_peer(k)))

    for k in range(1, group):
        g_copy(k).start()
    for p in range(planes):
        g_in[p, member] = g_att[member, p]

    for c in range(parts):
        span = slice(c * width, (c + 1) * width)
        acc[span, :] = mm_tn(sum_ref[c * count:(c + 1) * count, :], g_ffn)
    advance(0, 0)
    for c in range(parts):
        g_inner = sum_ref[inner_width + c * count:inner_width + (c + 1) * count, :]
        small_sent[0, 6 + c:7 + c, :] = col_sum(g_inner.astype(F32))
        acc[inner_width + c * width:inner_width + (c + 1) * width, :] = mm(hid_t[...], g_inner)
    acc[2 * inner_width:2 * inner_width + width, :] = mm_tn(att[...], g_branch)
    if acc.shape[0] > 2 * inner_width + width:
        acc[2 * inner_width + width:, :] = jnp.zeros((acc.shape[0] - 2 * inner_width - width, width), F32)
    advance(0, 1)
    advance(1, 0)
    small_sent[0, 3:4, :] = col_sum(g_hidden * xhat1)
    small_sent[0, 4:5, :] = col_sum(g_hidden)
    small_sent[0, 5:6, :] = col_sum(g_branch.astype(F32))
    chunk = group * rows
    lane = lax.broadcasted_iota(jnp.int32, (chunk, LANES), 1)

    def prepare_q(step, carry):
        span = pl.ds(pl.multiple_of(step * chunk, chunk), chunk)
        for h in range(heads):
            q_rows = q_ref[h, span, :].astype(F32)
            ext = q_rows
            for i, value in enumerate(three(-o_ref[h, span, HD:HD + 1])):
                ext = jnp.where(lane == HD + 1 + i, value, ext)
            qx[h, span, :] = ext.astype(BF16)
            qt[h, :, span] = q_rows[:, :HD].T.astype(BF16)
        return carry

    lax.fori_loop(0, planes, prepare_q, 0)
    for k in range(1, group):
        g_copy(k, True).wait_recv()

    def prepare_g(step, carry):
        span = pl.ds(pl.multiple_of(step * chunk, chunk), chunk)
        g_block = g_in[step].reshape(chunk, cols)
        for h in range(heads):
            g_rows = g_block[:, h * HD:(h + 1) * HD].astype(F32)
            g_rows = jnp.concatenate([g_rows, jnp.zeros_like(g_rows)], axis=1)
            delta = jnp.sum(g_rows * o_ref[h, span, :], axis=1, keepdims=True)
            ext = g_rows
            for i, value in enumerate(three(-delta)):
                ext = jnp.where(lane == HD + i, value, ext)
            gx[h, span, :] = ext.astype(BF16)
            gt[h, :, span] = g_rows[:, :HD].T.astype(BF16)
        return carry

    lax.fori_loop(0, planes, prepare_g, 0)
    for which, number in EVENTS_BEFORE:
        advance(which, number)

    k_blocks = length_all // k_block
    per_block = k_block // rows
    ones = jnp.ones((8, k_block), BF16)
    dwt[...] = jnp.zeros_like(dwt)
    bias[...] = jnp.zeros_like(bias)

    def kv_copy(h, p, g, slot, r):
        return send_to(kv_send.at[h, p, g], kv_in.at[slot, h, p], kv_sems.at[0, h, p, r], kv_sems.at[1, h, p, r],
                       at.in_plane(g))

    def gq_copy(h, r, receive=False):
        slot = at.member_source(r) if receive else member
        return send_to(gq_send.at[h, :, at.member_peer(r)], gq_in.at[slot, h], gq_sems.at[0, h, r],
                       gq_sems.at[1, h, r], at.in_plane(at.member_peer(r)))

    total_steps = heads * k_blocks
    timed = [(which, step, t) for which, table in enumerate(EVENT_STEPS) for step, t in table.items()
             if t < total_steps]
    done = [max([1 - which] + [n for w, n in EVENTS_BEFORE if w == which] + [n for w, n, _ in timed if w == which]) + 1
            for which in range(2)]

    def block(step, carry):
        h, i = step // k_blocks, lax.rem(step, k_blocks)
        which = lax.rem(i + member // per_block + 1, k_blocks)
        span = pl.ds(pl.multiple_of(which * k_block, k_block), k_block)
        k_rows, v_rows = k_ref[h, span, :], v_ref[h, span, :]

        @pl.when(i == 0)
        def _():
            gq_acc[...] = jnp.zeros_like(gq_acc)

        gk = jnp.zeros((HD, k_block), F32)
        gv = jnp.zeros((HD, k_block), F32)
        for t in range(length_all // q_tile):
            tile = slice(t * q_tile, (t + 1) * q_tile)
            weights = jnp.exp(mm_nt(qx[h, tile, :], k_rows))
            centred = mm_nt(gx[h, tile, :], v_rows)
            g_scores = (weights * centred).astype(BF16)
            gv = gv + mm(gt[h, :, tile], weights.astype(BF16))
            gk = gk + mm(qt[h, :, tile], g_scores)
            gq_acc[tile, :] += mm(g_scores, k_rows)
        kv = jnp.concatenate([gk, gv], axis=0).astype(BF16)
        tok_rows = tok_ref[pl.ds(which * per_block, per_block)].reshape(k_block, width)
        dwt[pl.ds(pl.multiple_of(h * 2 * HD, 2 * HD), 2 * HD), :] += mm(kv, tok_rows)
        bias[h, 0] += mm_nt(ones, kv[HD:])
        for u in range(per_block):
            d = which * per_block + u
            p, g = d // group, lax.rem(d, group)
            kv_send[h, p, g] = kv[:, u * rows:(u + 1) * rows]

            @pl.when(g != member)
            def _():
                kv_copy(h, p, g, member, lax.rem(g + group - member, group)).start()

            @pl.when(g == member)
            def _():
                kv_in[member, h, p] = kv[:, u * rows:(u + 1) * rows]

        @pl.when(i == k_blocks - 1)
        def _():
            for n in range(blocks):
                gq_send[h, n // group, n % group] = (
                    gq_acc[n * rows:(n + 1) * rows, :HD] * (HD ** -0.5)).T.astype(BF16)
            for r in range(1, group):
                gq_copy(h, r).start()
            for p in range(planes):
                gq_in[member, h, p] = gq_send[h, p, member]

        for which_group, number, t in timed:
            pl.when(step == t)(functools.partial(advance, which_group, number))
        return carry

    lax.fori_loop(0, total_steps, block, 0)

    q_base = heads * 2 * HD
    for h in range(heads):
        part = jnp.zeros((HD, width), F32)
        q_bias = jnp.zeros((8, HD), F32)
        for n in range(blocks):
            low = gq_send[h, n // group, n % group]
            part = part + mm(low, tok_ref[n])
            q_bias = q_bias + mm_nt(jnp.ones((8, rows), BF16), low)
        dwt[q_base + h * HD:q_base + (h + 1) * HD, :] = part
        bias[h, 1] = q_bias
    half = dwt.shape[0] // 2
    my_core = lax.rem(at.doc, 2)
    w_sum = Summer(at, dwt, sent_w, came_w, qkv_ref, 0, 0, 2 * half, [("docs", 1)], rest, w_sems,
                   out_shift=my_core * (half * group - half) + member * half)
    w_back = [s for s in w_sum.back if w_sum.stages[s][0] == "planes"]
    w_chain = w_sum.events(w_back)
    w_chain[0]()
    lane_w = lax.broadcasted_iota(jnp.int32, (8, width), 1)
    sub = lax.broadcasted_iota(jnp.int32, (8, width), 0)
    wide = [jnp.concatenate([bias[h, i] for h in range(heads)] * group, axis=1) for i in range(2)]
    small_sent[0, 16:24, :] = jnp.where(
        (lane_w // cols) == member, jnp.where(sub == 0, wide[1], jnp.where(sub == 1, wide[0], 0.0)), 0.0)
    small_order = [("docs", 1)] + [("blk", bit) for bit in member_bits]

    def small_copy(s):
        return send_to(small_sent.at[s], small_came.at[s], small_sems.at[0, s], small_sems.at[1, s],
                       at.pair(*small_order[s])[0])

    small_last = len(small_order)

    def small_line(k, receive=False):
        slot = small_last + k
        return send_to(small_sent.at[small_last], small_came.at[slot], small_sems.at[0, slot],
                       small_sems.at[1, slot], at.in_line(at.plane_peer(k)))

    def small_rest(i):
        slot = small_last + planes + i
        return send_to(small_sent.at[small_last + 1 + i], small_came.at[slot], small_sems.at[0, slot],
                       small_sems.at[1, slot], at.pair(*rest[i])[0])

    def small_step(s):
        small_copy(s).wait_recv()
        small_sent[s + 1] = small_sent[s] + small_came[s]
        if s + 1 < small_last:
            small_copy(s + 1).start()
        else:
            for k in range(1, planes):
                small_line(k).start()

    def small_end():
        for k in range(1, planes):
            small_line(k).wait_recv()
        total = jnp.zeros(small_sent.shape[1:], F32)
        for p in range(planes):
            value = small_sent[small_last]
            for k in range(1, planes):
                value = jnp.where(at.plane_source(k) == p, small_came[small_last + k], value)
            total = total + value
        for i in range(len(rest)):
            small_sent[small_last + 1 + i] = total
            small_rest(i).start()
            small_rest(i).wait_recv()
            total = total + small_came[small_last + planes + i]
        small_out[...] = total

    small_copy(0).start()

    def slab(m):
        return rows_of(my_core * half * group + m * half, half)

    def wide_copy(k, m):
        return send_to(qkv_ref.at[slab(m)], qkv_ref.at[slab(m)], wide_sems.at[0, k], wide_sems.at[1, k],
                       at.in_plane(at.member_peer(k)))

    def core_copy(core):
        span = rows_of(core * half * group, half * group)
        return send_to(qkv_ref.at[span], qkv_ref.at[span], core_sems.at[0], core_sems.at[1],
                       at.pair("docs", 1)[0])

    def wide_start():
        for k in range(1, group):
            wide_copy(k, member).start()

    def wide_wait():
        for k in range(1, group):
            wide_copy(k, at.member_source(k)).wait_recv()
        core_copy(my_core).start()

    def gather_part(which):
        for p in range(planes):
            for g in range(group):
                for h in range(heads):
                    low = gq_in[g, h, p] if which == 0 else kv_in[g, h, p, (which - 1) * HD:which * HD, :]
                    hid_t[g * cols + h * HD:g * cols + (h + 1) * HD, p * rows:(p + 1) * rows] = low
        return hid_t[...].T

    def key_value_rows():
        for h in range(heads):
            for p in range(planes):
                for r in range(1, group):
                    kv_copy(h, p, member, at.member_source(r), r).wait_recv()
        gz[...] += mm_nt(gather_part(1), wk_ref[...])
        gz[...] += mm_nt(gather_part(2), wv_ref[...])

    def query_rows():
        for h in range(heads):
            for r in range(1, group):
                gq_copy(h, r, True).wait_recv()
        total = gz[...] + mm_nt(gather_part(0), wq_ref[...])
        for copy in line_copies(out_in, out_sems, True):
            copy.wait_recv()
        for copy in line_copies(out_in, out_sems):
            copy.wait_send()
        away[...] = total.astype(BF16).reshape(planes, rows, width)
        for copy in line_copies(grad_in, grad_sems):
            copy.start()
        grad_in[plane] = away[plane]

    w_events = w_chain[1:] + [wide_start, wide_wait]
    left = [[functools.partial(advance, which, step) for step in range(done[which], len(chains[groups[which][0]]))]
            for which in range(2)]
    small_events = [functools.partial(small_step, s) for s in range(small_last)] + [small_end]
    lanes_of_work = [w_events, [key_value_rows, query_rows], left[0], left[1], small_events]
    for e in range(max(len(work) for work in lanes_of_work)):
        for work in lanes_of_work:
            if e < len(work):
                work[e]()
    core_copy(1 - my_core).wait_recv()
    for copy in line_copies(grad_in, grad_sems, True):
        copy.wait_recv()
    for copy in line_copies(grad_in, grad_sems):
        copy.wait_send()
    for r in range(1, group):
        g_copy(r).wait_send()
        for h in range(heads):
            gq_copy(h, r).wait_send()
            for p in range(planes):
                kv_copy(h, p, at.member_peer(r), member, r).wait_send()
    for part in sums:
        part.drain(part.back)
    w_sum.drain(w_back)
    for k in range(1, group):
        wide_copy(k, member).wait_send()
    core_copy(my_core).wait_send()
    for s in range(small_last):
        small_copy(s).wait_send()
    for k in range(1, planes):
        small_line(k).wait_send()
    for i in range(len(rest)):
        small_rest(i).wait_send()


EVENTS_BEFORE = ((0, 2),)
EVENT_STEPS = ({3: 2, 4: 6, 5: 10, 6: 13}, {1: 2, 2: 5, 3: 9, 4: 13})


def main(docs, blocks, group, att_in, cotangent, lengths, weights, attention, tok_doc, collective_id,
         k_block=256, q_tile=512):
    q = attention[0]
    heads, length_all, _ = q.shape
    _, rows, width = tok_doc.shape
    planes = blocks // group
    count = planes * rows
    cols = heads * HD
    inner_width = weights[4].shape[1]
    features = -(-3 * cols // 128) * 128
    unit = 32 * blocks
    second = -(-(inner_width + width) // unit)
    first = inner_width // 2
    split = second // 2 * unit
    cuts = [(0, first), (first, first), (inner_width, split), (inner_width + split, second * unit - split)]
    total = inner_width + second * unit
    members, rest = len(bits_of(group)), len(bits_of(docs)) - 1
    placed = sum(Summer.placed(size, 1 + members, planes, rest) for _, size in cuts)
    w_placed = Summer.placed(features, 1, planes, rest)
    stages = 2 + members + rest
    steps = 1 + members + planes + rest
    dma, vmem = pltpu.SemaphoreType.DMA, pltpu.VMEM
    return pl.pallas_call(
        functools.partial(main_kernel, docs, blocks, group, cuts, k_block, q_tile),
        out_shape=(
            jax.ShapeDtypeStruct((planes, rows, width), BF16),
            jax.ShapeDtypeStruct((planes, rows, width), BF16),
            jax.ShapeDtypeStruct((total, width), BF16),
            jax.ShapeDtypeStruct((features * group, width), BF16),
            jax.ShapeDtypeStruct((24, width), F32),
        ),
        in_specs=[VMEM] * 2 + [SMEM] + [VMEM] * 4 + [ANY, VMEM, ANY] + [VMEM] * 11,
        out_specs=(VMEM,) * 5,
        scratch_shapes=[
            vmem((count, width), BF16),
            vmem((width, count), BF16),
            vmem((count, width), F32),
            vmem((planes, rows, width), BF16),
            vmem((group, heads, planes, 2 * HD, rows), BF16),
            vmem((group, heads, planes, HD, rows), BF16),
            vmem((group, planes, rows, cols), BF16),
            vmem((planes, group, rows, cols), BF16),
            vmem((heads, length_all, LANES), BF16),
            vmem((heads, length_all, LANES), BF16),
            vmem((heads, HD, length_all), BF16),
            vmem((heads, HD, length_all), BF16),
            vmem((length_all, LANES), F32),
            vmem((heads, planes, group, 2 * HD, rows), BF16),
            vmem((heads, planes, group, HD, rows), BF16),
            vmem((total, width), F32),
            vmem((max(placed, 2 * inner_width), width), BF16),
            vmem((placed, width), BF16),
            vmem((features, width), F32),
            vmem((w_placed, width), BF16),
            vmem((w_placed, width), BF16),
            vmem((heads, 2, 8, HD), F32),
            vmem((steps, 24, width), F32),
            vmem((steps, 24, width), F32),
            dma((2, group)),
            dma((2, heads, planes, group)),
            dma((2, heads, group)),
            dma((len(cuts), 2, 2, stages, planes)),
            dma((2, 2, 2 + rest, planes)),
            dma((2, steps)),
            dma((2, group)),
            dma((2,)),
            dma((inner_width // width + 1,)),
            dma((2, planes)),
            dma((2, planes)),
        ],
        compiler_params=params(collective_id),
    )(att_in, cotangent, lengths, *weights, *attention, tok_doc)


def last_kernel(group, heads, out_in, grad_in, sum_ref, qkv_ref, small_ref,
                out_ref, grad_ref, qw_ref, qb_ref, kw_ref, vw_ref, vb_ref, ow_ref, ob_ref, g1_ref, s1_ref,
                uw_ref, ub_ref, dw_ref, db_ref, g2_ref, s2_ref, stack):
    width = ow_ref.shape[0]
    inner_width = uw_ref.shape[1]
    cols = width // group

    def widen(out, rows_out, cols_out, base):
        step = row_tile(rows_out)

        def run(i, carry):
            span = pl.ds(pl.multiple_of(i * step, step), step)
            out[span, cols_out] = sum_ref[pl.ds(pl.multiple_of(base + i * step, 16), step), :].astype(F32)
            return carry

        lax.fori_loop(0, rows_out // step, run, 0)

    widen(dw_ref, inner_width, slice(None), 0)
    for c in range(inner_width // width):
        widen(uw_ref, width, slice(c * width, (c + 1) * width), inner_width + c * width)
    widen(ow_ref, width, slice(None), 2 * inner_width)
    out_ref[...] = out_in[...].astype(F32)
    grad_ref[...] = grad_in[...].astype(F32)
    half = qkv_ref.shape[0] // group // 2
    unit = HD // 2
    for which, out in enumerate((qw_ref, kw_ref, vw_ref)):
        for g in range(group):
            for h in range(heads):
                first = heads * 2 * HD + h * HD if which == 0 else h * 2 * HD + (which - 1) * HD
                for u in range(2):
                    f = first + u * unit
                    at = f // half * half * group + g * half + f % half
                    to = g * cols + h * HD + u * unit
                    stack[to:to + unit, :] = qkv_ref[at:at + unit, :]
        out[...] = stack[...].T.astype(F32)

    def vector(out, i):
        out[...] = small_ref[i:i + 1, :].reshape(out.shape)

    for i, out in ((16, qb_ref), (17, vb_ref), (0, g2_ref), (1, s2_ref), (2, db_ref), (3, g1_ref), (4, s1_ref),
                   (5, ob_ref)):
        vector(out, i)
    parts = inner_width // width
    ub_ref[...] = jnp.concatenate([small_ref[6 + i:7 + i, :] for i in range(parts)], axis=1).reshape(ub_ref.shape)


def last(group, shape, inner_width, *arrays):
    width = shape[-1]
    heads = width // group // HD
    whole = jax.ShapeDtypeStruct(shape, F32)
    square = jax.ShapeDtypeStruct((width, width), F32)
    vector = jax.ShapeDtypeStruct((width,), F32)
    return pl.pallas_call(
        functools.partial(last_kernel, group, heads),
        out_shape=(
            whole, whole, square, vector, square, square, vector, square, vector,
            vector, vector, jax.ShapeDtypeStruct((width, inner_width), F32),
            jax.ShapeDtypeStruct((inner_width,), F32), jax.ShapeDtypeStruct((inner_width, width), F32),
            vector, vector, vector,
        ),
        in_specs=[VMEM] * len(arrays),
        out_specs=(VMEM,) * 17,
        scratch_shapes=[pltpu.VMEM((width, width), BF16)],
        compiler_params=params(),
    )(*arrays)


def device_program(docs, blocks, tokens, query_weight, query_bias, key_weight, value_weight, value_bias,
                   out_weight, out_bias, first_gain, first_shift, up_weight, up_bias, down_weight,
                   down_bias, second_gain, second_shift, cotangent, lengths):
    slots, rows, width = tokens.shape
    inner_width = up_weight.shape[1]
    group = blocks // slots
    cols = width // group
    projections = (query_weight, key_weight, value_weight)
    tok_doc, cot = gather_tokens(tokens, cotangent, blocks, 0)
    att, q, k, v, o = attention_forward(tok_doc.reshape(blocks * rows, width), projections,
                                        (query_bias, value_bias), lengths, group)
    att_in = exchange(att.reshape(slots, group, rows, cols), 1)
    parts = main(
        docs, blocks, group, att_in, cot, lengths,
        (out_weight, out_bias, first_gain, first_shift, up_weight, up_bias, down_weight, down_bias,
         second_gain, second_shift, *projections), (q, k, v, o), tok_doc, 2)
    return last(group, tokens.shape, inner_width, *parts)


def solution(mesh):
    split = P("docs", "blk", None)
    return jax.shard_map(
        functools.partial(device_program, mesh.shape["docs"], mesh.shape["blk"]),
        mesh=mesh,
        in_specs=(split,) + (P(),) * 15 + (split, P("docs")),
        out_specs=(split, split) + (P(),) * 15,
        check_vma=False,
    )
```

```python
import functools

import jax
import jax.numpy as jnp
from jax import lax
from jax.experimental import pallas as pl
from jax.experimental.pallas import tpu as pltpu
from jax.sharding import PartitionSpec as P

HD = 64
LANES = 128
EPS = 1e-05
MASKED = -1e30
F32 = jnp.float32
BF16 = jnp.bfloat16
VMEM = pl.BlockSpec(memory_space=pltpu.VMEM)
ANY = pl.BlockSpec(memory_space=pl.ANY)
SMEM = pl.BlockSpec(memory_space=pltpu.SMEM)
MESH = pl.DeviceIdType.MESH
VMEM_LIMIT = 63 * 1024 * 1024


def mm(left, right):
    return jnp.dot(left, right, preferred_element_type=F32)


def mm_nt(left, right):
    return lax.dot_general(left, right, (((1,), (1,)), ((), ())), preferred_element_type=F32)


def mm_tn(left, right):
    return lax.dot_general(left, right, (((0,), (0,)), ((), ())), preferred_element_type=F32)


def params(collective_id=None):
    if collective_id is None:
        return pltpu.CompilerParams(vmem_limit_bytes=VMEM_LIMIT)
    return pltpu.CompilerParams(
        vmem_limit_bytes=VMEM_LIMIT, collective_id=collective_id, has_side_effects=True
    )


def greet(peers):
    barrier = pltpu.get_barrier_semaphore()
    for peer in peers:
        pl.semaphore_signal(barrier, inc=1, device_id=peer, device_id_type=MESH)
    pl.semaphore_wait(barrier, len(peers))


def send_to(src, dst, send_sem, recv_sem, peer):
    return pltpu.make_async_remote_copy(
        src_ref=src, dst_ref=dst, send_sem=send_sem, recv_sem=recv_sem,
        device_id=peer, device_id_type=MESH,
    )


def row(ref):
    return ref[...].astype(F32).reshape(1, ref.shape[0])


def own_columns(ref, member, cols):
    if cols % LANES == 0:
        return ref[:, pl.ds(pl.multiple_of(member * cols, LANES), cols)]
    per = LANES // cols
    both = ref[:, pl.ds(pl.multiple_of(member // per * LANES, LANES), LANES)].astype(F32)
    return sum(jnp.where(lax.rem(member, per) == i, both[:, i * cols:(i + 1) * cols], 0.0)
               for i in range(per)).astype(BF16)


def own_entries(ref, member, cols):
    values = row(ref)
    return sum(jnp.where(member == i, values[:, i * cols:(i + 1) * cols], 0.0)
               for i in range(ref.shape[0] // cols))


def first_kernel(slots, group, q_block, tok_in, cot_in, wq_ref, wk_ref, wv_ref, qb_ref, vb_ref, len_ref,
                 tok_ref, cot_out, att_in, q_ref, k_ref, v_ref, o_ref,
                 low, cot_low, vt, w_ref, att, send_a, recv_a, send_b, recv_b, cot_sems, att_sems):
    me = lax.axis_index("blk")
    plane, member = me // group, lax.rem(me, group)
    blocks, rows, width = tok_ref.shape
    total = width // group
    heads = total // HD
    planes = [lax.rem(plane + k, slots) for k in range(1, slots)]
    members = [lax.rem(member + k, group) for k in range(1, group)]
    greet([{"blk": p * group + member} for p in planes]
          + [{"blk": plane * group + m} for m in members])

    low[...] = tok_in[...].astype(BF16)
    pending = []
    for k in range(1, slots):
        target = planes[k - 1]
        copy = send_to(low.at[target], tok_ref.at[me], send_a.at[k], recv_a.at[k],
                       {"blk": target * group + member})
        copy.start()
        pending.append(copy)
    tok_ref[me] = low[plane]

    def spread(k):
        block = lax.rem(plane + slots - k, slots) * group + member
        if k > 0:
            send_to(low.at[plane], tok_ref.at[block], send_a.at[k], recv_a.at[k],
                    {"blk": block}).wait_recv()
        for j in range(1, group):
            copy = send_to(tok_ref.at[block], tok_ref.at[block], send_b.at[k, j], recv_b.at[k, j],
                           {"blk": plane * group + members[j - 1]})
            copy.start()
            pending.append(copy)

    spread(0)
    cot_low[...] = cot_in[...].astype(BF16)
    for i, ref in enumerate((wq_ref, wk_ref, wv_ref)):
        w_ref[:, i * total:(i + 1) * total] = own_columns(ref, member, total)
    bias = jnp.concatenate(
        [own_entries(qb_ref, member, total), jnp.zeros((1, total), F32),
         own_entries(vb_ref, member, total)], axis=1)
    doc_len = len_ref[plane]
    chunk = group * rows

    def project(k):
        source = lax.rem(plane + slots - k, slots)
        for j in range(1, group):
            block = source * group + lax.rem(member + group - j, group)
            send_to(tok_ref.at[block], tok_ref.at[block], send_b.at[k, j], recv_b.at[k, j],
                    {"blk": plane * group + members[j - 1]}).wait_recv()
        span = pl.ds(pl.multiple_of(source * chunk, chunk), chunk)
        qkv = mm(tok_ref[pl.ds(source * group, group)].reshape(chunk, width), w_ref[...]) + bias
        lane = lax.broadcasted_iota(jnp.int32, (chunk, LANES), 1)
        position = source * chunk + lax.broadcasted_iota(jnp.int32, (chunk, LANES), 0)
        mask = jnp.where(position < doc_len, 0.0, MASKED)
        for h in range(heads):
            def part(which):
                cols = qkv[:, which * total + h * HD:which * total + (h + 1) * HD]
                return jnp.concatenate([cols, jnp.zeros_like(cols)], axis=1)
            q_ref[h, span, :] = jnp.where(
                lane == HD, 1.0, part(0).astype(BF16).astype(F32) * (HD ** -0.5)).astype(BF16)
            k_ref[h, span, :] = jnp.where(
                lane == HD, mask, jnp.where((lane > HD) & (lane < HD + 4), 1.0, part(1))).astype(BF16)
            v_rows = jnp.where((lane >= HD) & (lane < HD + 4), 1.0, part(2)).astype(BF16)
            v_ref[h, span, :] = v_rows
            vt[h, :, span] = v_rows.T

    for k in range(1, slots):
        spread(k)
        if k == slots - 1:
            for j in range(1, slots):
                target = planes[j - 1]
                copy = send_to(cot_low.at[target], cot_out.at[plane], cot_sems.at[0, j], cot_sems.at[1, j],
                               {"blk": target * group + member})
                copy.start()
                pending.append(copy)
            cot_out[plane] = cot_low[plane]
        project(k - 1)
    project(slots - 1)

    per_block = q_block // rows
    q_blocks = blocks // per_block

    def att_copy(p, g, slot, r):
        return send_to(att.at[p, g], att_in.at[slot, p], att_sems.at[0, p, r], att_sems.at[1, p, r],
                       {"blk": plane * group + g})

    def block(step, carry):
        which = lax.rem(step + member // per_block + 1, q_blocks)
        span = pl.ds(pl.multiple_of(which * q_block, q_block), q_block)
        done = []
        for h in range(heads):
            scores = mm_nt(k_ref[h], q_ref[h, span, :])
            top = jnp.max(scores, axis=0, keepdims=True)
            weights = jnp.exp(scores - top).astype(BF16)
            mixed = mm(vt[h], weights)
            denom = mixed[HD:HD + 1, :]
            scaled = mixed * (1.0 / denom)
            sub = lax.broadcasted_iota(jnp.int32, scaled.shape, 0)
            o_rows = jnp.where(sub == HD, top + jnp.log(denom), scaled).T
            o_ref[h, span, :] = o_rows
            done.append(o_rows[:, :HD].astype(BF16))
        attended = jnp.concatenate(done, axis=1)
        for u in range(per_block):
            d = which * per_block + u
            p, g = d // group, lax.rem(d, group)
            att[p, g] = attended[u * rows:(u + 1) * rows, :]

            @pl.when(g != member)
            def _():
                att_copy(p, g, member, lax.rem(g + group - member, group)).start()

            @pl.when(g == member)
            def _():
                att_in[member, p] = attended[u * rows:(u + 1) * rows, :]
        return carry

    lax.fori_loop(0, q_blocks, block, 0)
    for k in range(1, slots):
        source = lax.rem(plane + slots - k, slots)
        send_to(cot_low.at[plane], cot_out.at[source], cot_sems.at[0, k], cot_sems.at[1, k],
                {"blk": source * group + member}).wait_recv()
    for p in range(slots):
        for r in range(1, group):
            att_copy(p, member, lax.rem(member + group - r, group), r).wait_recv()
    for p in range(slots):
        for r in range(1, group):
            att_copy(p, members[r - 1], member, r).wait_send()
    for copy in pending:
        copy.wait_send()


def first(tokens, cotangent, weights, biases, lengths, blocks, collective_id, q_block=256):
    slots, rows, width = tokens.shape
    group = blocks // slots
    length_all, total = blocks * rows, width // group
    heads = total // HD
    per_head = jax.ShapeDtypeStruct((heads, length_all, LANES), BF16)
    dma, vmem = pltpu.SemaphoreType.DMA, pltpu.VMEM
    return pl.pallas_call(
        functools.partial(first_kernel, slots, group, q_block),
        out_shape=(
            jax.ShapeDtypeStruct((blocks, rows, width), BF16),
            jax.ShapeDtypeStruct((slots, rows, width), BF16),
            jax.ShapeDtypeStruct((group, slots, rows, total), BF16),
            per_head, per_head, per_head,
            jax.ShapeDtypeStruct((heads, length_all, LANES), F32),
        ),
        in_specs=[VMEM] * 7 + [SMEM],
        out_specs=(VMEM,) * 7,
        scratch_shapes=[
            vmem((slots, rows, width), BF16),
            vmem((slots, rows, width), BF16),
            vmem((heads, LANES, length_all), BF16),
            vmem((width, 3 * total), BF16),
            vmem((slots, group, rows, total), BF16),
            dma((slots,)), dma((slots,)), dma((slots, group)), dma((slots, group)), dma((2, slots)),
            dma((2, slots, group)),
        ],
        compiler_params=params(collective_id),
    )(tokens, cotangent, *weights, *biases, lengths)


def three(value):
    high = value.astype(BF16).astype(F32)
    mid = (value - high).astype(BF16).astype(F32)
    return high, mid, value - high - mid


def row_tile(rows):
    return next(t for t in (96, 64, 48, 32, 16) if rows % t == 0)


def over_rows(rows, body):
    step = row_tile(rows)

    def run(i, carry):
        body(i * step, step)
        return carry

    lax.fori_loop(0, rows // step, run, 0)


def rows_at(offset, i, step):
    return pl.ds(pl.multiple_of(offset + i, 16), step)


def rows_of(offset, n):
    return pl.ds(pl.multiple_of(offset, 16), n)


def bits_of(size):
    return [1 << i for i in range(size.bit_length() - 1)]


class Place:
    def __init__(self, docs, blocks, group):
        self.docs, self.blocks, self.group = docs, blocks, group
        self.planes = blocks // group
        self.me, self.doc = lax.axis_index("blk"), lax.axis_index("docs")
        self.plane, self.member = self.me // group, lax.rem(self.me, group)

    def pair(self, axis, bit):
        mine = self.me if axis == "blk" else self.doc
        on = lax.rem(mine // bit, 2)
        return {axis: mine + bit - 2 * bit * on}, on

    def member_peer(self, k):
        return lax.rem(self.member + k, self.group)

    def member_source(self, k):
        return lax.rem(self.member + self.group - k, self.group)

    def in_plane(self, member):
        return {"blk": self.plane * self.group + member}

    def in_line(self, plane):
        return {"blk": plane * self.group + self.member}

    def plane_peer(self, k):
        return lax.rem(self.plane + k, self.planes)

    def plane_source(self, k):
        return lax.rem(self.plane + self.planes - k, self.planes)


class Summer:
    def __init__(self, at, acc, sent, came, out, place, offset, rows, pairs, rest, sems, out_shift=0):
        self.at, self.acc, self.sent, self.came, self.out, self.sems = at, acc, sent, came, out, sems
        self.shift = out_shift
        self.stages = []
        for axis, bit in pairs:
            to, on = at.pair(axis, bit)
            n = rows // 2
            self.stages.append(("pair", to, n, offset + (1 - on) * n, offset + on * n, place))
            offset, rows, place = offset + on * n, n, place + n
        n = rows // at.planes
        self.stages.append(("planes", None, n, offset, offset + at.plane * n, place))
        offset, rows, place = offset + at.plane * n, n, place + (at.planes - 1) * n
        for axis, bit in rest:
            self.stages.append(("full", at.pair(axis, bit)[0], rows, offset, offset, place))
            place += rows
        self.count = len(self.stages)
        self.back = [s for s in range(self.count) if self.stages[s][0] != "full"][::-1]

    @staticmethod
    def placed(rows, pairs, planes, rest):
        total = 0
        for _ in range(pairs):
            rows //= 2
            total += rows
        rows //= planes
        return total + (planes - 1 + rest) * rows

    def copies(self, s, back=False, receive=False):
        kind, to, n, give, keep, place = self.stages[s]
        at, out = self.at, self.out
        w = 1 if back else 0
        if kind == "planes":
            found = []
            for k in range(1, at.planes):
                if back:
                    which = at.plane_source(k) if receive else at.plane
                    span = rows_of(give + which * n + self.shift, n)
                    src, dst = out.at[span], out.at[span]
                else:
                    src, dst = (ref.at[rows_of(place + (k - 1) * n, n)] for ref in (self.sent, self.came))
                to = at.in_line(at.plane_peer(k))
                found.append(send_to(src, dst, self.sems.at[w, 0, s, k], self.sems.at[w, 1, s, k], to))
            return found
        if back:
            span = rows_of((give if receive else keep) + self.shift, n)
            src, dst = out.at[span], out.at[span]
        else:
            src, dst = self.sent.at[rows_of(place, n)], self.came.at[rows_of(place, n)]
        return [send_to(src, dst, self.sems.at[w, 0, s, 0], self.sems.at[w, 1, s, 0], to)]

    def pack(self, give, place, n):
        def run(i, step):
            self.sent[rows_at(place, i, step), :] = self.acc[rows_at(give, i, step), :].astype(BF16)
        over_rows(n, run)

    def start(self, s):
        kind, to, n, give, keep, place = self.stages[s]
        if kind == "planes":
            for k in range(1, self.at.planes):
                self.pack(give + self.at.plane_peer(k) * n, place + (k - 1) * n, n)
        else:
            self.pack(give, place, n)
        for copy in self.copies(s):
            copy.start()

    def finish(self, s):
        kind, to, n, give, keep, place = self.stages[s]
        for copy in self.copies(s):
            copy.wait_recv()
        parts = self.at.planes - 1 if kind == "planes" else 1
        last = s == self.count - 1

        def run(i, step):
            total = self.acc[rows_at(keep, i, step), :]
            if kind == "full":
                total = total.astype(BF16).astype(F32)
            for k in range(parts):
                total = total + self.came[rows_at(place + k * n, i, step), :].astype(F32)
            if last:
                self.out[rows_at(keep + self.shift, i, step), :] = total.astype(BF16)
            else:
                self.acc[rows_at(keep, i, step), :] = total
        over_rows(n, run)

    def start_back(self, s):
        for copy in self.copies(s, back=True):
            copy.start()

    def finish_back(self, s):
        for copy in self.copies(s, back=True, receive=True):
            copy.wait_recv()

    def events(self, back):
        def first():
            self.start(0)

        def inward(s):
            self.finish(s)
            if s + 1 < self.count:
                self.start(s + 1)
            elif back:
                self.start_back(back[0])

        def outward(d):
            self.finish_back(back[d])
            if d + 1 < len(back):
                self.start_back(back[d + 1])

        return ([first] + [functools.partial(inward, s) for s in range(self.count)]
                + [functools.partial(outward, d) for d in range(len(back))])

    def drain(self, back):
        for s in range(self.count):
            for copy in self.copies(s):
                copy.wait_send()
        for s in back:
            for copy in self.copies(s, back=True):
                copy.wait_send()


def row_mean(value):
    return jnp.mean(value, axis=1, keepdims=True)


def col_sum(value):
    return jnp.sum(value, axis=0, keepdims=True)


def main_kernel(docs, blocks, group, cuts, k_block, q_tile,
                att_in, cot_ref, len_ref, wo_ref, ob_ref, g1_ref, s1_ref, up_hbm, ub_ref, down_hbm,
                db_ref, g2_ref, s2_ref, wq_ref, wk_ref, wv_ref, q_ref, k_ref, v_ref, o_ref, tok_ref,
                out_in, grad_in, sum_ref, qkv_ref, small_out,
                att, hid_t, gz, away, kv_in, gq_in, g_att, g_in, qx, gx, qt, gt, gq_acc, kv_send, gq_send,
                acc, sent, came, dwt, sent_w, came_w, bias, small_sent, small_came,
                g_sems, kv_sems, gq_sems, sum_sems, w_sems, small_sems, wide_sems, core_sems, load_sems,
                out_sems, grad_sems):
    at = Place(docs, blocks, group)
    me, member, plane, planes = at.me, at.member, at.plane, at.planes
    _, rows, width = tok_ref.shape
    count = planes * rows
    cols = width // group
    inner_width = up_hbm.shape[1]
    heads, length_all, _ = q_ref.shape
    parts = inner_width // width
    doc_bits, member_bits = bits_of(docs), bits_of(group)

    loads = [pltpu.make_async_copy(up_hbm.at[:, c * width:(c + 1) * width],
                                   sent.at[inner_width + c * width:inner_width + (c + 1) * width], load_sems.at[c])
             for c in range(parts)]
    loads.append(pltpu.make_async_copy(down_hbm, sent.at[:inner_width], load_sems.at[parts]))
    for load in loads:
        load.start()

    def up_part(c):
        return sent[inner_width + c * width:inner_width + (c + 1) * width, :]

    greet([at.in_plane(at.member_peer(k)) for k in range(1, group)]
          + [at.in_line(at.plane_peer(k)) for k in range(1, planes)]
          + [at.pair("docs", bit)[0] for bit in doc_bits])

    rest = [("docs", bit) for bit in doc_bits[1:]]
    sums, place = [], 0
    for c, (offset, size) in enumerate(cuts):
        turn = c % len(member_bits)
        pairs = [("docs", 1)] + [("blk", bit) for bit in member_bits[turn:] + member_bits[:turn]]
        sums.append(Summer(at, acc, sent, came, sum_ref, place, offset, size, pairs, rest, sum_sems.at[c]))
        place = place + Summer.placed(size, len(pairs), planes, len(rest))
    chains = [s.events(s.back) for s in sums]
    groups = [[c for c in range(len(cuts)) if cuts[c][0] < inner_width],
              [c for c in range(len(cuts)) if cuts[c][0] >= inner_width]]

    def advance(which, step):
        for c in groups[which]:
            chains[c][step]()

    flat = jnp.concatenate([tok_ref[p * group + member].astype(F32) for p in range(planes)], axis=0)
    for p in range(planes):
        for g in range(group):
            att[p * rows:(p + 1) * rows, g * cols:(g + 1) * cols] = att_in[g, p]
    up_bias = row(ub_ref)
    gain1, gain2 = row(g1_ref), row(g2_ref)
    summed = flat + mm(att[...], wo_ref[...]) + row(ob_ref)
    centred = summed - row_mean(summed)
    rstd1 = lax.rsqrt(row_mean(centred * centred) + EPS)
    xhat1 = centred * rstd1
    hidden = xhat1 * gain1 + row(s1_ref)
    hidden_low = hidden.astype(BF16)
    hid_t[...] = hidden_low.T
    for load in loads:
        load.wait()
    ffn = jnp.zeros((count, width), F32)
    for c in range(parts):
        span = slice(c * width, (c + 1) * width)
        inner = mm(hidden_low, up_part(c)) + up_bias[:, span]
        square = inner * inner
        slope_in = 0.7978845608 * (1.0 + (3 * 0.044715) * square)
        tanh = jnp.tanh(inner * (0.7978845608 * (1.0 + 0.044715 * square)))
        half = 0.5 * (1.0 + tanh)
        acc[c * count:(c + 1) * count, :] = half + (0.5 * inner) * ((1.0 - tanh * tanh) * slope_in)
        low = (inner * half).astype(BF16)
        sum_ref[c * count:(c + 1) * count, :] = low
        ffn = ffn + mm(low, sent[span, :])
    summed = flat + hidden + ffn + row(db_ref)
    centred = summed - row_mean(summed)
    rstd2 = lax.rsqrt(row_mean(centred * centred) + EPS)
    xhat2 = centred * rstd2
    away[...] = (xhat2 * gain2 + row(s2_ref)).astype(BF16).reshape(planes, rows, width)

    def line_copies(dst, sems, receive=False):
        return [send_to(away.at[at.plane_peer(k)], dst.at[at.plane_source(k) if receive else plane],
                        sems.at[0, k], sems.at[1, k], at.in_line(at.plane_peer(k))) for k in range(1, planes)]

    for copy in line_copies(out_in, out_sems):
        copy.start()
    out_in[plane] = away[plane]
    lane_r = lax.broadcasted_iota(jnp.int32, (rows, width), 0)
    g_out = jnp.concatenate(
        [jnp.where((p * group + member) * rows + lane_r < len_ref[plane], cot_ref[p].astype(F32), 0.0)
         for p in range(planes)], axis=0)
    small_sent[0] = jnp.zeros(small_sent.shape[1:], F32)
    small_sent[0, 0:1, :] = col_sum(g_out * xhat2)
    small_sent[0, 1:2, :] = col_sum(g_out)
    scaled = g_out * gain2
    g_z2 = rstd2 * (scaled - row_mean(scaled) - xhat2 * row_mean(scaled * xhat2))
    g_ffn = g_z2.astype(BF16)
    small_sent[0, 2:3, :] = col_sum(g_ffn.astype(F32))
    g_hidden = g_z2
    for c in range(parts):
        span = slice(c * width, (c + 1) * width)
        g_inner = (mm_nt(g_ffn, sent[span, :]) * acc[c * count:(c + 1) * count, :]).astype(BF16)
        sum_ref[inner_width + c * count:inner_width + (c + 1) * count, :] = g_inner
        g_hidden = g_hidden + mm_nt(g_inner, up_part(c))
    scaled = g_hidden * gain1
    g_z1 = rstd1 * (scaled - row_mean(scaled) - xhat1 * row_mean(scaled * xhat1))
    g_branch = g_z1.astype(BF16)
    gz[...] = g_z1 + g_z2
    g_low = mm_nt(g_branch, wo_ref[...]).astype(BF16)
    for p in range(planes):
        for g in range(group):
            g_att[g, p] = g_low[p * rows:(p + 1) * rows, g * cols:(g + 1) * cols]

    def g_copy(k, receive=False):
        slot = at.member_source(k) if receive else member
        return send_to(g_att.at[at.member_peer(k)], g_in.at[:, slot], g_sems.at[0, k], g_sems.at[1, k],
                       at.in_plane(at.member_peer(k)))

    for k in range(1, group):
        g_copy(k).start()
    for p in range(planes):
        g_in[p, member] = g_att[member, p]

    for c in range(parts):
        span = slice(c * width, (c + 1) * width)
        acc[span, :] = mm_tn(sum_ref[c * count:(c + 1) * count, :], g_ffn)
    advance(0, 0)
    for c in range(parts):
        g_inner = sum_ref[inner_width + c * count:inner_width + (c + 1) * count, :]
        small_sent[0, 6 + c:7 + c, :] = col_sum(g_inner.astype(F32))
        acc[inner_width + c * width:inner_width + (c + 1) * width, :] = mm(hid_t[...], g_inner)
    acc[2 * inner_width:2 * inner_width + width, :] = mm_tn(att[...], g_branch)
    if acc.shape[0] > 2 * inner_width + width:
        acc[2 * inner_width + width:, :] = jnp.zeros((acc.shape[0] - 2 * inner_width - width, width), F32)
    advance(0, 1)
    advance(1, 0)
    small_sent[0, 3:4, :] = col_sum(g_hidden * xhat1)
    small_sent[0, 4:5, :] = col_sum(g_hidden)
    small_sent[0, 5:6, :] = col_sum(g_branch.astype(F32))
    chunk = group * rows
    lane = lax.broadcasted_iota(jnp.int32, (chunk, LANES), 1)

    def prepare_q(step, carry):
        span = pl.ds(pl.multiple_of(step * chunk, chunk), chunk)
        for h in range(heads):
            q_rows = q_ref[h, span, :].astype(F32)
            ext = q_rows
            for i, value in enumerate(three(-o_ref[h, span, HD:HD + 1])):
                ext = jnp.where(lane == HD + 1 + i, value, ext)
            qx[h, span, :] = ext.astype(BF16)
            qt[h, :, span] = q_rows[:, :HD].T.astype(BF16)
        return carry

    lax.fori_loop(0, planes, prepare_q, 0)
    for k in range(1, group):
        g_copy(k, True).wait_recv()

    def prepare_g(step, carry):
        span = pl.ds(pl.multiple_of(step * chunk, chunk), chunk)
        g_block = g_in[step].reshape(chunk, cols)
        for h in range(heads):
            g_rows = g_block[:, h * HD:(h + 1) * HD].astype(F32)
            g_rows = jnp.concatenate([g_rows, jnp.zeros_like(g_rows)], axis=1)
            delta = jnp.sum(g_rows * o_ref[h, span, :], axis=1, keepdims=True)
            ext = g_rows
            for i, value in enumerate(three(-delta)):
                ext = jnp.where(lane == HD + i, value, ext)
            gx[h, span, :] = ext.astype(BF16)
            gt[h, :, span] = g_rows[:, :HD].T.astype(BF16)
        return carry

    lax.fori_loop(0, planes, prepare_g, 0)
    for which, number in EVENTS_BEFORE:
        advance(which, number)

    k_blocks = length_all // k_block
    per_block = k_block // rows
    ones = jnp.ones((8, k_block), BF16)
    dwt[...] = jnp.zeros_like(dwt)
    bias[...] = jnp.zeros_like(bias)

    def kv_copy(h, p, g, slot, r):
        return send_to(kv_send.at[h, p, g], kv_in.at[slot, h, p], kv_sems.at[0, h, p, r], kv_sems.at[1, h, p, r],
                       at.in_plane(g))

    def gq_copy(h, r, receive=False):
        slot = at.member_source(r) if receive else member
        return send_to(gq_send.at[h, :, at.member_peer(r)], gq_in.at[slot, h], gq_sems.at[0, h, r],
                       gq_sems.at[1, h, r], at.in_plane(at.member_peer(r)))

    total_steps = heads * k_blocks
    timed = [(which, step, t) for which, table in enumerate(EVENT_STEPS) for step, t in table.items()
             if t < total_steps]
    done = [max([1 - which] + [n for w, n in EVENTS_BEFORE if w == which] + [n for w, n, _ in timed if w == which]) + 1
            for which in range(2)]

    def block(step, carry):
        h, i = step // k_blocks, lax.rem(step, k_blocks)
        which = lax.rem(i + member // per_block + 1, k_blocks)
        span = pl.ds(pl.multiple_of(which * k_block, k_block), k_block)
        k_rows, v_rows = k_ref[h, span, :], v_ref[h, span, :]

        @pl.when(i == 0)
        def _():
            gq_acc[...] = jnp.zeros_like(gq_acc)

        gk = jnp.zeros((HD, k_block), F32)
        gv = jnp.zeros((HD, k_block), F32)
        for t in range(length_all // q_tile):
            tile = slice(t * q_tile, (t + 1) * q_tile)
            weights = jnp.exp(mm_nt(qx[h, tile, :], k_rows))
            centred = mm_nt(gx[h, tile, :], v_rows)
            g_scores = (weights * centred).astype(BF16)
            gv = gv + mm(gt[h, :, tile], weights.astype(BF16))
            gk = gk + mm(qt[h, :, tile], g_scores)
            gq_acc[tile, :] += mm(g_scores, k_rows)
        kv = jnp.concatenate([gk, gv], axis=0).astype(BF16)
        tok_rows = tok_ref[pl.ds(which * per_block, per_block)].reshape(k_block, width)
        dwt[pl.ds(pl.multiple_of(h * 2 * HD, 2 * HD), 2 * HD), :] += mm(kv, tok_rows)
        bias[h, 0] += mm_nt(ones, kv[HD:])
        for u in range(per_block):
            d = which * per_block + u
            p, g = d // group, lax.rem(d, group)
            kv_send[h, p, g] = kv[:, u * rows:(u + 1) * rows]

            @pl.when(g != member)
            def _():
                kv_copy(h, p, g, member, lax.rem(g + group - member, group)).start()

            @pl.when(g == member)
            def _():
                kv_in[member, h, p] = kv[:, u * rows:(u + 1) * rows]

        @pl.when(i == k_blocks - 1)
        def _():
            for n in range(blocks):
                gq_send[h, n // group, n % group] = (
                    gq_acc[n * rows:(n + 1) * rows, :HD] * (HD ** -0.5)).T.astype(BF16)
            for r in range(1, group):
                gq_copy(h, r).start()
            for p in range(planes):
                gq_in[member, h, p] = gq_send[h, p, member]

        for which_group, number, t in timed:
            pl.when(step == t)(functools.partial(advance, which_group, number))
        return carry

    lax.fori_loop(0, total_steps, block, 0)

    q_base = heads * 2 * HD
    for h in range(heads):
        part = jnp.zeros((HD, width), F32)
        q_bias = jnp.zeros((8, HD), F32)
        for n in range(blocks):
            low = gq_send[h, n // group, n % group]
            part = part + mm(low, tok_ref[n])
            q_bias = q_bias + mm_nt(jnp.ones((8, rows), BF16), low)
        dwt[q_base + h * HD:q_base + (h + 1) * HD, :] = part
        bias[h, 1] = q_bias
    half = dwt.shape[0] // 2
    my_core = lax.rem(at.doc, 2)
    w_sum = Summer(at, dwt, sent_w, came_w, qkv_ref, 0, 0, 2 * half, [("docs", 1)], rest, w_sems,
                   out_shift=my_core * (half * group - half) + member * half)
    w_back = [s for s in w_sum.back if w_sum.stages[s][0] == "planes"]
    w_chain = w_sum.events(w_back)
    w_chain[0]()
    lane_w = lax.broadcasted_iota(jnp.int32, (8, width), 1)
    sub = lax.broadcasted_iota(jnp.int32, (8, width), 0)
    wide = [jnp.concatenate([bias[h, i] for h in range(heads)] * group, axis=1) for i in range(2)]
    small_sent[0, 16:24, :] = jnp.where(
        (lane_w // cols) == member, jnp.where(sub == 0, wide[1], jnp.where(sub == 1, wide[0], 0.0)), 0.0)
    small_order = [("docs", 1)] + [("blk", bit) for bit in member_bits]

    def small_copy(s):
        return send_to(small_sent.at[s], small_came.at[s], small_sems.at[0, s], small_sems.at[1, s],
                       at.pair(*small_order[s])[0])

    small_last = len(small_order)

    def small_line(k, receive=False):
        slot = small_last + k
        return send_to(small_sent.at[small_last], small_came.at[slot], small_sems.at[0, slot],
                       small_sems.at[1, slot], at.in_line(at.plane_peer(k)))

    def small_rest(i):
        slot = small_last + planes + i
        return send_to(small_sent.at[small_last + 1 + i], small_came.at[slot], small_sems.at[0, slot],
                       small_sems.at[1, slot], at.pair(*rest[i])[0])

    def small_step(s):
        small_copy(s).wait_recv()
        small_sent[s + 1] = small_sent[s] + small_came[s]
        if s + 1 < small_last:
            small_copy(s + 1).start()
        else:
            for k in range(1, planes):
                small_line(k).start()

    def small_end():
        for k in range(1, planes):
            small_line(k).wait_recv()
        total = jnp.zeros(small_sent.shape[1:], F32)
        for p in range(planes):
            value = small_sent[small_last]
            for k in range(1, planes):
                value = jnp.where(at.plane_source(k) == p, small_came[small_last + k], value)
            total = total + value
        for i in range(len(rest)):
            small_sent[small_last + 1 + i] = total
            small_rest(i).start()
            small_rest(i).wait_recv()
            total = total + small_came[small_last + planes + i]
        small_out[...] = total

    small_copy(0).start()

    def slab(m):
        return rows_of(my_core * half * group + m * half, half)

    def wide_copy(k, m):
        return send_to(qkv_ref.at[slab(m)], qkv_ref.at[slab(m)], wide_sems.at[0, k], wide_sems.at[1, k],
                       at.in_plane(at.member_peer(k)))

    def core_copy(core):
        span = rows_of(core * half * group, half * group)
        return send_to(qkv_ref.at[span], qkv_ref.at[span], core_sems.at[0], core_sems.at[1],
                       at.pair("docs", 1)[0])

    def wide_start():
        for k in range(1, group):
            wide_copy(k, member).start()

    def wide_wait():
        for k in range(1, group):
            wide_copy(k, at.member_source(k)).wait_recv()
        core_copy(my_core).start()

    def gather_part(which):
        for p in range(planes):
            for g in range(group):
                for h in range(heads):
                    low = gq_in[g, h, p] if which == 0 else kv_in[g, h, p, (which - 1) * HD:which * HD, :]
                    hid_t[g * cols + h * HD:g * cols + (h + 1) * HD, p * rows:(p + 1) * rows] = low
        return hid_t[...].T

    def key_value_rows():
        for h in range(heads):
            for p in range(planes):
                for r in range(1, group):
                    kv_copy(h, p, member, at.member_source(r), r).wait_recv()
        gz[...] += mm_nt(gather_part(1), wk_ref[...])
        gz[...] += mm_nt(gather_part(2), wv_ref[...])

    def query_rows():
        for h in range(heads):
            for r in range(1, group):
                gq_copy(h, r, True).wait_recv()
        total = gz[...] + mm_nt(gather_part(0), wq_ref[...])
        for copy in line_copies(out_in, out_sems, True):
            copy.wait_recv()
        for copy in line_copies(out_in, out_sems):
            copy.wait_send()
        away[...] = total.astype(BF16).reshape(planes, rows, width)
        for copy in line_copies(grad_in, grad_sems):
            copy.start()
        grad_in[plane] = away[plane]

    w_events = w_chain[1:] + [wide_start, wide_wait]
    left = [[functools.partial(advance, which, step) for step in range(done[which], len(chains[groups[which][0]]))]
            for which in range(2)]
    small_events = [functools.partial(small_step, s) for s in range(small_last)] + [small_end]
    lanes_of_work = [w_events, [key_value_rows, query_rows], left[0], left[1], small_events]
    for e in range(max(len(work) for work in lanes_of_work)):
        for work in lanes_of_work:
            if e < len(work):
                work[e]()
    core_copy(1 - my_core).wait_recv()
    for copy in line_copies(grad_in, grad_sems, True):
        copy.wait_recv()
    for copy in line_copies(grad_in, grad_sems):
        copy.wait_send()
    for r in range(1, group):
        g_copy(r).wait_send()
        for h in range(heads):
            gq_copy(h, r).wait_send()
            for p in range(planes):
                kv_copy(h, p, at.member_peer(r), member, r).wait_send()
    for part in sums:
        part.drain(part.back)
    w_sum.drain(w_back)
    for k in range(1, group):
        wide_copy(k, member).wait_send()
    core_copy(my_core).wait_send()
    for s in range(small_last):
        small_copy(s).wait_send()
    for k in range(1, planes):
        small_line(k).wait_send()
    for i in range(len(rest)):
        small_rest(i).wait_send()


EVENTS_BEFORE = ((0, 2),)
EVENT_STEPS = ({3: 2, 4: 6, 5: 10, 6: 13}, {1: 2, 2: 5, 3: 9, 4: 13})


def main(docs, blocks, group, att_in, cotangent, lengths, weights, attention, tok_doc, collective_id,
         k_block=256, q_tile=512):
    q = attention[0]
    heads, length_all, _ = q.shape
    _, rows, width = tok_doc.shape
    planes = blocks // group
    count = planes * rows
    cols = heads * HD
    inner_width = weights[4].shape[1]
    features = -(-3 * cols // 128) * 128
    unit = 32 * blocks
    second = -(-(inner_width + width) // unit)
    first = inner_width // 2
    split = second // 2 * unit
    cuts = [(0, first), (first, first), (inner_width, split), (inner_width + split, second * unit - split)]
    total = inner_width + second * unit
    members, rest = len(bits_of(group)), len(bits_of(docs)) - 1
    placed = sum(Summer.placed(size, 1 + members, planes, rest) for _, size in cuts)
    w_placed = Summer.placed(features, 1, planes, rest)
    stages = 2 + members + rest
    steps = 1 + members + planes + rest
    dma, vmem = pltpu.SemaphoreType.DMA, pltpu.VMEM
    return pl.pallas_call(
        functools.partial(main_kernel, docs, blocks, group, cuts, k_block, q_tile),
        out_shape=(
            jax.ShapeDtypeStruct((planes, rows, width), BF16),
            jax.ShapeDtypeStruct((planes, rows, width), BF16),
            jax.ShapeDtypeStruct((total, width), BF16),
            jax.ShapeDtypeStruct((features * group, width), BF16),
            jax.ShapeDtypeStruct((24, width), F32),
        ),
        in_specs=[VMEM] * 2 + [SMEM] + [VMEM] * 4 + [ANY, VMEM, ANY] + [VMEM] * 11,
        out_specs=(VMEM,) * 5,
        scratch_shapes=[
            vmem((count, width), BF16),
            vmem((width, count), BF16),
            vmem((count, width), F32),
            vmem((planes, rows, width), BF16),
            vmem((group, heads, planes, 2 * HD, rows), BF16),
            vmem((group, heads, planes, HD, rows), BF16),
            vmem((group, planes, rows, cols), BF16),
            vmem((planes, group, rows, cols), BF16),
            vmem((heads, length_all, LANES), BF16),
            vmem((heads, length_all, LANES), BF16),
            vmem((heads, HD, length_all), BF16),
            vmem((heads, HD, length_all), BF16),
            vmem((length_all, LANES), F32),
            vmem((heads, planes, group, 2 * HD, rows), BF16),
            vmem((heads, planes, group, HD, rows), BF16),
            vmem((total, width), F32),
            vmem((max(placed, 2 * inner_width), width), BF16),
            vmem((placed, width), BF16),
            vmem((features, width), F32),
            vmem((w_placed, width), BF16),
            vmem((w_placed, width), BF16),
            vmem((heads, 2, 8, HD), F32),
            vmem((steps, 24, width), F32),
            vmem((steps, 24, width), F32),
            dma((2, group)),
            dma((2, heads, planes, group)),
            dma((2, heads, group)),
            dma((len(cuts), 2, 2, stages, planes)),
            dma((2, 2, 2 + rest, planes)),
            dma((2, steps)),
            dma((2, group)),
            dma((2,)),
            dma((inner_width // width + 1,)),
            dma((2, planes)),
            dma((2, planes)),
        ],
        compiler_params=params(collective_id),
    )(att_in, cotangent, lengths, *weights, *attention, tok_doc)


def last_kernel(group, heads, out_in, grad_in, sum_ref, qkv_ref, small_ref,
                out_ref, grad_ref, qw_ref, qb_ref, kw_ref, vw_ref, vb_ref, ow_ref, ob_ref, g1_ref, s1_ref,
                uw_ref, ub_ref, dw_ref, db_ref, g2_ref, s2_ref, stack):
    width = ow_ref.shape[0]
    inner_width = uw_ref.shape[1]
    cols = width // group

    def widen(out, rows_out, cols_out, base):
        step = row_tile(rows_out)

        def run(i, carry):
            span = pl.ds(pl.multiple_of(i * step, step), step)
            out[span, cols_out] = sum_ref[pl.ds(pl.multiple_of(base + i * step, 16), step), :].astype(F32)
            return carry

        lax.fori_loop(0, rows_out // step, run, 0)

    widen(dw_ref, inner_width, slice(None), 0)
    for c in range(inner_width // width):
        widen(uw_ref, width, slice(c * width, (c + 1) * width), inner_width + c * width)
    widen(ow_ref, width, slice(None), 2 * inner_width)
    out_ref[...] = out_in[...].astype(F32)
    grad_ref[...] = grad_in[...].astype(F32)
    half = qkv_ref.shape[0] // group // 2
    unit = HD // 2
    for which, out in enumerate((qw_ref, kw_ref, vw_ref)):
        for g in range(group):
            for h in range(heads):
                first = heads * 2 * HD + h * HD if which == 0 else h * 2 * HD + (which - 1) * HD
                for u in range(2):
                    f = first + u * unit
                    at = f // half * half * group + g * half + f % half
                    to = g * cols + h * HD + u * unit
                    stack[to:to + unit, :] = qkv_ref[at:at + unit, :]
        out[...] = stack[...].T.astype(F32)

    def vector(out, i):
        out[...] = small_ref[i:i + 1, :].reshape(out.shape)

    for i, out in ((16, qb_ref), (17, vb_ref), (0, g2_ref), (1, s2_ref), (2, db_ref), (3, g1_ref), (4, s1_ref),
                   (5, ob_ref)):
        vector(out, i)
    parts = inner_width // width
    ub_ref[...] = jnp.concatenate([small_ref[6 + i:7 + i, :] for i in range(parts)], axis=1).reshape(ub_ref.shape)


def last(group, shape, inner_width, *arrays):
    width = shape[-1]
    heads = width // group // HD
    whole = jax.ShapeDtypeStruct(shape, F32)
    square = jax.ShapeDtypeStruct((width, width), F32)
    vector = jax.ShapeDtypeStruct((width,), F32)
    return pl.pallas_call(
        functools.partial(last_kernel, group, heads),
        out_shape=(
            whole, whole, square, vector, square, square, vector, square, vector,
            vector, vector, jax.ShapeDtypeStruct((width, inner_width), F32),
            jax.ShapeDtypeStruct((inner_width,), F32), jax.ShapeDtypeStruct((inner_width, width), F32),
            vector, vector, vector,
        ),
        in_specs=[VMEM] * len(arrays),
        out_specs=(VMEM,) * 17,
        scratch_shapes=[pltpu.VMEM((width, width), BF16)],
        compiler_params=params(),
    )(*arrays)


def device_program(docs, blocks, tokens, query_weight, query_bias, key_weight, value_weight, value_bias,
                   out_weight, out_bias, first_gain, first_shift, up_weight, up_bias, down_weight,
                   down_bias, second_gain, second_shift, cotangent, lengths):
    slots, rows, width = tokens.shape
    inner_width = up_weight.shape[1]
    group = blocks // slots
    projections = (query_weight, key_weight, value_weight)
    tok_doc, cot, att_in, q, k, v, o = first(tokens, cotangent, projections, (query_bias, value_bias), lengths,
                                             blocks, 0)
    parts = main(
        docs, blocks, group, att_in, cot, lengths,
        (out_weight, out_bias, first_gain, first_shift, up_weight, up_bias, down_weight, down_bias,
         second_gain, second_shift, *projections), (q, k, v, o), tok_doc, 1)
    return last(group, tokens.shape, inner_width, *parts)


def solution(mesh):
    split = P("docs", "blk", None)
    return jax.shard_map(
        functools.partial(device_program, mesh.shape["docs"], mesh.shape["blk"]),
        mesh=mesh,
        in_specs=(split,) + (P(),) * 15 + (split, P("docs")),
        out_specs=(split, split) + (P(),) * 15,
        check_vma=False,
    )
```

```python
import functools

import jax
import jax.numpy as jnp
from jax import lax
from jax.experimental import pallas as pl
from jax.experimental.pallas import tpu as pltpu
from jax.sharding import PartitionSpec as P

HD = 64
LANES = 128
EPS = 1e-05
MASKED = -1e30
F32 = jnp.float32
BF16 = jnp.bfloat16
VMEM = pl.BlockSpec(memory_space=pltpu.VMEM)
ANY = pl.BlockSpec(memory_space=pl.ANY)
SMEM = pl.BlockSpec(memory_space=pltpu.SMEM)
MESH = pl.DeviceIdType.MESH
VMEM_LIMIT = 63 * 1024 * 1024


def mm(left, right):
    return jnp.dot(left, right, preferred_element_type=F32)


def mm_nt(left, right):
    return lax.dot_general(left, right, (((1,), (1,)), ((), ())), preferred_element_type=F32)


def mm_tn(left, right):
    return lax.dot_general(left, right, (((0,), (0,)), ((), ())), preferred_element_type=F32)


def params(collective_id=None):
    if collective_id is None:
        return pltpu.CompilerParams(vmem_limit_bytes=VMEM_LIMIT)
    return pltpu.CompilerParams(
        vmem_limit_bytes=VMEM_LIMIT, collective_id=collective_id, has_side_effects=True
    )


def greet(peers):
    barrier = pltpu.get_barrier_semaphore()
    for peer in peers:
        pl.semaphore_signal(barrier, inc=1, device_id=peer, device_id_type=MESH)
    pl.semaphore_wait(barrier, len(peers))


def send_to(src, dst, send_sem, recv_sem, peer):
    return pltpu.make_async_remote_copy(
        src_ref=src, dst_ref=dst, send_sem=send_sem, recv_sem=recv_sem,
        device_id=peer, device_id_type=MESH,
    )


def row(ref):
    return ref[...].astype(F32).reshape(1, ref.shape[0])


def own_columns(ref, member, cols):
    if cols % LANES == 0:
        return ref[:, pl.ds(pl.multiple_of(member * cols, LANES), cols)]
    per = LANES // cols
    both = ref[:, pl.ds(pl.multiple_of(member // per * LANES, LANES), LANES)].astype(F32)
    return sum(jnp.where(lax.rem(member, per) == i, both[:, i * cols:(i + 1) * cols], 0.0)
               for i in range(per)).astype(BF16)


def own_entries(ref, member, cols):
    values = row(ref)
    return sum(jnp.where(member == i, values[:, i * cols:(i + 1) * cols], 0.0)
               for i in range(ref.shape[0] // cols))


def first_kernel(slots, group, q_block, key_tile, tok_in, cot_in, wq_ref, wk_ref, wv_ref, qb_ref, vb_ref, len_ref,
                 tok_ref, cot_out, att_in, q_ref, k_ref, v_ref, o_ref,
                 low, cot_low, vt, w_ref, att, scores, send_a, recv_a, send_b, recv_b, cot_sems, att_sems):
    me = lax.axis_index("blk")
    plane, member = me // group, lax.rem(me, group)
    blocks, rows, width = tok_ref.shape
    length_all, total = blocks * rows, width // group
    heads = total // HD
    planes = [lax.rem(plane + k, slots) for k in range(1, slots)]
    members = [lax.rem(member + k, group) for k in range(1, group)]
    greet([{"blk": p * group + member} for p in planes]
          + [{"blk": plane * group + m} for m in members])

    low[...] = tok_in[...].astype(BF16)
    pending = []
    for k in range(1, slots):
        target = planes[k - 1]
        copy = send_to(low.at[target], tok_ref.at[me], send_a.at[k], recv_a.at[k],
                       {"blk": target * group + member})
        copy.start()
        pending.append(copy)
    tok_ref[me] = low[plane]

    def spread(k):
        block = lax.rem(plane + slots - k, slots) * group + member
        if k > 0:
            send_to(low.at[plane], tok_ref.at[block], send_a.at[k], recv_a.at[k],
                    {"blk": block}).wait_recv()
        for j in range(1, group):
            copy = send_to(tok_ref.at[block], tok_ref.at[block], send_b.at[k, j], recv_b.at[k, j],
                           {"blk": plane * group + members[j - 1]})
            copy.start()
            pending.append(copy)

    spread(0)
    cot_low[...] = cot_in[...].astype(BF16)
    for i, ref in enumerate((wq_ref, wk_ref, wv_ref)):
        w_ref[:, i * total:(i + 1) * total] = own_columns(ref, member, total)
    bias = jnp.concatenate(
        [own_entries(qb_ref, member, total), jnp.zeros((1, total), F32),
         own_entries(vb_ref, member, total)], axis=1)
    doc_len = len_ref[plane]
    chunk = group * rows

    def project(k):
        source = lax.rem(plane + slots - k, slots)
        for j in range(1, group):
            block = source * group + lax.rem(member + group - j, group)
            send_to(tok_ref.at[block], tok_ref.at[block], send_b.at[k, j], recv_b.at[k, j],
                    {"blk": plane * group + members[j - 1]}).wait_recv()
        span = pl.ds(pl.multiple_of(source * chunk, chunk), chunk)
        qkv = mm(tok_ref[pl.ds(source * group, group)].reshape(chunk, width), w_ref[...]) + bias
        lane = lax.broadcasted_iota(jnp.int32, (chunk, LANES), 1)
        position = source * chunk + lax.broadcasted_iota(jnp.int32, (chunk, LANES), 0)
        mask = jnp.where(position < doc_len, 0.0, MASKED)
        for h in range(heads):
            def part(which):
                cols = qkv[:, which * total + h * HD:which * total + (h + 1) * HD]
                return jnp.concatenate([cols, jnp.zeros_like(cols)], axis=1)
            q_ref[h, span, :] = jnp.where(
                lane == HD, 1.0, part(0).astype(BF16).astype(F32) * (HD ** -0.5)).astype(BF16)
            k_ref[h, span, :] = jnp.where(
                lane == HD, mask, jnp.where((lane > HD) & (lane < HD + 4), 1.0, part(1))).astype(BF16)
            v_rows = jnp.where((lane >= HD) & (lane < HD + 4), 1.0, part(2)).astype(BF16)
            v_ref[h, span, :] = v_rows
            vt[h, :, span] = v_rows.T

    for k in range(1, slots):
        spread(k)
        if k == slots - 1:
            for j in range(1, slots):
                target = planes[j - 1]
                copy = send_to(cot_low.at[target], cot_out.at[plane], cot_sems.at[0, j], cot_sems.at[1, j],
                               {"blk": target * group + member})
                copy.start()
                pending.append(copy)
            cot_out[plane] = cot_low[plane]
        project(k - 1)
    project(slots - 1)

    per_block = q_block // rows
    q_blocks = blocks // per_block

    def att_copy(p, g, slot, r):
        return send_to(att.at[p, g], att_in.at[slot, p], att_sems.at[0, p, r], att_sems.at[1, p, r],
                       {"blk": plane * group + g})

    def block(step, carry):
        which = lax.rem(step + member // per_block + 1, q_blocks)
        span = pl.ds(pl.multiple_of(which * q_block, q_block), q_block)
        done, tops = [], []
        for h in range(heads):
            top = jnp.full((8, q_block), MASKED, F32)
            for t in range(length_all // key_tile):
                keys = slice(t * key_tile, (t + 1) * key_tile)
                part = mm_nt(k_ref[h, keys, :], q_ref[h, span, :])
                scores[h, keys, :] = part
                top = jnp.maximum(top, jnp.max(part.reshape(key_tile // 8, 8, q_block), axis=0))
            tops.append(jnp.max(top, axis=0, keepdims=True))
        for h in range(heads):
            top = tops[h]
            mixed = jnp.zeros((LANES, q_block), F32)
            for t in range(length_all // key_tile):
                keys = slice(t * key_tile, (t + 1) * key_tile)
                weights = jnp.exp(scores[h, keys, :] - top).astype(BF16)
                mixed = mixed + mm(vt[h, :, keys], weights)
            denom = mixed[HD:HD + 1, :]
            scaled = mixed * (1.0 / denom)
            sub = lax.broadcasted_iota(jnp.int32, scaled.shape, 0)
            o_rows = jnp.where(sub == HD, top + jnp.log(denom), scaled).T
            o_ref[h, span, :] = o_rows
            done.append(o_rows[:, :HD].astype(BF16))
        attended = jnp.concatenate(done, axis=1)
        for u in range(per_block):
            d = which * per_block + u
            p, g = d // group, lax.rem(d, group)
            att[p, g] = attended[u * rows:(u + 1) * rows, :]

            @pl.when(g != member)
            def _():
                att_copy(p, g, member, lax.rem(g + group - member, group)).start()

            @pl.when(g == member)
            def _():
                att_in[member, p] = attended[u * rows:(u + 1) * rows, :]
        return carry

    lax.fori_loop(0, q_blocks, block, 0)
    for k in range(1, slots):
        source = lax.rem(plane + slots - k, slots)
        send_to(cot_low.at[plane], cot_out.at[source], cot_sems.at[0, k], cot_sems.at[1, k],
                {"blk": source * group + member}).wait_recv()
    for p in range(slots):
        for r in range(1, group):
            att_copy(p, member, lax.rem(member + group - r, group), r).wait_recv()
    for p in range(slots):
        for r in range(1, group):
            att_copy(p, members[r - 1], member, r).wait_send()
    for copy in pending:
        copy.wait_send()


def first(tokens, cotangent, weights, biases, lengths, blocks, collective_id, q_block=512, key_tile=256):
    slots, rows, width = tokens.shape
    group = blocks // slots
    length_all, total = blocks * rows, width // group
    heads = total // HD
    per_head = jax.ShapeDtypeStruct((heads, length_all, LANES), BF16)
    dma, vmem = pltpu.SemaphoreType.DMA, pltpu.VMEM
    return pl.pallas_call(
        functools.partial(first_kernel, slots, group, q_block, key_tile),
        out_shape=(
            jax.ShapeDtypeStruct((blocks, rows, width), BF16),
            jax.ShapeDtypeStruct((slots, rows, width), BF16),
            jax.ShapeDtypeStruct((group, slots, rows, total), BF16),
            per_head, per_head, per_head,
            jax.ShapeDtypeStruct((heads, length_all, LANES), F32),
        ),
        in_specs=[VMEM] * 7 + [SMEM],
        out_specs=(VMEM,) * 7,
        scratch_shapes=[
            vmem((slots, rows, width), BF16),
            vmem((slots, rows, width), BF16),
            vmem((heads, LANES, length_all), BF16),
            vmem((width, 3 * total), BF16),
            vmem((slots, group, rows, total), BF16),
            vmem((heads, length_all, q_block), F32),
            dma((slots,)), dma((slots,)), dma((slots, group)), dma((slots, group)), dma((2, slots)),
            dma((2, slots, group)),
        ],
        compiler_params=params(collective_id),
    )(tokens, cotangent, *weights, *biases, lengths)


def three(value):
    high = value.astype(BF16).astype(F32)
    mid = (value - high).astype(BF16).astype(F32)
    return high, mid, value - high - mid


def row_tile(rows):
    return next(t for t in (96, 64, 48, 32, 16) if rows % t == 0)


def over_rows(rows, body):
    step = row_tile(rows)

    def run(i, carry):
        body(i * step, step)
        return carry

    lax.fori_loop(0, rows // step, run, 0)


def rows_at(offset, i, step):
    return pl.ds(pl.multiple_of(offset + i, 16), step)


def rows_of(offset, n):
    return pl.ds(pl.multiple_of(offset, 16), n)


def bits_of(size):
    return [1 << i for i in range(size.bit_length() - 1)]


class Place:
    def __init__(self, docs, blocks, group):
        self.docs, self.blocks, self.group = docs, blocks, group
        self.planes = blocks // group
        self.me, self.doc = lax.axis_index("blk"), lax.axis_index("docs")
        self.plane, self.member = self.me // group, lax.rem(self.me, group)

    def pair(self, axis, bit):
        mine = self.me if axis == "blk" else self.doc
        on = lax.rem(mine // bit, 2)
        return {axis: mine + bit - 2 * bit * on}, on

    def member_peer(self, k):
        return lax.rem(self.member + k, self.group)

    def member_source(self, k):
        return lax.rem(self.member + self.group - k, self.group)

    def in_plane(self, member):
        return {"blk": self.plane * self.group + member}

    def in_line(self, plane):
        return {"blk": plane * self.group + self.member}

    def plane_peer(self, k):
        return lax.rem(self.plane + k, self.planes)

    def plane_source(self, k):
        return lax.rem(self.plane + self.planes - k, self.planes)


class Summer:
    def __init__(self, at, acc, sent, came, out, place, offset, rows, order, rest, sems, out_shift=0):
        self.at, self.acc, self.sent, self.came, self.out, self.sems = at, acc, sent, came, out, sems
        self.shift = out_shift
        self.stages = []
        for axis, bit in order:
            if axis == "planes":
                n = rows // at.planes
                self.stages.append(("planes", None, n, offset, offset + at.plane * n, place))
                offset, rows, place = offset + at.plane * n, n, place + (at.planes - 1) * n
                continue
            to, on = at.pair(axis, bit)
            n = rows // 2
            self.stages.append(("pair", to, n, offset + (1 - on) * n, offset + on * n, place))
            offset, rows, place = offset + on * n, n, place + n
        for axis, bit in rest:
            self.stages.append(("full", at.pair(axis, bit)[0], rows, offset, offset, place))
            place += rows
        self.count = len(self.stages)
        self.back = [s for s in range(self.count) if self.stages[s][0] != "full"][::-1]

    @staticmethod
    def placed(rows, order, planes, rest):
        total = 0
        for axis, _ in order:
            share = rows // planes if axis == "planes" else rows // 2
            total, rows = total + rows - share, share
        return total + rest * rows

    def copies(self, s, back=False, receive=False):
        kind, to, n, give, keep, place = self.stages[s]
        at, out = self.at, self.out
        w = 1 if back else 0
        if kind == "planes":
            found = []
            for k in range(1, at.planes):
                if back:
                    which = at.plane_source(k) if receive else at.plane
                    span = rows_of(give + which * n + self.shift, n)
                    src, dst = out.at[span], out.at[span]
                else:
                    src, dst = (ref.at[rows_of(place + (k - 1) * n, n)] for ref in (self.sent, self.came))
                to = at.in_line(at.plane_peer(k))
                found.append(send_to(src, dst, self.sems.at[w, 0, s, k], self.sems.at[w, 1, s, k], to))
            return found
        if back:
            span = rows_of((give if receive else keep) + self.shift, n)
            src, dst = out.at[span], out.at[span]
        else:
            src, dst = self.sent.at[rows_of(place, n)], self.came.at[rows_of(place, n)]
        return [send_to(src, dst, self.sems.at[w, 0, s, 0], self.sems.at[w, 1, s, 0], to)]

    def pack(self, give, place, n):
        def run(i, step):
            self.sent[rows_at(place, i, step), :] = self.acc[rows_at(give, i, step), :].astype(BF16)
        over_rows(n, run)

    def start(self, s):
        kind, to, n, give, keep, place = self.stages[s]
        if kind == "planes":
            for k in range(1, self.at.planes):
                self.pack(give + self.at.plane_peer(k) * n, place + (k - 1) * n, n)
        else:
            self.pack(give, place, n)
        for copy in self.copies(s):
            copy.start()

    def finish(self, s):
        kind, to, n, give, keep, place = self.stages[s]
        for copy in self.copies(s):
            copy.wait_recv()
        parts = self.at.planes - 1 if kind == "planes" else 1
        last = s == self.count - 1

        def run(i, step):
            total = self.acc[rows_at(keep, i, step), :]
            if kind == "full":
                total = total.astype(BF16).astype(F32)
            for k in range(parts):
                total = total + self.came[rows_at(place + k * n, i, step), :].astype(F32)
            if last:
                self.out[rows_at(keep + self.shift, i, step), :] = total.astype(BF16)
            else:
                self.acc[rows_at(keep, i, step), :] = total
        over_rows(n, run)

    def start_back(self, s):
        for copy in self.copies(s, back=True):
            copy.start()

    def finish_back(self, s):
        for copy in self.copies(s, back=True, receive=True):
            copy.wait_recv()

    def events(self, back):
        def first():
            self.start(0)

        def inward(s):
            self.finish(s)
            if s + 1 < self.count:
                self.start(s + 1)
            elif back:
                self.start_back(back[0])

        def outward(d):
            self.finish_back(back[d])
            if d + 1 < len(back):
                self.start_back(back[d + 1])

        return ([first] + [functools.partial(inward, s) for s in range(self.count)]
                + [functools.partial(outward, d) for d in range(len(back))])

    def drain(self, back):
        for s in range(self.count):
            for copy in self.copies(s):
                copy.wait_send()
        for s in back:
            for copy in self.copies(s, back=True):
                copy.wait_send()


def row_mean(value):
    return jnp.mean(value, axis=1, keepdims=True)


def col_sum(value):
    return jnp.sum(value, axis=0, keepdims=True)


def main_kernel(docs, blocks, group, cuts, k_block, q_tile,
                att_in, cot_ref, len_ref, wo_ref, ob_ref, g1_ref, s1_ref, up_hbm, ub_ref, down_hbm,
                db_ref, g2_ref, s2_ref, wq_ref, wk_ref, wv_ref, q_ref, k_ref, v_ref, o_ref, tok_ref,
                out_in, grad_in, sum_ref, qkv_ref, small_out,
                att, hid_t, gz, away, kv_in, gq_in, g_att, g_in, qx, gx, qt, gt, gq_acc, kv_send, gq_send,
                acc, sent, came, dwt, sent_w, came_w, bias, small_sent, small_came,
                g_sems, kv_sems, gq_sems, sum_sems, w_sems, small_sems, wide_sems, core_sems, load_sems,
                out_sems, grad_sems):
    at = Place(docs, blocks, group)
    me, member, plane, planes = at.me, at.member, at.plane, at.planes
    _, rows, width = tok_ref.shape
    count = planes * rows
    cols = width // group
    inner_width = up_hbm.shape[1]
    heads, length_all, _ = q_ref.shape
    parts = inner_width // width
    doc_bits = bits_of(docs)

    loads = [pltpu.make_async_copy(up_hbm.at[:, c * width:(c + 1) * width],
                                   sent.at[inner_width + c * width:inner_width + (c + 1) * width], load_sems.at[c])
             for c in range(parts)]
    loads.append(pltpu.make_async_copy(down_hbm, sent.at[:inner_width], load_sems.at[parts]))
    for load in loads:
        load.start()

    def up_part(c):
        return sent[inner_width + c * width:inner_width + (c + 1) * width, :]

    greet([at.in_plane(at.member_peer(k)) for k in range(1, group)]
          + [at.in_line(at.plane_peer(k)) for k in range(1, planes)]
          + [at.pair("docs", bit)[0] for bit in doc_bits])

    rest = [("docs", bit) for bit in doc_bits[1:]]
    sums, place = [], 0
    for c, (offset, size, order) in enumerate(cuts):
        sums.append(Summer(at, acc, sent, came, sum_ref, place, offset, size, order, rest, sum_sems.at[c]))
        place = place + Summer.placed(size, order, planes, len(rest))
    chains = [s.events(s.back) for s in sums]
    at_event = [0] * len(cuts)

    def upcoming(numbers):
        found = []
        for c in numbers:
            if at_event[c] < len(chains[c]):
                found.append(chains[c][at_event[c]])
                at_event[c] += 1
        return found

    def advance(numbers):
        for event in upcoming(numbers):
            event()

    flat = jnp.concatenate([tok_ref[p * group + member].astype(F32) for p in range(planes)], axis=0)
    for p in range(planes):
        for g in range(group):
            att[p * rows:(p + 1) * rows, g * cols:(g + 1) * cols] = att_in[g, p]
    up_bias = row(ub_ref)
    gain1, gain2 = row(g1_ref), row(g2_ref)
    summed = flat + mm(att[...], wo_ref[...]) + row(ob_ref)
    centred = summed - row_mean(summed)
    rstd1 = lax.rsqrt(row_mean(centred * centred) + EPS)
    xhat1 = centred * rstd1
    hidden = xhat1 * gain1 + row(s1_ref)
    hidden_low = hidden.astype(BF16)
    hid_t[...] = hidden_low.T
    for load in loads:
        load.wait()
    ffn = jnp.zeros((count, width), F32)
    for c in range(parts):
        span = slice(c * width, (c + 1) * width)
        inner = mm(hidden_low, up_part(c)) + up_bias[:, span]
        square = inner * inner
        slope_in = 0.7978845608 * (1.0 + (3 * 0.044715) * square)
        tanh = jnp.tanh(inner * (0.7978845608 * (1.0 + 0.044715 * square)))
        half = 0.5 * (1.0 + tanh)
        acc[c * count:(c + 1) * count, :] = half + (0.5 * inner) * ((1.0 - tanh * tanh) * slope_in)
        low = (inner * half).astype(BF16)
        sum_ref[c * count:(c + 1) * count, :] = low
        ffn = ffn + mm(low, sent[span, :])
    summed = flat + hidden + ffn + row(db_ref)
    centred = summed - row_mean(summed)
    rstd2 = lax.rsqrt(row_mean(centred * centred) + EPS)
    xhat2 = centred * rstd2
    away[...] = (xhat2 * gain2 + row(s2_ref)).astype(BF16).reshape(planes, rows, width)

    def line_copies(dst, sems, receive=False):
        return [send_to(away.at[at.plane_peer(k)], dst.at[at.plane_source(k) if receive else plane],
                        sems.at[0, k], sems.at[1, k], at.in_line(at.plane_peer(k))) for k in range(1, planes)]

    for copy in line_copies(out_in, out_sems):
        copy.start()
    out_in[plane] = away[plane]
    lane_r = lax.broadcasted_iota(jnp.int32, (rows, width), 0)
    g_out = jnp.concatenate(
        [jnp.where((p * group + member) * rows + lane_r < len_ref[plane], cot_ref[p].astype(F32), 0.0)
         for p in range(planes)], axis=0)
    small_sent[0] = jnp.zeros(small_sent.shape[1:], F32)
    small_sent[0, 0:1, :] = col_sum(g_out * xhat2)
    small_sent[0, 1:2, :] = col_sum(g_out)
    scaled = g_out * gain2
    g_z2 = rstd2 * (scaled - row_mean(scaled) - xhat2 * row_mean(scaled * xhat2))
    g_ffn = g_z2.astype(BF16)
    small_sent[0, 2:3, :] = col_sum(g_ffn.astype(F32))
    g_hidden = g_z2
    for c in range(parts):
        span = slice(c * width, (c + 1) * width)
        g_inner = (mm_nt(g_ffn, sent[span, :]) * acc[c * count:(c + 1) * count, :]).astype(BF16)
        sum_ref[inner_width + c * count:inner_width + (c + 1) * count, :] = g_inner
        g_hidden = g_hidden + mm_nt(g_inner, up_part(c))
    scaled = g_hidden * gain1
    g_z1 = rstd1 * (scaled - row_mean(scaled) - xhat1 * row_mean(scaled * xhat1))
    g_branch = g_z1.astype(BF16)
    gz[...] = g_z1 + g_z2
    g_low = mm_nt(g_branch, wo_ref[...]).astype(BF16)
    for p in range(planes):
        for g in range(group):
            g_att[g, p] = g_low[p * rows:(p + 1) * rows, g * cols:(g + 1) * cols]

    def g_copy(k, receive=False):
        slot = at.member_source(k) if receive else member
        return send_to(g_att.at[at.member_peer(k)], g_in.at[:, slot], g_sems.at[0, k], g_sems.at[1, k],
                       at.in_plane(at.member_peer(k)))

    for k in range(1, group):
        g_copy(k).start()
    for p in range(planes):
        g_in[p, member] = g_att[member, p]

    for c in range(parts):
        span = slice(c * width, (c + 1) * width)
        acc[span, :] = mm_tn(sum_ref[c * count:(c + 1) * count, :], g_ffn)
    advance(POINTS[0])
    for c in range(parts):
        g_inner = sum_ref[inner_width + c * count:inner_width + (c + 1) * count, :]
        small_sent[0, 6 + c:7 + c, :] = col_sum(g_inner.astype(F32))
        acc[inner_width + c * width:inner_width + (c + 1) * width, :] = mm(hid_t[...], g_inner)
    acc[2 * inner_width:2 * inner_width + width, :] = mm_tn(att[...], g_branch)
    if acc.shape[0] > 2 * inner_width + width:
        acc[2 * inner_width + width:, :] = jnp.zeros((acc.shape[0] - 2 * inner_width - width, width), F32)
    advance(POINTS[1])
    small_sent[0, 3:4, :] = col_sum(g_hidden * xhat1)
    small_sent[0, 4:5, :] = col_sum(g_hidden)
    small_sent[0, 5:6, :] = col_sum(g_branch.astype(F32))
    chunk = group * rows
    lane = lax.broadcasted_iota(jnp.int32, (chunk, LANES), 1)

    def prepare_q(step, carry):
        span = pl.ds(pl.multiple_of(step * chunk, chunk), chunk)
        for h in range(heads):
            q_rows = q_ref[h, span, :].astype(F32)
            ext = q_rows
            for i, value in enumerate(three(-o_ref[h, span, HD:HD + 1])):
                ext = jnp.where(lane == HD + 1 + i, value, ext)
            qx[h, span, :] = ext.astype(BF16)
            qt[h, :, span] = q_rows[:, :HD].T.astype(BF16)
        return carry

    lax.fori_loop(0, planes, prepare_q, 0)
    advance(POINTS[2])
    for k in range(1, group):
        g_copy(k, True).wait_recv()

    def prepare_g(step, carry):
        span = pl.ds(pl.multiple_of(step * chunk, chunk), chunk)
        g_block = g_in[step].reshape(chunk, cols)
        for h in range(heads):
            g_rows = g_block[:, h * HD:(h + 1) * HD].astype(F32)
            g_rows = jnp.concatenate([g_rows, jnp.zeros_like(g_rows)], axis=1)
            delta = jnp.sum(g_rows * o_ref[h, span, :], axis=1, keepdims=True)
            ext = g_rows
            for i, value in enumerate(three(-delta)):
                ext = jnp.where(lane == HD + i, value, ext)
            gx[h, span, :] = ext.astype(BF16)
            gt[h, :, span] = g_rows[:, :HD].T.astype(BF16)
        return carry

    lax.fori_loop(0, planes, prepare_g, 0)
    advance(POINTS[3])

    k_blocks = length_all // k_block
    per_block = k_block // rows
    ones = jnp.ones((8, k_block), BF16)
    dwt[...] = jnp.zeros_like(dwt)
    bias[...] = jnp.zeros_like(bias)

    def kv_copy(h, p, g, slot, r):
        return send_to(kv_send.at[h, p, g], kv_in.at[slot, h, p], kv_sems.at[0, h, p, r], kv_sems.at[1, h, p, r],
                       at.in_plane(g))

    def gq_copy(h, r, receive=False):
        slot = at.member_source(r) if receive else member
        return send_to(gq_send.at[h, :, at.member_peer(r)], gq_in.at[slot, h], gq_sems.at[0, h, r],
                       gq_sems.at[1, h, r], at.in_plane(at.member_peer(r)))

    total_steps = heads * k_blocks
    timed = [(t, event) for t in range(min(total_steps, len(AT_BLOCK))) for event in upcoming(AT_BLOCK[t])]

    def block(step, carry):
        h, i = step // k_blocks, lax.rem(step, k_blocks)
        which = lax.rem(i + member // per_block + 1, k_blocks)
        span = pl.ds(pl.multiple_of(which * k_block, k_block), k_block)
        k_rows, v_rows = k_ref[h, span, :], v_ref[h, span, :]

        @pl.when(i == 0)
        def _():
            gq_acc[...] = jnp.zeros_like(gq_acc)

        gk = jnp.zeros((HD, k_block), F32)
        gv = jnp.zeros((HD, k_block), F32)
        tiles = [slice(t, t + q_tile) for t in range(0, length_all, q_tile)]

        def products(tile):
            return mm_nt(qx[h, tile, :], k_rows), mm_nt(gx[h, tile, :], v_rows)

        ahead = products(tiles[0])
        for tile, later in zip(tiles, tiles[1:] + [None]):
            scores, centred = ahead
            ahead = products(later) if later else None
            weights = jnp.exp(scores)
            g_scores = (weights * centred).astype(BF16)
            gv = gv + mm(gt[h, :, tile], weights.astype(BF16))
            gk = gk + mm(qt[h, :, tile], g_scores)
            gq_acc[tile, :] += mm(g_scores, k_rows)
        kv = jnp.concatenate([gk, gv], axis=0).astype(BF16)
        tok_rows = tok_ref[pl.ds(which * per_block, per_block)].reshape(k_block, width)
        dwt[pl.ds(pl.multiple_of(h * 2 * HD, 2 * HD), 2 * HD), :] += mm(kv, tok_rows)
        bias[h, 0] += mm_nt(ones, kv[HD:])
        for u in range(per_block):
            d = which * per_block + u
            p, g = d // group, lax.rem(d, group)
            kv_send[h, p, g] = kv[:, u * rows:(u + 1) * rows]

            @pl.when(g != member)
            def _():
                kv_copy(h, p, g, member, lax.rem(g + group - member, group)).start()

            @pl.when(g == member)
            def _():
                kv_in[member, h, p] = kv[:, u * rows:(u + 1) * rows]

        @pl.when(i == k_blocks - 1)
        def _():
            for n in range(blocks):
                gq_send[h, n // group, n % group] = (
                    gq_acc[n * rows:(n + 1) * rows, :HD] * (HD ** -0.5)).T.astype(BF16)
            for r in range(1, group):
                gq_copy(h, r).start()
            for p in range(planes):
                gq_in[member, h, p] = gq_send[h, p, member]

        for t, event in timed:
            pl.when(step == t)(event)
        return carry

    lax.fori_loop(0, total_steps, block, 0)

    q_base = heads * 2 * HD
    for h in range(heads):
        part = jnp.zeros((HD, width), F32)
        q_bias = jnp.zeros((8, HD), F32)
        for n in range(blocks):
            low = gq_send[h, n // group, n % group]
            part = part + mm(low, tok_ref[n])
            q_bias = q_bias + mm_nt(jnp.ones((8, rows), BF16), low)
        dwt[q_base + h * HD:q_base + (h + 1) * HD, :] = part
        bias[h, 1] = q_bias
    half = dwt.shape[0] // 2
    my_core = lax.rem(at.doc, 2)
    w_sum = Summer(at, dwt, sent_w, came_w, qkv_ref, 0, 0, 2 * half, W_ORDER, rest, w_sems,
                   out_shift=my_core * (half * group - half) + member * half)
    w_back = [s for s in w_sum.back if w_sum.stages[s][0] == "planes"]
    w_chain = w_sum.events(w_back)
    w_chain[0]()
    lane_w = lax.broadcasted_iota(jnp.int32, (8, width), 1)
    sub = lax.broadcasted_iota(jnp.int32, (8, width), 0)
    wide = [jnp.concatenate([bias[h, i] for h in range(heads)] * group, axis=1) for i in range(2)]
    small_sent[0, 16:24, :] = jnp.where(
        (lane_w // cols) == member, jnp.where(sub == 0, wide[1], jnp.where(sub == 1, wide[0], 0.0)), 0.0)
    small_order = [("docs", 1)] + [("blk", bit) for bit in bits_of(group)]

    def small_copy(s):
        return send_to(small_sent.at[s], small_came.at[s], small_sems.at[0, s], small_sems.at[1, s],
                       at.pair(*small_order[s])[0])

    small_last = len(small_order)

    def small_line(k, receive=False):
        slot = small_last + k
        return send_to(small_sent.at[small_last], small_came.at[slot], small_sems.at[0, slot],
                       small_sems.at[1, slot], at.in_line(at.plane_peer(k)))

    def small_rest(i):
        slot = small_last + planes + i
        return send_to(small_sent.at[small_last + 1 + i], small_came.at[slot], small_sems.at[0, slot],
                       small_sems.at[1, slot], at.pair(*rest[i])[0])

    def small_step(s):
        small_copy(s).wait_recv()
        small_sent[s + 1] = small_sent[s] + small_came[s]
        if s + 1 < small_last:
            small_copy(s + 1).start()
        else:
            for k in range(1, planes):
                small_line(k).start()

    def small_end():
        for k in range(1, planes):
            small_line(k).wait_recv()
        total = jnp.zeros(small_sent.shape[1:], F32)
        for p in range(planes):
            value = small_sent[small_last]
            for k in range(1, planes):
                value = jnp.where(at.plane_source(k) == p, small_came[small_last + k], value)
            total = total + value
        for i in range(len(rest)):
            small_sent[small_last + 1 + i] = total
            small_rest(i).start()
            small_rest(i).wait_recv()
            total = total + small_came[small_last + planes + i]
        small_out[...] = total

    small_copy(0).start()

    def slab(m):
        return rows_of(my_core * half * group + m * half, half)

    def wide_copy(k, m):
        return send_to(qkv_ref.at[slab(m)], qkv_ref.at[slab(m)], wide_sems.at[0, k], wide_sems.at[1, k],
                       at.in_plane(at.member_peer(k)))

    def core_copy(core):
        span = rows_of(core * half * group, half * group)
        return send_to(qkv_ref.at[span], qkv_ref.at[span], core_sems.at[0], core_sems.at[1],
                       at.pair("docs", 1)[0])

    def wide_start():
        for k in range(1, group):
            wide_copy(k, member).start()

    def wide_wait():
        for k in range(1, group):
            wide_copy(k, at.member_source(k)).wait_recv()
        core_copy(my_core).start()

    def gather_part(which):
        for p in range(planes):
            for g in range(group):
                for h in range(heads):
                    low = gq_in[g, h, p] if which == 0 else kv_in[g, h, p, (which - 1) * HD:which * HD, :]
                    hid_t[g * cols + h * HD:g * cols + (h + 1) * HD, p * rows:(p + 1) * rows] = low
        return hid_t[...].T

    def key_value_rows():
        for h in range(heads):
            for p in range(planes):
                for r in range(1, group):
                    kv_copy(h, p, member, at.member_source(r), r).wait_recv()
        gz[...] += mm_nt(gather_part(1), wk_ref[...])
        gz[...] += mm_nt(gather_part(2), wv_ref[...])

    def query_rows():
        for h in range(heads):
            for r in range(1, group):
                gq_copy(h, r, True).wait_recv()
        total = gz[...] + mm_nt(gather_part(0), wq_ref[...])
        for copy in line_copies(out_in, out_sems, True):
            copy.wait_recv()
        for copy in line_copies(out_in, out_sems):
            copy.wait_send()
        away[...] = total.astype(BF16).reshape(planes, rows, width)
        for copy in line_copies(grad_in, grad_sems):
            copy.start()
        grad_in[plane] = away[plane]

    w_events = w_chain[1:] + [wide_start, wide_wait]
    small_events = [functools.partial(small_step, s) for s in range(small_last)] + [small_end]
    named = {"w": w_events, "g": [key_value_rows, query_rows], "s": small_events}
    for name in AFTER:
        if name in named:
            if named[name]:
                named[name].pop(0)()
        else:
            advance((name,))
    while any(named.values()) or any(at_event[c] < len(chains[c]) for c in range(len(cuts))):
        for work in named.values():
            if work:
                work.pop(0)()
        advance(range(len(cuts)))
    core_copy(1 - my_core).wait_recv()
    for copy in line_copies(grad_in, grad_sems, True):
        copy.wait_recv()
    for copy in line_copies(grad_in, grad_sems):
        copy.wait_send()
    for r in range(1, group):
        g_copy(r).wait_send()
        for h in range(heads):
            gq_copy(h, r).wait_send()
            for p in range(planes):
                kv_copy(h, p, at.member_peer(r), member, r).wait_send()
    for part in sums:
        part.drain(part.back)
    w_sum.drain(w_back)
    for k in range(1, group):
        wide_copy(k, member).wait_send()
    core_copy(my_core).wait_send()
    for s in range(small_last):
        small_copy(s).wait_send()
    for k in range(1, planes):
        small_line(k).wait_send()
    for i in range(len(rest)):
        small_rest(i).wait_send()


def member_bits(group, name):
    bits = bits_of(group)
    return bits[:len(bits) // 2] if name == "x" else bits[len(bits) // 2:]


SUMS = ((2, ("yxz", "xyz")), (3, ("zxy", "yxz", "xyz")))
W_ORDER = [("docs", 1), ("planes", 0)]
POINTS = ((0,), (4, 0, 3, 4, 2,), (1, 3, 2, 0, 1, 4,), ())
AT_BLOCK = ((0,), (2, 3, 4, 1,), (2, 0,),
            (3, 4, 1, 2,), (), (2, 3,),
            (0, 1, 2, 4,), ())
AFTER = ("w", 1, 3, "s", "w", "s", 4, 0, "g", "w", "s", 2, 1, 3, "g", 0, "w", 1, 0, 4, "s", 3, 3, "w", "g",
         1, 2, 4, "s", "w",)


def main(docs, blocks, group, att_in, cotangent, lengths, weights, attention, tok_doc, collective_id,
         k_block=512, q_tile=256):
    q = attention[0]
    heads, length_all, _ = q.shape
    _, rows, width = tok_doc.shape
    planes = blocks // group
    count = planes * rows
    cols = heads * HD
    inner_width = weights[4].shape[1]
    features = -(-3 * cols // 128) * 128
    unit = 32 * blocks
    second = -(-(inner_width + width) // unit)
    cuts, offset = [], 0
    for (pieces, turns), units in zip(SUMS, (inner_width // unit, second)):
        pieces = min(pieces, units)
        for i in range(pieces):
            size = unit * (units // pieces + (1 if i >= pieces - units % pieces else 0))
            cuts.append((offset, size, [("docs", 1)] + [
                step for name in turns[i] for step in (
                    [("planes", 0)] if name == "z" else [("blk", bit) for bit in member_bits(group, name)])]))
            offset += size
    total = inner_width + second * unit
    members, rest = len(bits_of(group)), len(bits_of(docs)) - 1
    placed = sum(Summer.placed(size, order, planes, rest) for _, size, order in cuts)
    w_placed = Summer.placed(features, W_ORDER, planes, rest)
    stages = 2 + members + rest
    steps = 1 + members + planes + rest
    dma, vmem = pltpu.SemaphoreType.DMA, pltpu.VMEM
    return pl.pallas_call(
        functools.partial(main_kernel, docs, blocks, group, cuts, k_block, q_tile),
        out_shape=(
            jax.ShapeDtypeStruct((planes, rows, width), BF16),
            jax.ShapeDtypeStruct((planes, rows, width), BF16),
            jax.ShapeDtypeStruct((total, width), BF16),
            jax.ShapeDtypeStruct((features * group, width), BF16),
            jax.ShapeDtypeStruct((24, width), F32),
        ),
        in_specs=[VMEM] * 2 + [SMEM] + [VMEM] * 4 + [ANY, VMEM, ANY] + [VMEM] * 11,
        out_specs=(VMEM,) * 5,
        scratch_shapes=[
            vmem((count, width), BF16),
            vmem((width, count), BF16),
            vmem((count, width), F32),
            vmem((planes, rows, width), BF16),
            vmem((group, heads, planes, 2 * HD, rows), BF16),
            vmem((group, heads, planes, HD, rows), BF16),
            vmem((group, planes, rows, cols), BF16),
            vmem((planes, group, rows, cols), BF16),
            vmem((heads, length_all, LANES), BF16),
            vmem((heads, length_all, LANES), BF16),
            vmem((heads, HD, length_all), BF16),
            vmem((heads, HD, length_all), BF16),
            vmem((length_all, LANES), F32),
            vmem((heads, planes, group, 2 * HD, rows), BF16),
            vmem((heads, planes, group, HD, rows), BF16),
            vmem((total, width), F32),
            vmem((max(placed, 2 * inner_width), width), BF16),
            vmem((placed, width), BF16),
            vmem((features, width), F32),
            vmem((w_placed, width), BF16),
            vmem((w_placed, width), BF16),
            vmem((heads, 2, 8, HD), F32),
            vmem((steps, 24, width), F32),
            vmem((steps, 24, width), F32),
            dma((2, group)),
            dma((2, heads, planes, group)),
            dma((2, heads, group)),
            dma((len(cuts), 2, 2, stages, planes)),
            dma((2, 2, 2 + rest, planes)),
            dma((2, steps)),
            dma((2, group)),
            dma((2,)),
            dma((inner_width // width + 1,)),
            dma((2, planes)),
            dma((2, planes)),
        ],
        compiler_params=params(collective_id),
    )(att_in, cotangent, lengths, *weights, *attention, tok_doc)


def last_kernel(group, heads, out_in, grad_in, sum_ref, qkv_ref, small_ref,
                out_ref, grad_ref, qw_ref, qb_ref, kw_ref, vw_ref, vb_ref, ow_ref, ob_ref, g1_ref, s1_ref,
                uw_ref, ub_ref, dw_ref, db_ref, g2_ref, s2_ref, stack):
    width = ow_ref.shape[0]
    inner_width = uw_ref.shape[1]
    cols = width // group

    def widen(out, rows_out, cols_out, base):
        step = row_tile(rows_out)

        def run(i, carry):
            span = pl.ds(pl.multiple_of(i * step, step), step)
            out[span, cols_out] = sum_ref[pl.ds(pl.multiple_of(base + i * step, 16), step), :].astype(F32)
            return carry

        lax.fori_loop(0, rows_out // step, run, 0)

    widen(dw_ref, inner_width, slice(None), 0)
    for c in range(inner_width // width):
        widen(uw_ref, width, slice(c * width, (c + 1) * width), inner_width + c * width)
    widen(ow_ref, width, slice(None), 2 * inner_width)
    out_ref[...] = out_in[...].astype(F32)
    grad_ref[...] = grad_in[...].astype(F32)
    half = qkv_ref.shape[0] // group // 2
    unit = HD // 2
    for which, out in enumerate((qw_ref, kw_ref, vw_ref)):
        for g in range(group):
            for h in range(heads):
                first = heads * 2 * HD + h * HD if which == 0 else h * 2 * HD + (which - 1) * HD
                for u in range(2):
                    f = first + u * unit
                    at = f // half * half * group + g * half + f % half
                    to = g * cols + h * HD + u * unit
                    stack[to:to + unit, :] = qkv_ref[at:at + unit, :]
        out[...] = stack[...].T.astype(F32)

    def vector(out, i):
        out[...] = small_ref[i:i + 1, :].reshape(out.shape)

    for i, out in ((16, qb_ref), (17, vb_ref), (0, g2_ref), (1, s2_ref), (2, db_ref), (3, g1_ref), (4, s1_ref),
                   (5, ob_ref)):
        vector(out, i)
    parts = inner_width // width
    ub_ref[...] = jnp.concatenate([small_ref[6 + i:7 + i, :] for i in range(parts)], axis=1).reshape(ub_ref.shape)


def last(group, shape, inner_width, *arrays):
    width = shape[-1]
    heads = width // group // HD
    whole = jax.ShapeDtypeStruct(shape, F32)
    square = jax.ShapeDtypeStruct((width, width), F32)
    vector = jax.ShapeDtypeStruct((width,), F32)
    return pl.pallas_call(
        functools.partial(last_kernel, group, heads),
        out_shape=(
            whole, whole, square, vector, square, square, vector, square, vector,
            vector, vector, jax.ShapeDtypeStruct((width, inner_width), F32),
            jax.ShapeDtypeStruct((inner_width,), F32), jax.ShapeDtypeStruct((inner_width, width), F32),
            vector, vector, vector,
        ),
        in_specs=[VMEM] * len(arrays),
        out_specs=(VMEM,) * 17,
        scratch_shapes=[pltpu.VMEM((width, width), BF16)],
        compiler_params=params(),
    )(*arrays)


def device_program(docs, blocks, tokens, query_weight, query_bias, key_weight, value_weight, value_bias,
                   out_weight, out_bias, first_gain, first_shift, up_weight, up_bias, down_weight,
                   down_bias, second_gain, second_shift, cotangent, lengths):
    slots, rows, width = tokens.shape
    inner_width = up_weight.shape[1]
    group = blocks // slots
    projections = (query_weight, key_weight, value_weight)
    tok_doc, cot, att_in, q, k, v, o = first(tokens, cotangent, projections, (query_bias, value_bias), lengths,
                                             blocks, 0)
    parts = main(
        docs, blocks, group, att_in, cot, lengths,
        (out_weight, out_bias, first_gain, first_shift, up_weight, up_bias, down_weight, down_bias,
         second_gain, second_shift, *projections), (q, k, v, o), tok_doc, 1)
    return last(group, tokens.shape, inner_width, *parts)


def solution(mesh):
    split = P("docs", "blk", None)
    return jax.shard_map(
        functools.partial(device_program, mesh.shape["docs"], mesh.shape["blk"]),
        mesh=mesh,
        in_specs=(split,) + (P(),) * 15 + (split, P("docs")),
        out_specs=(split, split) + (P(),) * 15,
        check_vma=False,
    )
```

```python
import functools

import jax
import jax.numpy as jnp
from jax import lax
from jax.experimental import pallas as pl
from jax.experimental.pallas import tpu as pltpu
from jax.sharding import PartitionSpec as P

HD = 64
LANES = 128
EPS = 1e-05
MASKED = -1e30
F32 = jnp.float32
BF16 = jnp.bfloat16
VMEM = pl.BlockSpec(memory_space=pltpu.VMEM)
ANY = pl.BlockSpec(memory_space=pl.ANY)
SMEM = pl.BlockSpec(memory_space=pltpu.SMEM)
MESH = pl.DeviceIdType.MESH
VMEM_LIMIT = 63 * 1024 * 1024


def mm(left, right):
    return jnp.dot(left, right, preferred_element_type=F32)


def mm_nt(left, right):
    return lax.dot_general(left, right, (((1,), (1,)), ((), ())), preferred_element_type=F32)


def mm_tn(left, right):
    return lax.dot_general(left, right, (((0,), (0,)), ((), ())), preferred_element_type=F32)


def params(collective_id=None):
    if collective_id is None:
        return pltpu.CompilerParams(vmem_limit_bytes=VMEM_LIMIT)
    return pltpu.CompilerParams(
        vmem_limit_bytes=VMEM_LIMIT, collective_id=collective_id, has_side_effects=True
    )


def greet(peers):
    barrier = pltpu.get_barrier_semaphore()
    for peer in peers:
        pl.semaphore_signal(barrier, inc=1, device_id=peer, device_id_type=MESH)
    pl.semaphore_wait(barrier, len(peers))


def send_to(src, dst, send_sem, recv_sem, peer):
    return pltpu.make_async_remote_copy(
        src_ref=src, dst_ref=dst, send_sem=send_sem, recv_sem=recv_sem,
        device_id=peer, device_id_type=MESH,
    )


def row(ref):
    return ref[...].astype(F32).reshape(1, ref.shape[0])


def own_columns(ref, member, cols):
    if cols % LANES == 0:
        return ref[:, pl.ds(pl.multiple_of(member * cols, LANES), cols)]
    per = LANES // cols
    both = ref[:, pl.ds(pl.multiple_of(member // per * LANES, LANES), LANES)].astype(F32)
    return sum(jnp.where(lax.rem(member, per) == i, both[:, i * cols:(i + 1) * cols], 0.0)
               for i in range(per)).astype(BF16)


def own_entries(ref, member, cols):
    values = row(ref)
    return sum(jnp.where(member == i, values[:, i * cols:(i + 1) * cols], 0.0)
               for i in range(ref.shape[0] // cols))


def first_kernel(slots, group, q_block, key_tile, tok_in, cot_in, wq_ref, wk_ref, wv_ref, qb_ref, vb_ref, len_ref,
                 tok_out, cot_out, att_in, q_out, k_out, v_out, o_out,
                 tok_ref, q_ref, k_ref, v_ref, o_ref, low, cot_low, vt, w_ref, att, scores, send_a, recv_a, send_b, recv_b, cot_sems, att_sems, leave_sems):
    me = lax.axis_index("blk")
    plane, member = me // group, lax.rem(me, group)
    blocks, rows, width = tok_ref.shape
    length_all, total = blocks * rows, width // group
    heads = total // HD
    planes = [lax.rem(plane + k, slots) for k in range(1, slots)]
    members = [lax.rem(member + k, group) for k in range(1, group)]
    greet([{"blk": p * group + member} for p in planes]
          + [{"blk": plane * group + m} for m in members])

    low[...] = tok_in[...].astype(BF16)
    pending = []
    for k in range(1, slots):
        target = planes[k - 1]
        copy = send_to(low.at[target], tok_ref.at[me], send_a.at[k], recv_a.at[k],
                       {"blk": target * group + member})
        copy.start()
        pending.append(copy)
    tok_ref[me] = low[plane]

    def spread(k):
        block = lax.rem(plane + slots - k, slots) * group + member
        if k > 0:
            send_to(low.at[plane], tok_ref.at[block], send_a.at[k], recv_a.at[k],
                    {"blk": block}).wait_recv()
        for j in range(1, group):
            copy = send_to(tok_ref.at[block], tok_ref.at[block], send_b.at[k, j], recv_b.at[k, j],
                           {"blk": plane * group + members[j - 1]})
            copy.start()
            pending.append(copy)

    spread(0)
    cot_low[...] = cot_in[...].astype(BF16)
    for i, ref in enumerate((wq_ref, wk_ref, wv_ref)):
        w_ref[:, i * total:(i + 1) * total] = own_columns(ref, member, total)
    bias = jnp.concatenate(
        [own_entries(qb_ref, member, total), jnp.zeros((1, total), F32),
         own_entries(vb_ref, member, total)], axis=1)
    doc_len = len_ref[plane]
    chunk = group * rows

    def project(k):
        source = lax.rem(plane + slots - k, slots)
        for j in range(1, group):
            block = source * group + lax.rem(member + group - j, group)
            send_to(tok_ref.at[block], tok_ref.at[block], send_b.at[k, j], recv_b.at[k, j],
                    {"blk": plane * group + members[j - 1]}).wait_recv()
        span = pl.ds(pl.multiple_of(source * chunk, chunk), chunk)
        qkv = mm(tok_ref[pl.ds(source * group, group)].reshape(chunk, width), w_ref[...]) + bias
        lane = lax.broadcasted_iota(jnp.int32, (chunk, LANES), 1)
        position = source * chunk + lax.broadcasted_iota(jnp.int32, (chunk, LANES), 0)
        mask = jnp.where(position < doc_len, 0.0, MASKED)
        for h in range(heads):
            def part(which):
                cols = qkv[:, which * total + h * HD:which * total + (h + 1) * HD]
                return jnp.concatenate([cols, jnp.zeros_like(cols)], axis=1)
            q_ref[h, span, :] = jnp.where(
                lane == HD, 1.0, part(0).astype(BF16).astype(F32) * (HD ** -0.5)).astype(BF16)
            k_ref[h, span, :] = jnp.where(
                lane == HD, mask, jnp.where((lane > HD) & (lane < HD + 4), 1.0, part(1))).astype(BF16)
            v_rows = jnp.where((lane >= HD) & (lane < HD + 4), 1.0, part(2)).astype(BF16)
            v_ref[h, span, :] = v_rows
            vt[h, :, span] = v_rows.T
        members_of = pl.ds(source * group, group)
        leave(tok_ref.at[members_of], tok_out.at[members_of], leave_sems.at[0, k])
        for i, (ref, out) in enumerate(((q_ref, q_out), (k_ref, k_out), (v_ref, v_out))):
            leave(ref.at[:, span], out.at[:, span], leave_sems.at[1 + i, k])

    leaving = []

    def leave(src, dst, sem):
        copy = pltpu.make_async_copy(src, dst, sem)
        copy.start()
        leaving.append(copy)

    for k in range(1, slots):
        spread(k)
        if k == slots - 1:
            for j in range(1, slots):
                target = planes[j - 1]
                copy = send_to(cot_low.at[target], cot_out.at[plane], cot_sems.at[0, j], cot_sems.at[1, j],
                               {"blk": target * group + member})
                copy.start()
                pending.append(copy)
            cot_out[plane] = cot_low[plane]
        project(k - 1)
    project(slots - 1)

    per_block = q_block // rows
    q_blocks = blocks // per_block

    def att_copy(p, g, slot, r):
        return send_to(att.at[p, g], att_in.at[slot, p], att_sems.at[0, p, r], att_sems.at[1, p, r],
                       {"blk": plane * group + g})

    def turned(step):
        return lax.rem(step + member // per_block + 1, q_blocks)

    def o_copy(step):
        span = pl.ds(pl.multiple_of(turned(step) * q_block, q_block), q_block)
        return pltpu.make_async_copy(o_ref.at[:, span], o_out.at[:, span], leave_sems.at[4, step])

    def block(step, carry):
        which = turned(step)
        span = pl.ds(pl.multiple_of(which * q_block, q_block), q_block)
        done, tops = [], []
        for h in range(heads):
            top = jnp.full((8, q_block), MASKED, F32)
            for t in range(length_all // key_tile):
                keys = slice(t * key_tile, (t + 1) * key_tile)
                part = mm_nt(k_ref[h, keys, :], q_ref[h, span, :])
                scores[h, keys, :] = part
                top = jnp.maximum(top, jnp.max(part.reshape(key_tile // 8, 8, q_block), axis=0))
            tops.append(jnp.max(top, axis=0, keepdims=True))
        for h in range(heads):
            top = tops[h]
            mixed = jnp.zeros((LANES, q_block), F32)
            for t in range(length_all // key_tile):
                keys = slice(t * key_tile, (t + 1) * key_tile)
                weights = jnp.exp(scores[h, keys, :] - top).astype(BF16)
                mixed = mixed + mm(vt[h, :, keys], weights)
            denom = mixed[HD:HD + 1, :]
            scaled = mixed * (1.0 / denom)
            sub = lax.broadcasted_iota(jnp.int32, scaled.shape, 0)
            o_rows = jnp.where(sub == HD, top + jnp.log(denom), scaled).T
            o_ref[h, span, :] = o_rows
            done.append(o_rows[:, :HD].astype(BF16))
        o_copy(step).start()
        attended = jnp.concatenate(done, axis=1)
        for u in range(per_block):
            d = which * per_block + u
            p, g = d // group, lax.rem(d, group)
            att[p, g] = attended[u * rows:(u + 1) * rows, :]

            @pl.when(g != member)
            def _():
                att_copy(p, g, member, lax.rem(g + group - member, group)).start()

            @pl.when(g == member)
            def _():
                att_in[member, p] = attended[u * rows:(u + 1) * rows, :]
        return carry

    lax.fori_loop(0, q_blocks, block, 0)
    for k in range(1, slots):
        source = lax.rem(plane + slots - k, slots)
        send_to(cot_low.at[plane], cot_out.at[source], cot_sems.at[0, k], cot_sems.at[1, k],
                {"blk": source * group + member}).wait_recv()
    for p in range(slots):
        for r in range(1, group):
            att_copy(p, member, lax.rem(member + group - r, group), r).wait_recv()
    for p in range(slots):
        for r in range(1, group):
            att_copy(p, members[r - 1], member, r).wait_send()
    for copy in pending:
        copy.wait_send()
    for copy in leaving + [o_copy(step) for step in range(q_blocks)]:
        copy.wait()


def first(tokens, cotangent, weights, biases, lengths, blocks, collective_id, q_block=512, key_tile=256):
    slots, rows, width = tokens.shape
    group = blocks // slots
    length_all, total = blocks * rows, width // group
    heads = total // HD
    per_head = jax.ShapeDtypeStruct((heads, length_all, LANES), BF16)
    dma, vmem = pltpu.SemaphoreType.DMA, pltpu.VMEM
    return pl.pallas_call(
        functools.partial(first_kernel, slots, group, q_block, key_tile),
        out_shape=(
            jax.ShapeDtypeStruct((blocks, rows, width), BF16),
            jax.ShapeDtypeStruct((slots, rows, width), BF16),
            jax.ShapeDtypeStruct((group, slots, rows, total), BF16),
            per_head, per_head, per_head,
            jax.ShapeDtypeStruct((heads, length_all, LANES), F32),
        ),
        in_specs=[VMEM] * 7 + [SMEM],
        out_specs=(ANY, VMEM, VMEM) + (ANY,) * 4,
        scratch_shapes=[
            vmem((blocks, rows, width), BF16),
            vmem(per_head.shape, BF16),
            vmem(per_head.shape, BF16),
            vmem(per_head.shape, BF16),
            vmem(per_head.shape, F32),
            vmem((slots, rows, width), BF16),
            vmem((slots, rows, width), BF16),
            vmem((heads, LANES, length_all), BF16),
            vmem((width, 3 * total), BF16),
            vmem((slots, group, rows, total), BF16),
            vmem((heads, length_all, q_block), F32),
            dma((slots,)), dma((slots,)), dma((slots, group)), dma((slots, group)), dma((2, slots)),
            dma((2, slots, group)),
            dma((5, max(slots, length_all // q_block))),
        ],
        compiler_params=params(collective_id),
    )(tokens, cotangent, *weights, *biases, lengths)


def three(value):
    high = value.astype(BF16).astype(F32)
    mid = (value - high).astype(BF16).astype(F32)
    return high, mid, value - high - mid


def row_tile(rows):
    return next(t for t in (256, 128, 96, 64, 48, 32, 16) if rows % t == 0)


def over_rows(rows, body):
    step = row_tile(rows)

    def run(i, carry):
        body(i * step, step)
        return carry

    lax.fori_loop(0, rows // step, run, 0)


def rows_at(offset, i, step):
    return pl.ds(pl.multiple_of(offset + i, 16), step)


def rows_of(offset, n):
    return pl.ds(pl.multiple_of(offset, 16), n)


def bits_of(size):
    return [1 << i for i in range(size.bit_length() - 1)]


class Place:
    def __init__(self, docs, blocks, group):
        self.docs, self.blocks, self.group = docs, blocks, group
        self.planes = blocks // group
        self.me, self.doc = lax.axis_index("blk"), lax.axis_index("docs")
        self.plane, self.member = self.me // group, lax.rem(self.me, group)

    def pair(self, axis, bit):
        mine = self.me if axis == "blk" else self.doc
        on = lax.rem(mine // bit, 2)
        return {axis: mine + bit - 2 * bit * on}, on

    def member_peer(self, k):
        return lax.rem(self.member + k, self.group)

    def member_source(self, k):
        return lax.rem(self.member + self.group - k, self.group)

    def in_plane(self, member):
        return {"blk": self.plane * self.group + member}

    def in_line(self, plane):
        return {"blk": plane * self.group + self.member}

    def plane_peer(self, k):
        return lax.rem(self.plane + k, self.planes)

    def plane_source(self, k):
        return lax.rem(self.plane + self.planes - k, self.planes)


class Summer:
    def __init__(self, at, acc, sent, came, out, place, offset, rows, order, rest, sems, out_shift=0):
        self.at, self.acc, self.sent, self.came, self.out, self.sems = at, acc, sent, came, out, sems
        self.shift = out_shift
        self.stages = []
        for axis, bit in order:
            if axis == "planes":
                n = rows // at.planes
                self.stages.append(("planes", None, n, offset, offset + at.plane * n, place))
                offset, rows, place = offset + at.plane * n, n, place + (at.planes - 1) * n
                continue
            to, on = at.pair(axis, bit)
            n = rows // 2
            self.stages.append(("pair", to, n, offset + (1 - on) * n, offset + on * n, place))
            offset, rows, place = offset + on * n, n, place + n
        for axis, bit in rest:
            self.stages.append(("full", at.pair(axis, bit)[0], rows, offset, offset, place))
            place += rows
        self.count = len(self.stages)
        self.back = [s for s in range(self.count) if self.stages[s][0] != "full"][::-1]

    @staticmethod
    def placed(rows, order, planes, rest):
        total = 0
        for axis, _ in order:
            share = rows // planes if axis == "planes" else rows // 2
            total, rows = total + rows - share, share
        return total + rest * rows

    def copies(self, s, back=False, receive=False):
        kind, to, n, give, keep, place = self.stages[s]
        at, out = self.at, self.out
        w = 1 if back else 0
        if kind == "planes":
            found = []
            for k in range(1, at.planes):
                if back:
                    which = at.plane_source(k) if receive else at.plane
                    span = rows_of(give + which * n + self.shift, n)
                    src, dst = out.at[span], out.at[span]
                else:
                    src, dst = (ref.at[rows_of(place + (k - 1) * n, n)] for ref in (self.sent, self.came))
                to = at.in_line(at.plane_peer(k))
                found.append(send_to(src, dst, self.sems.at[w, 0, s, k], self.sems.at[w, 1, s, k], to))
            return found
        if back:
            span = rows_of((give if receive else keep) + self.shift, n)
            src, dst = out.at[span], out.at[span]
        else:
            src, dst = self.sent.at[rows_of(place, n)], self.came.at[rows_of(place, n)]
        return [send_to(src, dst, self.sems.at[w, 0, s, 0], self.sems.at[w, 1, s, 0], to)]

    def pack(self, give, place, n):
        def run(i, step):
            self.sent[rows_at(place, i, step), :] = self.acc[rows_at(give, i, step), :].astype(BF16)
        over_rows(n, run)

    def start(self, s):
        kind, to, n, give, keep, place = self.stages[s]
        if kind == "planes":
            for k in range(1, self.at.planes):
                self.pack(give + self.at.plane_peer(k) * n, place + (k - 1) * n, n)
        else:
            self.pack(give, place, n)
        for copy in self.copies(s):
            copy.start()

    def finish(self, s):
        kind, to, n, give, keep, place = self.stages[s]
        for copy in self.copies(s):
            copy.wait_recv()
        parts = self.at.planes - 1 if kind == "planes" else 1
        last = s == self.count - 1

        def run(i, step):
            total = self.acc[rows_at(keep, i, step), :]
            if kind == "full":
                total = total.astype(BF16).astype(F32)
            for k in range(parts):
                total = total + self.came[rows_at(place + k * n, i, step), :].astype(F32)
            if last:
                self.out[rows_at(keep + self.shift, i, step), :] = total.astype(BF16)
            else:
                self.acc[rows_at(keep, i, step), :] = total
        over_rows(n, run)

    def start_back(self, s):
        for copy in self.copies(s, back=True):
            copy.start()

    def finish_back(self, s):
        for copy in self.copies(s, back=True, receive=True):
            copy.wait_recv()

    def events(self, back):
        def first():
            self.start(0)

        def inward(s):
            self.finish(s)
            if s + 1 < self.count:
                self.start(s + 1)
            elif back:
                self.start_back(back[0])

        def outward(d):
            self.finish_back(back[d])
            if d + 1 < len(back):
                self.start_back(back[d + 1])

        return ([first] + [functools.partial(inward, s) for s in range(self.count)]
                + [functools.partial(outward, d) for d in range(len(back))])

    def drain(self, back):
        for s in range(self.count):
            for copy in self.copies(s):
                copy.wait_send()
        for s in back:
            for copy in self.copies(s, back=True):
                copy.wait_send()


def row_mean(value):
    return jnp.mean(value, axis=1, keepdims=True)


def col_sum(value):
    return jnp.sum(value, axis=0, keepdims=True)


def main_kernel(docs, blocks, group, cuts, k_block, q_tile,
                att_in, cot_ref, len_ref, wo_ref, ob_ref, g1_ref, s1_ref, up_hbm, ub_ref, down_hbm,
                db_ref, g2_ref, s2_ref, wq_hbm, wk_hbm, wv_hbm, q_hbm, k_hbm, v_hbm, o_hbm, tok_hbm,
                out_in, grad_in, sum_ref, qkv_ref, small_out,
                wq_ref, wk_ref, wv_ref, q_ref, k_ref, v_ref, o_ref, tok_ref, att, hid_t, gz, away, kv_in, gq_in, g_att, g_in, qx, gx, qt, gt, kv_send, gq_send,
                acc, sent, came, dwt, sent_w, came_w, bias, small_sent, small_came,
                g_sems, kv_sems, gq_sems, sum_sems, w_sems, small_sems, wide_sems, core_sems, load_sems,
                out_sems, grad_sems, enter_sems):
    at = Place(docs, blocks, group)
    me, member, plane, planes = at.me, at.member, at.plane, at.planes
    _, rows, width = tok_ref.shape
    count = planes * rows
    cols = width // group
    inner_width = up_hbm.shape[1]
    heads, length_all, _ = q_ref.shape
    parts = inner_width // width
    doc_bits = bits_of(docs)

    loads = [pltpu.make_async_copy(up_hbm.at[:, c * width:(c + 1) * width],
                                   sent.at[inner_width + c * width:inner_width + (c + 1) * width], load_sems.at[c])
             for c in range(parts)]
    loads.append(pltpu.make_async_copy(down_hbm, sent.at[:inner_width], load_sems.at[parts]))
    enter = [pltpu.make_async_copy(src, dst, enter_sems.at[i]) for i, (src, dst) in enumerate((
        (tok_hbm, tok_ref), (q_hbm, q_ref), (o_hbm, o_ref), (k_hbm, k_ref), (v_hbm, v_ref),
        (wq_hbm, wq_ref), (wk_hbm, wk_ref), (wv_hbm, wv_ref)))]
    for load in enter[:1] + loads + enter[1:]:
        load.start()

    def up_part(c):
        return sent[inner_width + c * width:inner_width + (c + 1) * width, :]

    greet([at.in_plane(at.member_peer(k)) for k in range(1, group)]
          + [at.in_line(at.plane_peer(k)) for k in range(1, planes)]
          + [at.pair("docs", bit)[0] for bit in doc_bits])

    rest = [("docs", bit) for bit in doc_bits[1:]]
    sums, place = [], 0
    for c, (offset, size, order) in enumerate(cuts):
        sums.append(Summer(at, acc, sent, came, sum_ref, place, offset, size, order, rest, sum_sems.at[c]))
        place = place + Summer.placed(size, order, planes, len(rest))
    chains = [s.events(s.back) for s in sums]
    at_event = [0] * len(cuts)

    def upcoming(numbers):
        found = []
        for c in numbers:
            if at_event[c] < len(chains[c]):
                found.append(chains[c][at_event[c]])
                at_event[c] += 1
        return found

    def advance(numbers):
        for event in upcoming(numbers):
            event()

    enter[0].wait()
    flat = jnp.concatenate([tok_ref[p * group + member].astype(F32) for p in range(planes)], axis=0)
    for p in range(planes):
        for g in range(group):
            att[p * rows:(p + 1) * rows, g * cols:(g + 1) * cols] = att_in[g, p]
    up_bias = row(ub_ref)
    gain1, gain2 = row(g1_ref), row(g2_ref)
    summed = flat + mm(att[...], wo_ref[...]) + row(ob_ref)
    centred = summed - row_mean(summed)
    rstd1 = lax.rsqrt(row_mean(centred * centred) + EPS)
    xhat1 = centred * rstd1
    hidden = xhat1 * gain1 + row(s1_ref)
    hidden_low = hidden.astype(BF16)
    hid_t[...] = hidden_low.T
    for load in loads:
        load.wait()
    ffn = jnp.zeros((count, width), F32)
    for c in range(parts):
        span = slice(c * width, (c + 1) * width)
        inner = mm(hidden_low, up_part(c)) + up_bias[:, span]
        square = inner * inner
        slope_in = 0.7978845608 * (1.0 + (3 * 0.044715) * square)
        tanh = jnp.tanh(inner * (0.7978845608 * (1.0 + 0.044715 * square)))
        half = 0.5 * (1.0 + tanh)
        acc[c * count:(c + 1) * count, :] = half + (0.5 * inner) * ((1.0 - tanh * tanh) * slope_in)
        low = (inner * half).astype(BF16)
        sum_ref[c * count:(c + 1) * count, :] = low
        ffn = ffn + mm(low, sent[span, :])
    summed = flat + hidden + ffn + row(db_ref)
    centred = summed - row_mean(summed)
    rstd2 = lax.rsqrt(row_mean(centred * centred) + EPS)
    xhat2 = centred * rstd2
    away[...] = (xhat2 * gain2 + row(s2_ref)).astype(BF16).reshape(planes, rows, width)

    def line_copies(dst, sems, receive=False):
        return [send_to(away.at[at.plane_peer(k)], dst.at[at.plane_source(k) if receive else plane],
                        sems.at[0, k], sems.at[1, k], at.in_line(at.plane_peer(k))) for k in range(1, planes)]

    for copy in line_copies(out_in, out_sems):
        copy.start()
    out_in[plane] = away[plane]
    lane_r = lax.broadcasted_iota(jnp.int32, (rows, width), 0)
    g_out = jnp.concatenate(
        [jnp.where((p * group + member) * rows + lane_r < len_ref[plane], cot_ref[p].astype(F32), 0.0)
         for p in range(planes)], axis=0)
    small_sent[0] = jnp.zeros(small_sent.shape[1:], F32)
    small_sent[0, 0:1, :] = col_sum(g_out * xhat2)
    small_sent[0, 1:2, :] = col_sum(g_out)
    scaled = g_out * gain2
    g_z2 = rstd2 * (scaled - row_mean(scaled) - xhat2 * row_mean(scaled * xhat2))
    g_ffn = g_z2.astype(BF16)
    small_sent[0, 2:3, :] = col_sum(g_ffn.astype(F32))
    g_hidden = g_z2
    for c in range(parts):
        span = slice(c * width, (c + 1) * width)
        g_inner = (mm_nt(g_ffn, sent[span, :]) * acc[c * count:(c + 1) * count, :]).astype(BF16)
        sum_ref[inner_width + c * count:inner_width + (c + 1) * count, :] = g_inner
        g_hidden = g_hidden + mm_nt(g_inner, up_part(c))
    scaled = g_hidden * gain1
    g_z1 = rstd1 * (scaled - row_mean(scaled) - xhat1 * row_mean(scaled * xhat1))
    g_branch = g_z1.astype(BF16)
    gz[...] = g_z1 + g_z2
    g_low = mm_nt(g_branch, wo_ref[...]).astype(BF16)
    for p in range(planes):
        for g in range(group):
            g_att[g, p] = g_low[p * rows:(p + 1) * rows, g * cols:(g + 1) * cols]

    def g_copy(k, receive=False):
        slot = at.member_source(k) if receive else member
        return send_to(g_att.at[at.member_peer(k)], g_in.at[:, slot], g_sems.at[0, k], g_sems.at[1, k],
                       at.in_plane(at.member_peer(k)))

    for k in range(1, group):
        g_copy(k).start()
    for p in range(planes):
        g_in[p, member] = g_att[member, p]

    for c in range(parts):
        span = slice(c * width, (c + 1) * width)
        acc[span, :] = mm_tn(sum_ref[c * count:(c + 1) * count, :], g_ffn)
    advance(POINTS[0])
    for c in range(parts):
        g_inner = sum_ref[inner_width + c * count:inner_width + (c + 1) * count, :]
        small_sent[0, 6 + c:7 + c, :] = col_sum(g_inner.astype(F32))
        acc[inner_width + c * width:inner_width + (c + 1) * width, :] = mm(hid_t[...], g_inner)
    acc[2 * inner_width:2 * inner_width + width, :] = mm_tn(att[...], g_branch)
    if acc.shape[0] > 2 * inner_width + width:
        acc[2 * inner_width + width:, :] = jnp.zeros((acc.shape[0] - 2 * inner_width - width, width), F32)
    advance(POINTS[1])
    small_sent[0, 3:4, :] = col_sum(g_hidden * xhat1)
    small_sent[0, 4:5, :] = col_sum(g_hidden)
    small_sent[0, 5:6, :] = col_sum(g_branch.astype(F32))
    chunk = group * rows
    lane = lax.broadcasted_iota(jnp.int32, (chunk, LANES), 1)

    for load in enter[1:]:
        load.wait()

    def prepare_q(step, carry):
        span = pl.ds(pl.multiple_of(step * chunk, chunk), chunk)
        for h in range(heads):
            q_rows = q_ref[h, span, :].astype(F32)
            ext = q_rows
            for i, value in enumerate(three(-o_ref[h, span, HD:HD + 1])):
                ext = jnp.where(lane == HD + 1 + i, value, ext)
            qx[h, span, :] = ext.astype(BF16)
            qt[h, :, span] = q_rows[:, :HD].T.astype(BF16)
        return carry

    lax.fori_loop(0, planes, prepare_q, 0)
    advance(POINTS[2])
    for k in range(1, group):
        g_copy(k, True).wait_recv()

    def prepare_g(step, carry):
        span = pl.ds(pl.multiple_of(step * chunk, chunk), chunk)
        g_block = g_in[step].reshape(chunk, cols)
        for h in range(heads):
            g_rows = g_block[:, h * HD:(h + 1) * HD].astype(F32)
            g_rows = jnp.concatenate([g_rows, jnp.zeros_like(g_rows)], axis=1)
            delta = jnp.sum(g_rows * o_ref[h, span, :], axis=1, keepdims=True)
            ext = g_rows
            for i, value in enumerate(three(-delta)):
                ext = jnp.where(lane == HD + i, value, ext)
            gx[h, span, :] = ext.astype(BF16)
            gt[h, :, span] = g_rows[:, :HD].T.astype(BF16)
        return carry

    lax.fori_loop(0, planes, prepare_g, 0)
    advance(POINTS[3])

    gq_acc = o_ref.at[0]
    k_blocks = length_all // k_block
    per_block = k_block // rows
    ones = jnp.ones((8, k_block), BF16)
    dwt[...] = jnp.zeros_like(dwt)
    bias[...] = jnp.zeros_like(bias)

    def kv_copy(h, p, g, slot, r):
        return send_to(kv_send.at[h, p, g], kv_in.at[slot, h, p], kv_sems.at[0, h, p, r], kv_sems.at[1, h, p, r],
                       at.in_plane(g))

    def gq_copy(h, r, receive=False):
        slot = at.member_source(r) if receive else member
        return send_to(gq_send.at[h, :, at.member_peer(r)], gq_in.at[slot, h], gq_sems.at[0, h, r],
                       gq_sems.at[1, h, r], at.in_plane(at.member_peer(r)))

    total_steps = heads * k_blocks
    timed = [(t, event) for t in range(min(total_steps, len(AT_BLOCK))) for event in upcoming(AT_BLOCK[t])]

    def block(step, carry):
        h, i = step // k_blocks, lax.rem(step, k_blocks)
        which = lax.rem(i + member // per_block + 1, k_blocks)
        span = pl.ds(pl.multiple_of(which * k_block, k_block), k_block)
        k_rows, v_rows = k_ref[h, span, :], v_ref[h, span, :]

        @pl.when(i == 0)
        def _():
            gq_acc[...] = jnp.zeros_like(gq_acc)

        gk = jnp.zeros((HD, k_block), F32)
        gv = jnp.zeros((HD, k_block), F32)
        tiles = [slice(t, t + q_tile) for t in range(0, length_all, q_tile)]

        def products(tile):
            return mm_nt(qx[h, tile, :], k_rows), mm_nt(gx[h, tile, :], v_rows)

        ahead = products(tiles[0])
        for tile, later in zip(tiles, tiles[1:] + [None]):
            scores, centred = ahead
            ahead = products(later) if later else None
            weights = jnp.exp(scores)
            g_scores = (weights * centred).astype(BF16)
            gv = gv + mm(gt[h, :, tile], weights.astype(BF16))
            gk = gk + mm(qt[h, :, tile], g_scores)
            gq_acc[tile, :] += mm(g_scores, k_rows)
        kv = jnp.concatenate([gk, gv], axis=0).astype(BF16)
        tok_rows = tok_ref[pl.ds(which * per_block, per_block)].reshape(k_block, width)
        dwt[pl.ds(pl.multiple_of(h * 2 * HD, 2 * HD), 2 * HD), :] += mm(kv, tok_rows)
        bias[h, 0] += mm_nt(ones, kv[HD:])
        for u in range(per_block):
            d = which * per_block + u
            p, g = d // group, lax.rem(d, group)
            kv_send[h, p, g] = kv[:, u * rows:(u + 1) * rows]

            @pl.when(g != member)
            def _():
                kv_copy(h, p, g, member, lax.rem(g + group - member, group)).start()

            @pl.when(g == member)
            def _():
                kv_in[member, h, p] = kv[:, u * rows:(u + 1) * rows]

        @pl.when(i == k_blocks - 1)
        def _():
            for n in range(blocks):
                gq_send[h, n // group, n % group] = (
                    gq_acc[n * rows:(n + 1) * rows, :HD] * (HD ** -0.5)).T.astype(BF16)
            for r in range(1, group):
                gq_copy(h, r).start()
            for p in range(planes):
                gq_in[member, h, p] = gq_send[h, p, member]

        for t, event in timed:
            pl.when(step == t)(event)
        return carry

    lax.fori_loop(0, total_steps, block, 0)

    q_base = heads * 2 * HD
    for h in range(heads):
        part = jnp.zeros((HD, width), F32)
        q_bias = jnp.zeros((8, HD), F32)
        for n in range(blocks):
            low = gq_send[h, n // group, n % group]
            part = part + mm(low, tok_ref[n])
            q_bias = q_bias + mm_nt(jnp.ones((8, rows), BF16), low)
        dwt[q_base + h * HD:q_base + (h + 1) * HD, :] = part
        bias[h, 1] = q_bias
    half = dwt.shape[0] // 2
    my_core = lax.rem(at.doc, 2)
    w_sum = Summer(at, dwt, sent_w, came_w, qkv_ref, 0, 0, 2 * half, W_ORDER, rest, w_sems,
                   out_shift=my_core * (half * group - half) + member * half)
    w_line = next(s for s in w_sum.back if w_sum.stages[s][0] == "planes")
    share = half // planes
    w_chain = w_sum.events([])
    lane_w = lax.broadcasted_iota(jnp.int32, (8, width), 1)
    sub = lax.broadcasted_iota(jnp.int32, (8, width), 0)
    wide = [jnp.concatenate([bias[h, i] for h in range(heads)] * group, axis=1) for i in range(2)]
    small_sent[0, 16:24, :] = jnp.where(
        (lane_w // cols) == member, jnp.where(sub == 0, wide[1], jnp.where(sub == 1, wide[0], 0.0)), 0.0)
    small_order = [("docs", 1)] + [("blk", bit) for bit in bits_of(group)]

    def small_copy(s):
        return send_to(small_sent.at[s], small_came.at[s], small_sems.at[0, s], small_sems.at[1, s],
                       at.pair(*small_order[s])[0])

    small_last = len(small_order)

    def small_line(k, receive=False):
        slot = small_last + k
        return send_to(small_sent.at[small_last], small_came.at[slot], small_sems.at[0, slot],
                       small_sems.at[1, slot], at.in_line(at.plane_peer(k)))

    def small_rest(i):
        slot = small_last + planes + i
        return send_to(small_sent.at[small_last + 1 + i], small_came.at[slot], small_sems.at[0, slot],
                       small_sems.at[1, slot], at.pair(*rest[i])[0])

    def small_step(s):
        small_copy(s).wait_recv()
        small_sent[s + 1] = small_sent[s] + small_came[s]
        if s + 1 < small_last:
            small_copy(s + 1).start()
        else:
            for k in range(1, planes):
                small_line(k).start()

    def small_end():
        for k in range(1, planes):
            small_line(k).wait_recv()
        total = jnp.zeros(small_sent.shape[1:], F32)
        for p in range(planes):
            value = small_sent[small_last]
            for k in range(1, planes):
                value = jnp.where(at.plane_source(k) == p, small_came[small_last + k], value)
            total = total + value
        for i in range(len(rest)):
            small_sent[small_last + 1 + i] = total
            small_rest(i).start()
            small_rest(i).wait_recv()
            total = total + small_came[small_last + planes + i]
        small_out[...] = total

    def slab(core, m, p=0, n=half):
        return qkv_ref.at[rows_of(core * half * group + m * half + p * share, n)]

    def wide_copy(k, j, m):
        piece = slab(my_core, m, at.plane_source(j), share)
        return send_to(piece, piece, wide_sems.at[0, k, j], wide_sems.at[1, k, j], at.in_plane(at.member_peer(k)))

    def core_copy(k, core):
        piece = slab(core, at.member_source(k))
        return send_to(piece, piece, core_sems.at[0, k], core_sems.at[1, k], at.pair("docs", 1)[0])

    def w_out():
        w_chain[-1]()
        w_sum.start_back(w_line)
        for k in range(1, group):
            wide_copy(k, 0, member).start()

    def w_forward():
        for j, copy in enumerate(w_sum.copies(w_line, back=True, receive=True)):
            copy.wait_recv()
            for k in range(1, group):
                wide_copy(k, j + 1, member).start()
        core_copy(0, my_core).start()

    def w_slabs():
        for k in range(1, group):
            for j in range(planes):
                wide_copy(k, j, at.member_source(k)).wait_recv()
            core_copy(k, my_core).start()

    def gather_part(which):
        for p in range(planes):
            for g in range(group):
                for h in range(heads):
                    low = gq_in[g, h, p] if which == 0 else kv_in[g, h, p, (which - 1) * HD:which * HD, :]
                    hid_t[g * cols + h * HD:g * cols + (h + 1) * HD, p * rows:(p + 1) * rows] = low
        return hid_t[...].T

    def key_value_rows():
        for h in range(heads):
            for p in range(planes):
                for r in range(1, group):
                    kv_copy(h, p, member, at.member_source(r), r).wait_recv()
        gz[...] += mm_nt(gather_part(1), wk_ref[...])
        gz[...] += mm_nt(gather_part(2), wv_ref[...])

    def query_rows():
        for h in range(heads):
            for r in range(1, group):
                gq_copy(h, r, True).wait_recv()
        total = gz[...] + mm_nt(gather_part(0), wq_ref[...])
        for copy in line_copies(out_in, out_sems, True):
            copy.wait_recv()
        for copy in line_copies(out_in, out_sems):
            copy.wait_send()
        away[...] = total.astype(BF16).reshape(planes, rows, width)
        for copy in line_copies(grad_in, grad_sems):
            copy.start()
        grad_in[plane] = away[plane]

    w_events = w_chain[:-1] + [w_out, w_forward, w_slabs]
    small_events = [small_copy(0).start] + [functools.partial(small_step, s) for s in range(small_last)] + [small_end]
    named = {"w": w_events, "g": [key_value_rows, query_rows], "s": small_events}
    for name in AFTER:
        if name in named:
            if named[name]:
                named[name].pop(0)()
        else:
            advance((name,))
    while any(named.values()) or any(at_event[c] < len(chains[c]) for c in range(len(cuts))):
        for work in named.values():
            if work:
                work.pop(0)()
        advance(range(len(cuts)))
    for k in range(group):
        core_copy(k, 1 - my_core).wait_recv()
    for copy in line_copies(grad_in, grad_sems, True):
        copy.wait_recv()
    for copy in line_copies(grad_in, grad_sems):
        copy.wait_send()
    for r in range(1, group):
        g_copy(r).wait_send()
        for h in range(heads):
            gq_copy(h, r).wait_send()
            for p in range(planes):
                kv_copy(h, p, at.member_peer(r), member, r).wait_send()
    for part in sums:
        part.drain(part.back)
    w_sum.drain([w_line])
    for k in range(group):
        core_copy(k, my_core).wait_send()
        for j in range(planes if k else 0):
            wide_copy(k, j, member).wait_send()
    for s in range(small_last):
        small_copy(s).wait_send()
    for k in range(1, planes):
        small_line(k).wait_send()
    for i in range(len(rest)):
        small_rest(i).wait_send()


def member_bits(group, name):
    bits = bits_of(group)
    return bits[:len(bits) // 2] if name == "x" else bits[len(bits) // 2:]


SUMS = ((2, ("yxz", "xyz")), (3, ("zxy", "yxz", "xyz")))
W_ORDER = [("docs", 1), ("planes", 0)]
POINTS = ((0,), (4, 0, 3, 4, 2,), (1, 3, 2, 0, 1, 4,), ())
AT_BLOCK = ((0,), (2, 3, 4, 1,), (2, 0,),
            (3, 4, 1, 2,), (), (2, 3,),
            (0, 1, 2, 4,), ())
AFTER = ("w", 1, 3, "s", "w", "s", 4, 0, "g", "w", "s", 2, 1, 3, "g", 0, "w", 1, 0, 4, "s", 3, 3, "w", "g",
         1, 2, 4, "s", "w",)


def main(docs, blocks, group, att_in, cotangent, lengths, weights, attention, tok_doc, collective_id,
         k_block=512, q_tile=256):
    q = attention[0]
    heads, length_all, _ = q.shape
    _, rows, width = tok_doc.shape
    planes = blocks // group
    count = planes * rows
    cols = heads * HD
    inner_width = weights[4].shape[1]
    features = -(-3 * cols // 128) * 128
    unit = 32 * blocks
    second = -(-(inner_width + width) // unit)
    cuts, offset = [], 0
    for (pieces, turns), units in zip(SUMS, (inner_width // unit, second)):
        pieces = min(pieces, units)
        for i in range(pieces):
            size = unit * (units // pieces + (1 if i >= pieces - units % pieces else 0))
            cuts.append((offset, size, [("docs", 1)] + [
                step for name in turns[i] for step in (
                    [("planes", 0)] if name == "z" else [("blk", bit) for bit in member_bits(group, name)])]))
            offset += size
    total = inner_width + second * unit
    members, rest = len(bits_of(group)), len(bits_of(docs)) - 1
    placed = sum(Summer.placed(size, order, planes, rest) for _, size, order in cuts)
    w_placed = Summer.placed(features, W_ORDER, planes, rest)
    stages = 2 + members + rest
    steps = 1 + members + planes + rest
    dma, vmem = pltpu.SemaphoreType.DMA, pltpu.VMEM
    return pl.pallas_call(
        functools.partial(main_kernel, docs, blocks, group, cuts, k_block, q_tile),
        out_shape=(
            jax.ShapeDtypeStruct((planes, rows, width), BF16),
            jax.ShapeDtypeStruct((planes, rows, width), BF16),
            jax.ShapeDtypeStruct((total, width), BF16),
            jax.ShapeDtypeStruct((features * group, width), BF16),
            jax.ShapeDtypeStruct((24, width), F32),
        ),
        in_specs=[VMEM] * 2 + [SMEM] + [VMEM] * 4 + [ANY, VMEM, ANY] + [VMEM] * 3 + [ANY] * 8,
        out_specs=(VMEM,) * 5,
        scratch_shapes=[
            *(vmem((width, width), BF16) for _ in range(3)),
            *(vmem(array.shape, array.dtype) for array in (*attention, tok_doc)),
            vmem((count, width), BF16),
            vmem((width, count), BF16),
            vmem((count, width), F32),
            vmem((planes, rows, width), BF16),
            vmem((group, heads, planes, 2 * HD, rows), BF16),
            vmem((group, heads, planes, HD, rows), BF16),
            vmem((group, planes, rows, cols), BF16),
            vmem((planes, group, rows, cols), BF16),
            vmem((heads, length_all, LANES), BF16),
            vmem((heads, length_all, LANES), BF16),
            vmem((heads, HD, length_all), BF16),
            vmem((heads, HD, length_all), BF16),
            vmem((heads, planes, group, 2 * HD, rows), BF16),
            vmem((heads, planes, group, HD, rows), BF16),
            vmem((total, width), F32),
            vmem((max(placed, 2 * inner_width), width), BF16),
            vmem((placed, width), BF16),
            vmem((features, width), F32),
            vmem((w_placed, width), BF16),
            vmem((w_placed, width), BF16),
            vmem((heads, 2, 8, HD), F32),
            vmem((steps, 24, width), F32),
            vmem((steps, 24, width), F32),
            dma((2, group)),
            dma((2, heads, planes, group)),
            dma((2, heads, group)),
            dma((len(cuts), 2, 2, stages, planes)),
            dma((2, 2, 2 + rest, planes)),
            dma((2, steps)),
            dma((2, group, planes)),
            dma((2, group)),
            dma((inner_width // width + 1,)),
            dma((2, planes)),
            dma((2, planes)),
            dma((8,)),
        ],
        compiler_params=params(collective_id),
    )(att_in, cotangent, lengths, *weights, *attention, tok_doc)


def last_kernel(group, heads, out_in, grad_in, sum_in, qkv_in, small_ref,
                out_ref, grad_ref, qw_ref, qb_ref, kw_ref, vw_ref, vb_ref, ow_ref, ob_ref, g1_ref, s1_ref,
                uw_ref, ub_ref, dw_ref, db_ref, g2_ref, s2_ref, rows_low, sums_low, qkv_low, stack, wide, come, go):
    width = ow_ref.shape[0]
    inner_width = uw_ref.shape[1]
    cols = width // group
    parts = inner_width // width
    spans = [slice(i * width, (i + 1) * width) for i in range(2 * parts + 1)]
    arrive = [pltpu.make_async_copy(sum_in.at[span], sums_low.at[span], come.at[i]) for i, span in enumerate(spans)]
    late = [pltpu.make_async_copy(qkv_in, qkv_low, come.at[len(spans)])]
    late += [pltpu.make_async_copy(src, rows_low.at[i], come.at[len(spans) + 1 + i])
             for i, src in enumerate((out_in, grad_in))]
    for copy in arrive + late:
        copy.start()
    targets = ([dw_ref.at[span] for span in spans[:parts]] + [uw_ref.at[:, span] for span in spans[:parts]] + [ow_ref])
    leaving = []

    def leave(slot, target):
        copy = pltpu.make_async_copy(wide.at[slot], target, go.at[slot])
        copy.start()
        leaving.append(copy)

    for i, span in enumerate(spans):
        arrive[i].wait()
        wide[i] = sums_low[span, :].astype(F32)
        leave(i, targets[i])
    for copy in late:
        copy.wait()
    slot = len(spans)
    planes, rows = out_ref.shape[0], out_ref.shape[1]
    for i, out in enumerate((out_ref, grad_ref)):
        for p in range(planes):
            wide[slot, p * rows:(p + 1) * rows, :] = rows_low[i, p].astype(F32)
            copy = pltpu.make_async_copy(wide.at[slot, p * rows:(p + 1) * rows], out.at[p], go.at[slot + 3 + i * planes + p])
            copy.start()
            leaving.append(copy)
        slot += 1
    half = qkv_low.shape[0] // group // 2
    unit = HD // 2
    for which, out in enumerate((qw_ref, kw_ref, vw_ref)):
        for g in range(group):
            for h in range(heads):
                first = heads * 2 * HD + h * HD if which == 0 else h * 2 * HD + (which - 1) * HD
                for u in range(2):
                    f = first + u * unit
                    at = f // half * half * group + g * half + f % half
                    to = g * cols + h * HD + u * unit
                    stack[to:to + unit, :] = qkv_low[at:at + unit, :]
        wide[slot] = stack[...].T.astype(F32)
        copy = pltpu.make_async_copy(wide.at[slot], out, go.at[len(spans) + which])
        copy.start()
        leaving.append(copy)
        slot += 1

    def vector(out, i):
        out[...] = small_ref[i:i + 1, :].reshape(out.shape)

    for i, out in ((16, qb_ref), (17, vb_ref), (0, g2_ref), (1, s2_ref), (2, db_ref), (3, g1_ref), (4, s1_ref),
                   (5, ob_ref)):
        vector(out, i)
    ub_ref[...] = jnp.concatenate([small_ref[6 + i:7 + i, :] for i in range(parts)], axis=1).reshape(ub_ref.shape)
    for copy in leaving:
        copy.wait()


def last(group, shape, inner_width, *arrays):
    slots, rows, width = shape
    heads = width // group // HD
    parts = 2 * inner_width // width + 1
    whole = jax.ShapeDtypeStruct(shape, F32)
    square = jax.ShapeDtypeStruct((width, width), F32)
    vector = jax.ShapeDtypeStruct((width,), F32)
    dma, vmem = pltpu.SemaphoreType.DMA, pltpu.VMEM
    shapes = (whole, whole, square, vector, square, square, vector, square, vector, vector, vector,
              jax.ShapeDtypeStruct((width, inner_width), F32), jax.ShapeDtypeStruct((inner_width,), F32),
              jax.ShapeDtypeStruct((inner_width, width), F32), vector, vector, vector)
    return pl.pallas_call(
        functools.partial(last_kernel, group, heads),
        out_shape=shapes,
        in_specs=[ANY] * 4 + [VMEM],
        out_specs=tuple(VMEM if len(shape.shape) == 1 else ANY for shape in shapes),
        scratch_shapes=[
            vmem((2, slots, rows, width), BF16),
            vmem((parts * width, width), BF16),
            vmem(arrays[3].shape, BF16),
            vmem((width, width), BF16),
            vmem((parts + 5, max(width, slots * rows), width), F32),
            dma((parts + 3,)),
            dma((parts + 5 + 2 * slots,)),
        ],
        compiler_params=params(),
    )(*arrays)


def device_program(docs, blocks, tokens, query_weight, query_bias, key_weight, value_weight, value_bias,
                   out_weight, out_bias, first_gain, first_shift, up_weight, up_bias, down_weight,
                   down_bias, second_gain, second_shift, cotangent, lengths):
    slots, rows, width = tokens.shape
    inner_width = up_weight.shape[1]
    group = blocks // slots
    projections = (query_weight, key_weight, value_weight)
    tok_doc, cot, att_in, q, k, v, o = first(tokens, cotangent, projections, (query_bias, value_bias), lengths,
                                             blocks, 0)
    parts = main(
        docs, blocks, group, att_in, cot, lengths,
        (out_weight, out_bias, first_gain, first_shift, up_weight, up_bias, down_weight, down_bias,
         second_gain, second_shift, *projections), (q, k, v, o), tok_doc, 1)
    return last(group, tokens.shape, inner_width, *parts)


def solution(mesh):
    split = P("docs", "blk", None)
    return jax.shard_map(
        functools.partial(device_program, mesh.shape["docs"], mesh.shape["blk"]),
        mesh=mesh,
        in_specs=(split,) + (P(),) * 15 + (split, P("docs")),
        out_specs=(split, split) + (P(),) * 15,
        check_vma=False,
    )
```

```python
import functools

import jax
import jax.numpy as jnp
from jax import lax
from jax.experimental import pallas as pl
from jax.experimental.pallas import tpu as pltpu
from jax.sharding import PartitionSpec as P

HD = 64
LANES = 128
EPS = 1e-05
MASKED = -1e30
F32 = jnp.float32
BF16 = jnp.bfloat16
VMEM = pl.BlockSpec(memory_space=pltpu.VMEM)
ANY = pl.BlockSpec(memory_space=pl.ANY)
SMEM = pl.BlockSpec(memory_space=pltpu.SMEM)
MESH = pl.DeviceIdType.MESH
VMEM_LIMIT = 63 * 1024 * 1024


def mm(left, right):
    return jnp.dot(left, right, preferred_element_type=F32)


def mm_nt(left, right):
    return lax.dot_general(left, right, (((1,), (1,)), ((), ())), preferred_element_type=F32)


def mm_tn(left, right):
    return lax.dot_general(left, right, (((0,), (0,)), ((), ())), preferred_element_type=F32)


def params(collective_id=None):
    if collective_id is None:
        return pltpu.CompilerParams(vmem_limit_bytes=VMEM_LIMIT)
    return pltpu.CompilerParams(
        vmem_limit_bytes=VMEM_LIMIT, collective_id=collective_id, has_side_effects=True
    )


def greet(peers):
    barrier = pltpu.get_barrier_semaphore()
    for peer in peers:
        pl.semaphore_signal(barrier, inc=1, device_id=peer, device_id_type=MESH)
    pl.semaphore_wait(barrier, len(peers))


def send_to(src, dst, send_sem, recv_sem, peer):
    return pltpu.make_async_remote_copy(
        src_ref=src, dst_ref=dst, send_sem=send_sem, recv_sem=recv_sem,
        device_id=peer, device_id_type=MESH,
    )


def row(ref):
    return ref[...].astype(F32).reshape(1, ref.shape[0])


def own_columns(ref, member, cols):
    if cols % LANES == 0:
        return ref[:, pl.ds(pl.multiple_of(member * cols, LANES), cols)]
    per = LANES // cols
    both = ref[:, pl.ds(pl.multiple_of(member // per * LANES, LANES), LANES)].astype(F32)
    return sum(jnp.where(lax.rem(member, per) == i, both[:, i * cols:(i + 1) * cols], 0.0)
               for i in range(per)).astype(BF16)


def own_entries(ref, member, cols):
    values = row(ref)
    return sum(jnp.where(member == i, values[:, i * cols:(i + 1) * cols], 0.0)
               for i in range(ref.shape[0] // cols))


def first_kernel(slots, group, q_block, key_tile, tok_in, cot_in, wq_ref, wk_ref, wv_ref, qb_ref, vb_ref, len_ref,
                 tok_out, cot_out, att_in, q_out, k_out, v_out, o_out,
                 tok_ref, q_ref, k_ref, v_ref, o_ref, low, cot_low, vt, w_ref, att, scores, send_a, recv_a, send_b, recv_b, cot_sems, att_sems, leave_sems):
    me = lax.axis_index("blk")
    plane, member = me // group, lax.rem(me, group)
    blocks, rows, width = tok_ref.shape
    length_all, total = blocks * rows, width // group
    heads = total // HD
    planes = [lax.rem(plane + k, slots) for k in range(1, slots)]
    members = [lax.rem(member + k, group) for k in range(1, group)]
    greet([{"blk": p * group + member} for p in planes]
          + [{"blk": plane * group + m} for m in members])

    low[...] = tok_in[...].astype(BF16)
    pending = []
    for k in range(1, slots):
        target = planes[k - 1]
        copy = send_to(low.at[target], tok_ref.at[me], send_a.at[k], recv_a.at[k],
                       {"blk": target * group + member})
        copy.start()
        pending.append(copy)
    tok_ref[me] = low[plane]

    def spread(k):
        block = lax.rem(plane + slots - k, slots) * group + member
        if k > 0:
            send_to(low.at[plane], tok_ref.at[block], send_a.at[k], recv_a.at[k],
                    {"blk": block}).wait_recv()
        for j in range(1, group):
            copy = send_to(tok_ref.at[block], tok_ref.at[block], send_b.at[k, j], recv_b.at[k, j],
                           {"blk": plane * group + members[j - 1]})
            copy.start()
            pending.append(copy)

    spread(0)
    cot_low[...] = cot_in[...].astype(BF16)
    for i, ref in enumerate((wq_ref, wk_ref, wv_ref)):
        w_ref[:, i * total:(i + 1) * total] = own_columns(ref, member, total)
    bias = jnp.concatenate(
        [own_entries(qb_ref, member, total), jnp.zeros((1, total), F32),
         own_entries(vb_ref, member, total)], axis=1)
    doc_len = len_ref[plane]
    chunk = group * rows

    def project(k):
        source = lax.rem(plane + slots - k, slots)
        for j in range(1, group):
            block = source * group + lax.rem(member + group - j, group)
            send_to(tok_ref.at[block], tok_ref.at[block], send_b.at[k, j], recv_b.at[k, j],
                    {"blk": plane * group + members[j - 1]}).wait_recv()
        span = pl.ds(pl.multiple_of(source * chunk, chunk), chunk)
        qkv = mm(tok_ref[pl.ds(source * group, group)].reshape(chunk, width), w_ref[...]) + bias
        lane = lax.broadcasted_iota(jnp.int32, (chunk, LANES), 1)
        position = source * chunk + lax.broadcasted_iota(jnp.int32, (chunk, LANES), 0)
        mask = jnp.where(position < doc_len, 0.0, MASKED)
        for h in range(heads):
            def part(which):
                cols = qkv[:, which * total + h * HD:which * total + (h + 1) * HD]
                return jnp.concatenate([cols, jnp.zeros_like(cols)], axis=1)
            q_ref[h, span, :] = jnp.where(
                lane == HD, 1.0, part(0).astype(BF16).astype(F32) * (HD ** -0.5)).astype(BF16)
            k_ref[h, span, :] = jnp.where(
                lane == HD, mask, jnp.where((lane > HD) & (lane < HD + 4), 1.0, part(1))).astype(BF16)
            v_rows = jnp.where((lane >= HD) & (lane < HD + 4), 1.0, part(2)).astype(BF16)
            v_ref[h, span, :] = v_rows
            vt[h, :, span] = v_rows.T
        members_of = pl.ds(source * group, group)
        leave(tok_ref.at[members_of], tok_out.at[members_of], leave_sems.at[0, k])
        for i, (ref, out) in enumerate(((q_ref, q_out), (k_ref, k_out), (v_ref, v_out))):
            leave(ref.at[:, span], out.at[:, span], leave_sems.at[1 + i, k])

    leaving = []

    def leave(src, dst, sem):
        copy = pltpu.make_async_copy(src, dst, sem)
        copy.start()
        leaving.append(copy)

    for k in range(1, slots):
        spread(k)
        if k == slots - 1:
            for j in range(1, slots):
                target = planes[j - 1]
                copy = send_to(cot_low.at[target], cot_out.at[plane], cot_sems.at[0, j], cot_sems.at[1, j],
                               {"blk": target * group + member})
                copy.start()
                pending.append(copy)
            cot_out[plane] = cot_low[plane]
        project(k - 1)
    project(slots - 1)

    per_block = q_block // rows
    q_blocks = blocks // per_block

    def att_copy(p, g, slot, r):
        return send_to(att.at[p, g], att_in.at[slot, p], att_sems.at[0, p, r], att_sems.at[1, p, r],
                       {"blk": plane * group + g})

    def turned(step):
        return lax.rem(step + member // per_block + 1, q_blocks)

    def o_copy(step):
        span = pl.ds(pl.multiple_of(turned(step) * q_block, q_block), q_block)
        return pltpu.make_async_copy(o_ref.at[:, span], o_out.at[:, span], leave_sems.at[4, step])

    def block(step, carry):
        which = turned(step)
        span = pl.ds(pl.multiple_of(which * q_block, q_block), q_block)
        done, tops = [], []
        for h in range(heads):
            top = jnp.full((8, q_block), MASKED, F32)
            for t in range(length_all // key_tile):
                keys = slice(t * key_tile, (t + 1) * key_tile)
                part = mm_nt(k_ref[h, keys, :], q_ref[h, span, :])
                scores[h, keys, :] = part
                top = jnp.maximum(top, jnp.max(part.reshape(key_tile // 8, 8, q_block), axis=0))
            tops.append(jnp.max(top, axis=0, keepdims=True))
        for h in range(heads):
            top = tops[h]
            mixed = jnp.zeros((LANES, q_block), F32)
            for t in range(length_all // key_tile):
                keys = slice(t * key_tile, (t + 1) * key_tile)
                weights = jnp.exp(scores[h, keys, :] - top).astype(BF16)
                mixed = mixed + mm(vt[h, :, keys], weights)
            denom = mixed[HD:HD + 1, :]
            scaled = mixed * (1.0 / denom)
            sub = lax.broadcasted_iota(jnp.int32, scaled.shape, 0)
            o_rows = jnp.where(sub == HD, top + jnp.log(denom), scaled).T
            o_ref[h, span, :] = o_rows
            done.append(o_rows[:, :HD].astype(BF16))
        o_copy(step).start()
        attended = jnp.concatenate(done, axis=1)
        for u in range(per_block):
            d = which * per_block + u
            p, g = d // group, lax.rem(d, group)
            att[p, g] = attended[u * rows:(u + 1) * rows, :]

            @pl.when(g != member)
            def _():
                att_copy(p, g, member, lax.rem(g + group - member, group)).start()

            @pl.when(g == member)
            def _():
                att_in[member, p] = attended[u * rows:(u + 1) * rows, :]
        return carry

    lax.fori_loop(0, q_blocks, block, 0)
    for k in range(1, slots):
        source = lax.rem(plane + slots - k, slots)
        send_to(cot_low.at[plane], cot_out.at[source], cot_sems.at[0, k], cot_sems.at[1, k],
                {"blk": source * group + member}).wait_recv()
    for p in range(slots):
        for r in range(1, group):
            att_copy(p, member, lax.rem(member + group - r, group), r).wait_recv()
    for p in range(slots):
        for r in range(1, group):
            att_copy(p, members[r - 1], member, r).wait_send()
    for copy in pending:
        copy.wait_send()
    for copy in leaving + [o_copy(step) for step in range(q_blocks)]:
        copy.wait()


def first(tokens, cotangent, weights, biases, lengths, blocks, collective_id, q_block=1024, key_tile=512):
    slots, rows, width = tokens.shape
    group = blocks // slots
    length_all, total = blocks * rows, width // group
    heads = total // HD
    per_head = jax.ShapeDtypeStruct((heads, length_all, LANES), BF16)
    dma, vmem = pltpu.SemaphoreType.DMA, pltpu.VMEM
    return pl.pallas_call(
        functools.partial(first_kernel, slots, group, q_block, key_tile),
        out_shape=(
            jax.ShapeDtypeStruct((blocks, rows, width), BF16),
            jax.ShapeDtypeStruct((slots, rows, width), BF16),
            jax.ShapeDtypeStruct((group, slots, rows, total), BF16),
            per_head, per_head, per_head,
            jax.ShapeDtypeStruct((heads, length_all, LANES), F32),
        ),
        in_specs=[VMEM] * 7 + [SMEM],
        out_specs=(ANY, VMEM, VMEM) + (ANY,) * 4,
        scratch_shapes=[
            vmem((blocks, rows, width), BF16),
            vmem(per_head.shape, BF16),
            vmem(per_head.shape, BF16),
            vmem(per_head.shape, BF16),
            vmem(per_head.shape, F32),
            vmem((slots, rows, width), BF16),
            vmem((slots, rows, width), BF16),
            vmem((heads, LANES, length_all), BF16),
            vmem((width, 3 * total), BF16),
            vmem((slots, group, rows, total), BF16),
            vmem((heads, length_all, q_block), F32),
            dma((slots,)), dma((slots,)), dma((slots, group)), dma((slots, group)), dma((2, slots)),
            dma((2, slots, group)),
            dma((5, max(slots, length_all // q_block))),
        ],
        compiler_params=params(collective_id),
    )(tokens, cotangent, *weights, *biases, lengths)


def three(value):
    high = value.astype(BF16).astype(F32)
    mid = (value - high).astype(BF16).astype(F32)
    return high, mid, value - high - mid


def row_tile(rows):
    return next(t for t in (256, 128, 96, 64, 48, 32, 16) if rows % t == 0)


def over_rows(rows, body):
    step = row_tile(rows)

    def run(i, carry):
        body(i * step, step)
        return carry

    lax.fori_loop(0, rows // step, run, 0)


def rows_at(offset, i, step):
    return pl.ds(pl.multiple_of(offset + i, 16), step)


def rows_of(offset, n):
    return pl.ds(pl.multiple_of(offset, 16), n)


def bits_of(size):
    return [1 << i for i in range(size.bit_length() - 1)]


class Place:
    def __init__(self, docs, blocks, group):
        self.docs, self.blocks, self.group = docs, blocks, group
        self.planes = blocks // group
        self.me, self.doc = lax.axis_index("blk"), lax.axis_index("docs")
        self.plane, self.member = self.me // group, lax.rem(self.me, group)

    def pair(self, axis, bit):
        mine = self.me if axis == "blk" else self.doc
        on = lax.rem(mine // bit, 2)
        return {axis: mine + bit - 2 * bit * on}, on

    def member_peer(self, k):
        return lax.rem(self.member + k, self.group)

    def member_source(self, k):
        return lax.rem(self.member + self.group - k, self.group)

    def in_plane(self, member):
        return {"blk": self.plane * self.group + member}

    def in_line(self, plane):
        return {"blk": plane * self.group + self.member}

    def plane_peer(self, k):
        return lax.rem(self.plane + k, self.planes)

    def plane_source(self, k):
        return lax.rem(self.plane + self.planes - k, self.planes)


class Summer:
    def __init__(self, at, acc, sent, came, out, place, offset, rows, order, rest, sems, out_shift=0):
        self.at, self.acc, self.sent, self.came, self.out, self.sems = at, acc, sent, came, out, sems
        self.shift = out_shift
        self.stages = []
        for axis, bit in order:
            if axis == "planes":
                n = rows // at.planes
                self.stages.append(("planes", None, n, offset, offset + at.plane * n, place))
                offset, rows, place = offset + at.plane * n, n, place + (at.planes - 1) * n
                continue
            to, on = at.pair(axis, bit)
            n = rows // 2
            self.stages.append(("pair", to, n, offset + (1 - on) * n, offset + on * n, place))
            offset, rows, place = offset + on * n, n, place + n
        for axis, bit in rest:
            self.stages.append(("full", at.pair(axis, bit)[0], rows, offset, offset, place))
            place += rows
        self.count = len(self.stages)
        self.back = [s for s in range(self.count) if self.stages[s][0] != "full"][::-1]

    @staticmethod
    def placed(rows, order, planes, rest):
        total = 0
        for axis, _ in order:
            share = rows // planes if axis == "planes" else rows // 2
            total, rows = total + rows - share, share
        return total + rest * rows

    def copies(self, s, back=False, receive=False):
        kind, to, n, give, keep, place = self.stages[s]
        at, out = self.at, self.out
        w = 1 if back else 0
        if kind == "planes":
            found = []
            for k in range(1, at.planes):
                if back:
                    which = at.plane_source(k) if receive else at.plane
                    span = rows_of(give + which * n + self.shift, n)
                    src, dst = out.at[span], out.at[span]
                else:
                    src, dst = (ref.at[rows_of(place + (k - 1) * n, n)] for ref in (self.sent, self.came))
                to = at.in_line(at.plane_peer(k))
                found.append(send_to(src, dst, self.sems.at[w, 0, s, k], self.sems.at[w, 1, s, k], to))
            return found
        if back:
            span = rows_of((give if receive else keep) + self.shift, n)
            src, dst = out.at[span], out.at[span]
        else:
            src, dst = self.sent.at[rows_of(place, n)], self.came.at[rows_of(place, n)]
        return [send_to(src, dst, self.sems.at[w, 0, s, 0], self.sems.at[w, 1, s, 0], to)]

    def pack(self, give, place, n):
        def run(i, step):
            self.sent[rows_at(place, i, step), :] = self.acc[rows_at(give, i, step), :].astype(BF16)
        over_rows(n, run)

    def start(self, s):
        kind, to, n, give, keep, place = self.stages[s]
        if kind == "planes":
            for k in range(1, self.at.planes):
                self.pack(give + self.at.plane_peer(k) * n, place + (k - 1) * n, n)
        else:
            self.pack(give, place, n)
        for copy in self.copies(s):
            copy.start()

    def finish(self, s):
        kind, to, n, give, keep, place = self.stages[s]
        for copy in self.copies(s):
            copy.wait_recv()
        parts = self.at.planes - 1 if kind == "planes" else 1
        last = s == self.count - 1

        def run(i, step):
            total = self.acc[rows_at(keep, i, step), :]
            if kind == "full":
                total = total.astype(BF16).astype(F32)
            for k in range(parts):
                total = total + self.came[rows_at(place + k * n, i, step), :].astype(F32)
            if last:
                self.out[rows_at(keep + self.shift, i, step), :] = total.astype(BF16)
            else:
                self.acc[rows_at(keep, i, step), :] = total
        over_rows(n, run)

    def start_back(self, s):
        for copy in self.copies(s, back=True):
            copy.start()

    def finish_back(self, s):
        for copy in self.copies(s, back=True, receive=True):
            copy.wait_recv()

    def events(self, back):
        def first():
            self.start(0)

        def inward(s):
            self.finish(s)
            if s + 1 < self.count:
                self.start(s + 1)
            elif back:
                self.start_back(back[0])

        def outward(d):
            self.finish_back(back[d])
            if d + 1 < len(back):
                self.start_back(back[d + 1])

        return ([first] + [functools.partial(inward, s) for s in range(self.count)]
                + [functools.partial(outward, d) for d in range(len(back))])

    def drain(self, back):
        for s in range(self.count):
            for copy in self.copies(s):
                copy.wait_send()
        for s in back:
            for copy in self.copies(s, back=True):
                copy.wait_send()


def row_mean(value):
    return jnp.mean(value, axis=1, keepdims=True)


def col_sum(value):
    return jnp.sum(value, axis=0, keepdims=True)


def main_kernel(docs, blocks, group, cuts, k_block, q_tile,
                att_in, cot_ref, len_ref, wo_ref, ob_ref, g1_ref, s1_ref, up_hbm, ub_ref, down_hbm,
                db_ref, g2_ref, s2_ref, wq_hbm, wk_hbm, wv_hbm, q_hbm, k_hbm, v_hbm, o_hbm, tok_hbm,
                out_in, grad_in, sum_ref, qkv_ref, small_out,
                wq_ref, wk_ref, wv_ref, q_ref, k_ref, v_ref, o_ref, tok_ref, att, hid_t, gz, away, kv_in, gq_in, g_att, g_in, qx, gx, qt, gt, kv_send, gq_send,
                acc, sent, came, dwt, sent_w, came_w, bias, small_sent, small_came,
                g_sems, kv_sems, gq_sems, sum_sems, w_sems, small_sems, wide_sems, core_sems, load_sems,
                out_sems, grad_sems, enter_sems):
    at = Place(docs, blocks, group)
    me, member, plane, planes = at.me, at.member, at.plane, at.planes
    _, rows, width = tok_ref.shape
    count = planes * rows
    cols = width // group
    inner_width = up_hbm.shape[1]
    heads, length_all, _ = q_ref.shape
    parts = inner_width // width
    doc_bits = bits_of(docs)

    loads = [pltpu.make_async_copy(up_hbm.at[:, c * width:(c + 1) * width],
                                   sent.at[inner_width + c * width:inner_width + (c + 1) * width], load_sems.at[c])
             for c in range(parts)]
    loads.append(pltpu.make_async_copy(down_hbm, sent.at[:inner_width], load_sems.at[parts]))
    enter = [pltpu.make_async_copy(src, dst, enter_sems.at[i]) for i, (src, dst) in enumerate((
        (tok_hbm, tok_ref), (q_hbm, q_ref), (o_hbm, o_ref), (k_hbm, k_ref), (v_hbm, v_ref),
        (wq_hbm, wq_ref), (wk_hbm, wk_ref), (wv_hbm, wv_ref)))]
    for load in enter[:1] + loads + enter[1:]:
        load.start()

    def up_part(c):
        return sent[inner_width + c * width:inner_width + (c + 1) * width, :]

    greet([at.in_plane(at.member_peer(k)) for k in range(1, group)]
          + [at.in_line(at.plane_peer(k)) for k in range(1, planes)]
          + [at.pair("docs", bit)[0] for bit in doc_bits])

    rest = [("docs", bit) for bit in doc_bits[1:]]
    sums, place = [], 0
    for c, (offset, size, order) in enumerate(cuts):
        sums.append(Summer(at, acc, sent, came, sum_ref, place, offset, size, order, rest, sum_sems.at[c]))
        place = place + Summer.placed(size, order, planes, len(rest))
    chains = [s.events(s.back) for s in sums]
    at_event = [0] * len(cuts)

    def upcoming(numbers):
        found = []
        for c in numbers:
            if c < len(chains) and at_event[c] < len(chains[c]):
                found.append(chains[c][at_event[c]])
                at_event[c] += 1
        return found

    def advance(numbers):
        for event in upcoming(numbers):
            event()

    enter[0].wait()
    flat = jnp.concatenate([tok_ref[p * group + member].astype(F32) for p in range(planes)], axis=0)
    for p in range(planes):
        for g in range(group):
            att[p * rows:(p + 1) * rows, g * cols:(g + 1) * cols] = att_in[g, p]
    up_bias = row(ub_ref)
    gain1, gain2 = row(g1_ref), row(g2_ref)
    summed = flat + mm(att[...], wo_ref[...]) + row(ob_ref)
    centred = summed - row_mean(summed)
    rstd1 = lax.rsqrt(row_mean(centred * centred) + EPS)
    xhat1 = centred * rstd1
    hidden = xhat1 * gain1 + row(s1_ref)
    hidden_low = hidden.astype(BF16)
    hid_t[...] = hidden_low.T
    for load in loads:
        load.wait()
    ffn = jnp.zeros((count, width), F32)
    for c in range(parts):
        span = slice(c * width, (c + 1) * width)
        inner = mm(hidden_low, up_part(c)) + up_bias[:, span]
        square = inner * inner
        slope_in = 0.7978845608 * (1.0 + (3 * 0.044715) * square)
        tanh = jnp.tanh(inner * (0.7978845608 * (1.0 + 0.044715 * square)))
        half = 0.5 * (1.0 + tanh)
        acc[c * count:(c + 1) * count, :] = half + (0.5 * inner) * ((1.0 - tanh * tanh) * slope_in)
        low = (inner * half).astype(BF16)
        sum_ref[c * count:(c + 1) * count, :] = low
        ffn = ffn + mm(low, sent[span, :])
    summed = flat + hidden + ffn + row(db_ref)
    centred = summed - row_mean(summed)
    rstd2 = lax.rsqrt(row_mean(centred * centred) + EPS)
    xhat2 = centred * rstd2
    away[...] = (xhat2 * gain2 + row(s2_ref)).astype(BF16).reshape(planes, rows, width)

    def line_copies(dst, sems, receive=False):
        return [send_to(away.at[at.plane_peer(k)], dst.at[at.plane_source(k) if receive else plane],
                        sems.at[0, k], sems.at[1, k], at.in_line(at.plane_peer(k))) for k in range(1, planes)]

    for copy in line_copies(out_in, out_sems):
        copy.start()
    out_in[plane] = away[plane]
    lane_r = lax.broadcasted_iota(jnp.int32, (rows, width), 0)
    g_out = jnp.concatenate(
        [jnp.where((p * group + member) * rows + lane_r < len_ref[plane], cot_ref[p].astype(F32), 0.0)
         for p in range(planes)], axis=0)
    small_sent[0] = jnp.zeros(small_sent.shape[1:], F32)
    small_sent[0, 0:1, :] = col_sum(g_out * xhat2)
    small_sent[0, 1:2, :] = col_sum(g_out)
    scaled = g_out * gain2
    g_z2 = rstd2 * (scaled - row_mean(scaled) - xhat2 * row_mean(scaled * xhat2))
    g_ffn = g_z2.astype(BF16)
    small_sent[0, 2:3, :] = col_sum(g_ffn.astype(F32))
    g_hidden = g_z2
    for c in range(parts):
        span = slice(c * width, (c + 1) * width)
        g_inner = (mm_nt(g_ffn, sent[span, :]) * acc[c * count:(c + 1) * count, :]).astype(BF16)
        sum_ref[inner_width + c * count:inner_width + (c + 1) * count, :] = g_inner
        g_hidden = g_hidden + mm_nt(g_inner, up_part(c))
    scaled = g_hidden * gain1
    g_z1 = rstd1 * (scaled - row_mean(scaled) - xhat1 * row_mean(scaled * xhat1))
    g_branch = g_z1.astype(BF16)
    gz[...] = g_z1 + g_z2
    g_low = mm_nt(g_branch, wo_ref[...]).astype(BF16)
    for p in range(planes):
        for g in range(group):
            g_att[g, p] = g_low[p * rows:(p + 1) * rows, g * cols:(g + 1) * cols]

    def g_copy(k, receive=False):
        slot = at.member_source(k) if receive else member
        return send_to(g_att.at[at.member_peer(k)], g_in.at[:, slot], g_sems.at[0, k], g_sems.at[1, k],
                       at.in_plane(at.member_peer(k)))

    for k in range(1, group):
        g_copy(k).start()
    for p in range(planes):
        g_in[p, member] = g_att[member, p]

    for c in range(parts):
        span = slice(c * width, (c + 1) * width)
        acc[span, :] = mm_tn(sum_ref[c * count:(c + 1) * count, :], g_ffn)
    advance(POINTS[0])
    for c in range(parts):
        g_inner = sum_ref[inner_width + c * count:inner_width + (c + 1) * count, :]
        small_sent[0, 6 + c:7 + c, :] = col_sum(g_inner.astype(F32))
        acc[inner_width + c * width:inner_width + (c + 1) * width, :] = mm(hid_t[...], g_inner)
    acc[2 * inner_width:2 * inner_width + width, :] = mm_tn(att[...], g_branch)
    if acc.shape[0] > 2 * inner_width + width:
        acc[2 * inner_width + width:, :] = jnp.zeros((acc.shape[0] - 2 * inner_width - width, width), F32)
    advance(POINTS[1])
    small_sent[0, 3:4, :] = col_sum(g_hidden * xhat1)
    small_sent[0, 4:5, :] = col_sum(g_hidden)
    small_sent[0, 5:6, :] = col_sum(g_branch.astype(F32))
    chunk = group * rows
    lane = lax.broadcasted_iota(jnp.int32, (chunk, LANES), 1)

    for load in enter[1:]:
        load.wait()

    def prepare_q(step, carry):
        span = pl.ds(pl.multiple_of(step * chunk, chunk), chunk)
        for h in range(heads):
            q_rows = q_ref[h, span, :].astype(F32)
            ext = q_rows
            for i, value in enumerate(three(-o_ref[h, span, HD:HD + 1])):
                ext = jnp.where(lane == HD + 1 + i, value, ext)
            qx[h, span, :] = ext.astype(BF16)
            qt[h, :, span] = q_rows[:, :HD].T.astype(BF16)
        return carry

    lax.fori_loop(0, planes, prepare_q, 0)
    advance(POINTS[2])
    for k in range(1, group):
        g_copy(k, True).wait_recv()

    def prepare_g(step, carry):
        span = pl.ds(pl.multiple_of(step * chunk, chunk), chunk)
        g_block = g_in[step].reshape(chunk, cols)
        for h in range(heads):
            g_rows = g_block[:, h * HD:(h + 1) * HD].astype(F32)
            g_rows = jnp.concatenate([g_rows, jnp.zeros_like(g_rows)], axis=1)
            delta = jnp.sum(g_rows * o_ref[h, span, :], axis=1, keepdims=True)
            ext = g_rows
            for i, value in enumerate(three(-delta)):
                ext = jnp.where(lane == HD + i, value, ext)
            gx[h, span, :] = ext.astype(BF16)
            gt[h, :, span] = g_rows[:, :HD].T.astype(BF16)
        return carry

    lax.fori_loop(0, planes, prepare_g, 0)
    advance(POINTS[3])

    gq_acc = o_ref.at[0]
    k_blocks = length_all // k_block
    per_block = k_block // rows
    ones = jnp.ones((8, k_block), BF16)
    dwt[...] = jnp.zeros_like(dwt)
    bias[...] = jnp.zeros_like(bias)

    def kv_copy(h, p, g, slot, r):
        return send_to(kv_send.at[h, p, g], kv_in.at[slot, h, p], kv_sems.at[0, h, p, r], kv_sems.at[1, h, p, r],
                       at.in_plane(g))

    def gq_copy(h, r, receive=False):
        slot = at.member_source(r) if receive else member
        return send_to(gq_send.at[h, :, at.member_peer(r)], gq_in.at[slot, h], gq_sems.at[0, h, r],
                       gq_sems.at[1, h, r], at.in_plane(at.member_peer(r)))

    total_steps = heads * k_blocks
    timed = [(t, event) for t in range(min(total_steps, len(AT_BLOCK))) for event in upcoming(AT_BLOCK[t])]

    def block(step, carry):
        h, i = step // k_blocks, lax.rem(step, k_blocks)
        which = lax.rem(i + member // per_block + 1, k_blocks)
        span = pl.ds(pl.multiple_of(which * k_block, k_block), k_block)
        k_rows, v_rows = k_ref[h, span, :], v_ref[h, span, :]

        @pl.when(i == 0)
        def _():
            gq_acc[...] = jnp.zeros_like(gq_acc)

        gk = jnp.zeros((HD, k_block), F32)
        gv = jnp.zeros((HD, k_block), F32)
        tiles = [slice(t, t + q_tile) for t in range(0, length_all, q_tile)]

        def products(tile):
            return mm_nt(qx[h, tile, :], k_rows), mm_nt(gx[h, tile, :], v_rows)

        ahead = products(tiles[0])
        for tile, later in zip(tiles, tiles[1:] + [None]):
            scores, centred = ahead
            ahead = products(later) if later else None
            weights = jnp.exp(scores)
            g_scores = (weights * centred).astype(BF16)
            gv = gv + mm(gt[h, :, tile], weights.astype(BF16))
            gk = gk + mm(qt[h, :, tile], g_scores)
            gq_acc[tile, :] += mm(g_scores, k_rows)
        kv = jnp.concatenate([gk, gv], axis=0).astype(BF16)
        tok_rows = tok_ref[pl.ds(which * per_block, per_block)].reshape(k_block, width)
        dwt[pl.ds(pl.multiple_of(h * 2 * HD, 2 * HD), 2 * HD), :] += mm(kv, tok_rows)
        bias[h, 0] += mm_nt(ones, kv[HD:])
        for u in range(per_block):
            d = which * per_block + u
            p, g = d // group, lax.rem(d, group)
            kv_send[h, p, g] = kv[:, u * rows:(u + 1) * rows]

            @pl.when(g != member)
            def _():
                kv_copy(h, p, g, member, lax.rem(g + group - member, group)).start()

            @pl.when(g == member)
            def _():
                kv_in[member, h, p] = kv[:, u * rows:(u + 1) * rows]

        @pl.when(i == k_blocks - 1)
        def _():
            for n in range(blocks):
                gq_send[h, n // group, n % group] = (
                    gq_acc[n * rows:(n + 1) * rows, :HD] * (HD ** -0.5)).T.astype(BF16)
            for r in range(1, group):
                gq_copy(h, r).start()
            for p in range(planes):
                gq_in[member, h, p] = gq_send[h, p, member]

        for t, event in timed:
            pl.when(step == t)(event)
        return carry

    lax.fori_loop(0, total_steps, block, 0)

    q_base = heads * 2 * HD
    for h in range(heads):
        part = jnp.zeros((HD, width), F32)
        q_bias = jnp.zeros((8, HD), F32)
        for n in range(blocks):
            low = gq_send[h, n // group, n % group]
            part = part + mm(low, tok_ref[n])
            q_bias = q_bias + mm_nt(jnp.ones((8, rows), BF16), low)
        dwt[q_base + h * HD:q_base + (h + 1) * HD, :] = part
        bias[h, 1] = q_bias
    half = dwt.shape[0] // 2
    my_core = lax.rem(at.doc, 2)
    w_sum = Summer(at, dwt, sent_w, came_w, qkv_ref, 0, 0, 2 * half, W_ORDER, rest, w_sems,
                   out_shift=my_core * (half * group - half) + member * half)
    w_line = next(s for s in w_sum.back if w_sum.stages[s][0] == "planes")
    share = half // planes
    w_chain = w_sum.events([])
    lane_w = lax.broadcasted_iota(jnp.int32, (8, width), 1)
    sub = lax.broadcasted_iota(jnp.int32, (8, width), 0)
    wide = [jnp.concatenate([bias[h, i] for h in range(heads)] * group, axis=1) for i in range(2)]
    small_sent[0, 16:24, :] = jnp.where(
        (lane_w // cols) == member, jnp.where(sub == 0, wide[1], jnp.where(sub == 1, wide[0], 0.0)), 0.0)
    small_order = [("docs", 1)] + [("blk", bit) for bit in bits_of(group)]

    def small_copy(s):
        return send_to(small_sent.at[s], small_came.at[s], small_sems.at[0, s], small_sems.at[1, s],
                       at.pair(*small_order[s])[0])

    small_last = len(small_order)

    def small_line(k, receive=False):
        slot = small_last + k
        return send_to(small_sent.at[small_last], small_came.at[slot], small_sems.at[0, slot],
                       small_sems.at[1, slot], at.in_line(at.plane_peer(k)))

    def small_rest(i):
        slot = small_last + planes + i
        return send_to(small_sent.at[small_last + 1 + i], small_came.at[slot], small_sems.at[0, slot],
                       small_sems.at[1, slot], at.pair(*rest[i])[0])

    def small_step(s):
        small_copy(s).wait_recv()
        small_sent[s + 1] = small_sent[s] + small_came[s]
        if s + 1 < small_last:
            small_copy(s + 1).start()
        else:
            for k in range(1, planes):
                small_line(k).start()

    def small_end():
        for k in range(1, planes):
            small_line(k).wait_recv()
        total = jnp.zeros(small_sent.shape[1:], F32)
        for p in range(planes):
            value = small_sent[small_last]
            for k in range(1, planes):
                value = jnp.where(at.plane_source(k) == p, small_came[small_last + k], value)
            total = total + value
        for i in range(len(rest)):
            small_sent[small_last + 1 + i] = total
            small_rest(i).start()
            small_rest(i).wait_recv()
            total = total + small_came[small_last + planes + i]
        small_out[...] = total

    def slab(core, m, p=0, n=half):
        return qkv_ref.at[rows_of(core * half * group + m * half + p * share, n)]

    def wide_copy(k, j, m):
        piece = slab(my_core, m, at.plane_source(j), share)
        return send_to(piece, piece, wide_sems.at[0, k, j], wide_sems.at[1, k, j], at.in_plane(at.member_peer(k)))

    def core_copy(k, core):
        piece = slab(core, at.member_source(k))
        return send_to(piece, piece, core_sems.at[0, k], core_sems.at[1, k], at.pair("docs", 1)[0])

    def w_out():
        w_chain[-1]()
        w_sum.start_back(w_line)
        for k in range(1, group):
            wide_copy(k, 0, member).start()

    def w_forward():
        for j, copy in enumerate(w_sum.copies(w_line, back=True, receive=True)):
            copy.wait_recv()
            for k in range(1, group):
                wide_copy(k, j + 1, member).start()
        core_copy(0, my_core).start()

    def w_slabs():
        for k in range(1, group):
            for j in range(planes):
                wide_copy(k, j, at.member_source(k)).wait_recv()
            core_copy(k, my_core).start()

    def gather_part(which):
        for p in range(planes):
            for g in range(group):
                for h in range(heads):
                    low = gq_in[g, h, p] if which == 0 else kv_in[g, h, p, (which - 1) * HD:which * HD, :]
                    hid_t[g * cols + h * HD:g * cols + (h + 1) * HD, p * rows:(p + 1) * rows] = low
        return hid_t[...].T

    def key_value_rows():
        for h in range(heads):
            for p in range(planes):
                for r in range(1, group):
                    kv_copy(h, p, member, at.member_source(r), r).wait_recv()
        gz[...] += mm_nt(gather_part(1), wk_ref[...])
        gz[...] += mm_nt(gather_part(2), wv_ref[...])

    def query_rows():
        for h in range(heads):
            for r in range(1, group):
                gq_copy(h, r, True).wait_recv()
        total = gz[...] + mm_nt(gather_part(0), wq_ref[...])
        for copy in line_copies(out_in, out_sems, True):
            copy.wait_recv()
        for copy in line_copies(out_in, out_sems):
            copy.wait_send()
        away[...] = total.astype(BF16).reshape(planes, rows, width)
        for copy in line_copies(grad_in, grad_sems):
            copy.start()
        grad_in[plane] = away[plane]

    w_events = w_chain[:-1] + [w_out, w_forward, w_slabs]
    small_events = [small_copy(0).start] + [functools.partial(small_step, s) for s in range(small_last)] + [small_end]
    named = {"w": w_events, "g": [key_value_rows, query_rows], "s": small_events}
    for name in AFTER:
        if name in named:
            if named[name]:
                named[name].pop(0)()
        else:
            advance((name,))
    while any(named.values()) or any(at_event[c] < len(chains[c]) for c in range(len(cuts))):
        for work in named.values():
            if work:
                work.pop(0)()
        advance(range(len(cuts)))
    for k in range(group):
        core_copy(k, 1 - my_core).wait_recv()
    for copy in line_copies(grad_in, grad_sems, True):
        copy.wait_recv()
    for copy in line_copies(grad_in, grad_sems):
        copy.wait_send()
    for r in range(1, group):
        g_copy(r).wait_send()
        for h in range(heads):
            gq_copy(h, r).wait_send()
            for p in range(planes):
                kv_copy(h, p, at.member_peer(r), member, r).wait_send()
    for part in sums:
        part.drain(part.back)
    w_sum.drain([w_line])
    for k in range(group):
        core_copy(k, my_core).wait_send()
        for j in range(planes if k else 0):
            wide_copy(k, j, member).wait_send()
    for s in range(small_last):
        small_copy(s).wait_send()
    for k in range(1, planes):
        small_line(k).wait_send()
    for i in range(len(rest)):
        small_rest(i).wait_send()


def member_bits(group, name):
    bits = bits_of(group)
    return bits[:len(bits) // 2] if name == "x" else bits[len(bits) // 2:]


SUMS = ((2, ("xyz", "yxz")), (4, ("yxz", "zxy", "xyz", "xyz")))
W_ORDER = [("docs", 1), ("planes", 0)]
POINTS = ((0, 1,), (0, 4, 1, 2, 3, 5,), (4, 3, 5, 2, 0,), (1,))
AT_BLOCK = ((), (3, 0, 4,), (1, 5, 2, 4, 0, 3,),
            (2, 1, 5, 3,), (0,), (2, 3, 4, 1,),
            (5, 3, 0,), ())
AFTER = ("w", 4, 5, "s", "w", 2, 1, 0, 4, 3, "s", "g", "w", 5, 2, "g", "s", "w", 4, 5, 1, 1, 2, "s", 0, 5,
         "w", 2, 3, 4, "g", "w", "s",)


def main(docs, blocks, group, att_in, cotangent, lengths, weights, attention, tok_doc, collective_id,
         k_block=512, q_tile=256):
    q = attention[0]
    heads, length_all, _ = q.shape
    _, rows, width = tok_doc.shape
    planes = blocks // group
    count = planes * rows
    cols = heads * HD
    inner_width = weights[4].shape[1]
    features = -(-3 * cols // 128) * 128
    unit = 32 * blocks
    second = -(-(inner_width + width) // unit)
    cuts, offset = [], 0
    for (pieces, turns), units in zip(SUMS, (inner_width // unit, second)):
        pieces = min(pieces, units)
        for i in range(pieces):
            size = unit * (units // pieces + (1 if i >= pieces - units % pieces else 0))
            cuts.append((offset, size, [("docs", 1)] + [
                step for name in turns[i] for step in (
                    [("planes", 0)] if name == "z" else [("blk", bit) for bit in member_bits(group, name)])]))
            offset += size
    total = inner_width + second * unit
    members, rest = len(bits_of(group)), len(bits_of(docs)) - 1
    placed = sum(Summer.placed(size, order, planes, rest) for _, size, order in cuts)
    w_placed = Summer.placed(features, W_ORDER, planes, rest)
    stages = 2 + members + rest
    steps = 1 + members + planes + rest
    dma, vmem = pltpu.SemaphoreType.DMA, pltpu.VMEM
    return pl.pallas_call(
        functools.partial(main_kernel, docs, blocks, group, cuts, k_block, q_tile),
        out_shape=(
            jax.ShapeDtypeStruct((planes, rows, width), BF16),
            jax.ShapeDtypeStruct((planes, rows, width), BF16),
            jax.ShapeDtypeStruct((total, width), BF16),
            jax.ShapeDtypeStruct((features * group, width), BF16),
            jax.ShapeDtypeStruct((24, width), F32),
        ),
        in_specs=[VMEM] * 2 + [SMEM] + [VMEM] * 4 + [ANY, VMEM, ANY] + [VMEM] * 3 + [ANY] * 8,
        out_specs=(VMEM,) * 5,
        scratch_shapes=[
            *(vmem((width, width), BF16) for _ in range(3)),
            *(vmem(array.shape, array.dtype) for array in (*attention, tok_doc)),
            vmem((count, width), BF16),
            vmem((width, count), BF16),
            vmem((count, width), F32),
            vmem((planes, rows, width), BF16),
            vmem((group, heads, planes, 2 * HD, rows), BF16),
            vmem((group, heads, planes, HD, rows), BF16),
            vmem((group, planes, rows, cols), BF16),
            vmem((planes, group, rows, cols), BF16),
            vmem((heads, length_all, LANES), BF16),
            vmem((heads, length_all, LANES), BF16),
            vmem((heads, HD, length_all), BF16),
            vmem((heads, HD, length_all), BF16),
            vmem((heads, planes, group, 2 * HD, rows), BF16),
            vmem((heads, planes, group, HD, rows), BF16),
            vmem((total, width), F32),
            vmem((max(placed, 2 * inner_width), width), BF16),
            vmem((placed, width), BF16),
            vmem((features, width), F32),
            vmem((w_placed, width), BF16),
            vmem((w_placed, width), BF16),
            vmem((heads, 2, 8, HD), F32),
            vmem((steps, 24, width), F32),
            vmem((steps, 24, width), F32),
            dma((2, group)),
            dma((2, heads, planes, group)),
            dma((2, heads, group)),
            dma((len(cuts), 2, 2, stages, planes)),
            dma((2, 2, 2 + rest, planes)),
            dma((2, steps)),
            dma((2, group, planes)),
            dma((2, group)),
            dma((inner_width // width + 1,)),
            dma((2, planes)),
            dma((2, planes)),
            dma((8,)),
        ],
        compiler_params=params(collective_id),
    )(att_in, cotangent, lengths, *weights, *attention, tok_doc)


def last_kernel(group, heads, out_in, grad_in, sum_in, qkv_in, small_ref,
                out_ref, grad_ref, qw_ref, qb_ref, kw_ref, vw_ref, vb_ref, ow_ref, ob_ref, g1_ref, s1_ref,
                uw_ref, ub_ref, dw_ref, db_ref, g2_ref, s2_ref, rows_low, sums_low, qkv_low, stack, wide, come, go):
    width = ow_ref.shape[0]
    inner_width = uw_ref.shape[1]
    cols = width // group
    parts = inner_width // width
    spans = [slice(i * width, (i + 1) * width) for i in range(2 * parts + 1)]
    arrive = [pltpu.make_async_copy(sum_in.at[span], sums_low.at[span], come.at[i]) for i, span in enumerate(spans)]
    late = [pltpu.make_async_copy(qkv_in, qkv_low, come.at[len(spans)])]
    late += [pltpu.make_async_copy(src, rows_low.at[i], come.at[len(spans) + 1 + i])
             for i, src in enumerate((out_in, grad_in))]
    for copy in arrive + late:
        copy.start()
    targets = ([dw_ref.at[span] for span in spans[:parts]] + [uw_ref.at[:, span] for span in spans[:parts]] + [ow_ref])
    leaving = []

    def leave(slot, target):
        copy = pltpu.make_async_copy(wide.at[slot], target, go.at[slot])
        copy.start()
        leaving.append(copy)

    for i, span in enumerate(spans):
        arrive[i].wait()
        wide[i] = sums_low[span, :].astype(F32)
        leave(i, targets[i])
    for copy in late:
        copy.wait()
    slot = len(spans)
    planes, rows = out_ref.shape[0], out_ref.shape[1]
    for i, out in enumerate((out_ref, grad_ref)):
        for p in range(planes):
            wide[slot, p * rows:(p + 1) * rows, :] = rows_low[i, p].astype(F32)
            copy = pltpu.make_async_copy(wide.at[slot, p * rows:(p + 1) * rows], out.at[p], go.at[slot + 3 + i * planes + p])
            copy.start()
            leaving.append(copy)
        slot += 1
    half = qkv_low.shape[0] // group // 2
    unit = HD // 2
    for which, out in enumerate((qw_ref, kw_ref, vw_ref)):
        for g in range(group):
            for h in range(heads):
                first = heads * 2 * HD + h * HD if which == 0 else h * 2 * HD + (which - 1) * HD
                for u in range(2):
                    f = first + u * unit
                    at = f // half * half * group + g * half + f % half
                    to = g * cols + h * HD + u * unit
                    stack[to:to + unit, :] = qkv_low[at:at + unit, :]
        wide[slot] = stack[...].T.astype(F32)
        copy = pltpu.make_async_copy(wide.at[slot], out, go.at[len(spans) + which])
        copy.start()
        leaving.append(copy)
        slot += 1

    def vector(out, i):
        out[...] = small_ref[i:i + 1, :].reshape(out.shape)

    for i, out in ((16, qb_ref), (17, vb_ref), (0, g2_ref), (1, s2_ref), (2, db_ref), (3, g1_ref), (4, s1_ref),
                   (5, ob_ref)):
        vector(out, i)
    ub_ref[...] = jnp.concatenate([small_ref[6 + i:7 + i, :] for i in range(parts)], axis=1).reshape(ub_ref.shape)
    for copy in leaving:
        copy.wait()


def last(group, shape, inner_width, *arrays):
    slots, rows, width = shape
    heads = width // group // HD
    parts = 2 * inner_width // width + 1
    whole = jax.ShapeDtypeStruct(shape, F32)
    square = jax.ShapeDtypeStruct((width, width), F32)
    vector = jax.ShapeDtypeStruct((width,), F32)
    dma, vmem = pltpu.SemaphoreType.DMA, pltpu.VMEM
    shapes = (whole, whole, square, vector, square, square, vector, square, vector, vector, vector,
              jax.ShapeDtypeStruct((width, inner_width), F32), jax.ShapeDtypeStruct((inner_width,), F32),
              jax.ShapeDtypeStruct((inner_width, width), F32), vector, vector, vector)
    return pl.pallas_call(
        functools.partial(last_kernel, group, heads),
        out_shape=shapes,
        in_specs=[ANY] * 4 + [VMEM],
        out_specs=tuple(VMEM if len(shape.shape) == 1 else ANY for shape in shapes),
        scratch_shapes=[
            vmem((2, slots, rows, width), BF16),
            vmem((parts * width, width), BF16),
            vmem(arrays[3].shape, BF16),
            vmem((width, width), BF16),
            vmem((parts + 5, max(width, slots * rows), width), F32),
            dma((parts + 3,)),
            dma((parts + 5 + 2 * slots,)),
        ],
        compiler_params=params(),
    )(*arrays)


def device_program(docs, blocks, tokens, query_weight, query_bias, key_weight, value_weight, value_bias,
                   out_weight, out_bias, first_gain, first_shift, up_weight, up_bias, down_weight,
                   down_bias, second_gain, second_shift, cotangent, lengths):
    slots, rows, width = tokens.shape
    inner_width = up_weight.shape[1]
    group = blocks // slots
    projections = (query_weight, key_weight, value_weight)
    tok_doc, cot, att_in, q, k, v, o = first(tokens, cotangent, projections, (query_bias, value_bias), lengths,
                                             blocks, 0)
    parts = main(
        docs, blocks, group, att_in, cot, lengths,
        (out_weight, out_bias, first_gain, first_shift, up_weight, up_bias, down_weight, down_bias,
         second_gain, second_shift, *projections), (q, k, v, o), tok_doc, 1)
    return last(group, tokens.shape, inner_width, *parts)


def solution(mesh):
    split = P("docs", "blk", None)
    return jax.shard_map(
        functools.partial(device_program, mesh.shape["docs"], mesh.shape["blk"]),
        mesh=mesh,
        in_specs=(split,) + (P(),) * 15 + (split, P("docs")),
        out_specs=(split, split) + (P(),) * 15,
        check_vma=False,
    )
```

```python
import functools

import jax
import jax.numpy as jnp
from jax import lax
from jax.experimental import pallas as pl
from jax.experimental.pallas import tpu as pltpu
from jax.sharding import PartitionSpec as P

HD = 64
LANES = 128
EPS = 1e-05
MASKED = -1e30
F32 = jnp.float32
BF16 = jnp.bfloat16
VMEM = pl.BlockSpec(memory_space=pltpu.VMEM)
ANY = pl.BlockSpec(memory_space=pl.ANY)
SMEM = pl.BlockSpec(memory_space=pltpu.SMEM)
MESH = pl.DeviceIdType.MESH
VMEM_LIMIT = 63 * 1024 * 1024


def mm(left, right):
    return jnp.dot(left, right, preferred_element_type=F32)


def mm_nt(left, right):
    return lax.dot_general(left, right, (((1,), (1,)), ((), ())), preferred_element_type=F32)


def mm_tn(left, right):
    return lax.dot_general(left, right, (((0,), (0,)), ((), ())), preferred_element_type=F32)


def params(collective_id=None):
    if collective_id is None:
        return pltpu.CompilerParams(vmem_limit_bytes=VMEM_LIMIT)
    return pltpu.CompilerParams(
        vmem_limit_bytes=VMEM_LIMIT, collective_id=collective_id, has_side_effects=True
    )


def greet(peers):
    barrier = pltpu.get_barrier_semaphore()
    for peer in peers:
        pl.semaphore_signal(barrier, inc=1, device_id=peer, device_id_type=MESH)
    return lambda: pl.semaphore_wait(barrier, len(peers))


def send_to(src, dst, send_sem, recv_sem, peer):
    return pltpu.make_async_remote_copy(
        src_ref=src, dst_ref=dst, send_sem=send_sem, recv_sem=recv_sem,
        device_id=peer, device_id_type=MESH,
    )


def row(ref):
    return ref[...].astype(F32).reshape(1, ref.shape[0])


def own_columns(ref, member, cols):
    if cols % LANES == 0:
        return ref[:, pl.ds(pl.multiple_of(member * cols, LANES), cols)]
    per = LANES // cols
    both = ref[:, pl.ds(pl.multiple_of(member // per * LANES, LANES), LANES)].astype(F32)
    return sum(jnp.where(lax.rem(member, per) == i, both[:, i * cols:(i + 1) * cols], 0.0)
               for i in range(per)).astype(BF16)


def own_entries(ref, member, cols):
    values = row(ref)
    return sum(jnp.where(member == i, values[:, i * cols:(i + 1) * cols], 0.0)
               for i in range(ref.shape[0] // cols))


def first_kernel(slots, group, q_block, key_tile, tok_hbm, cot_hbm, wq_hbm, wk_hbm, wv_hbm, qb_ref, vb_ref, len_ref,
                 tok_out, cot_out, att_in, q_out, k_out, v_out, o_out,
                 tok_in, cot_in, wq_ref, wk_ref, wv_ref, tok_ref, q_ref, k_ref, v_ref, o_ref, low, cot_low, vt, w_ref, att, scores, send_a, recv_a, send_b, recv_b, cot_sems, att_sems, leave_sems, enter_sems):
    me = lax.axis_index("blk")
    plane, member = me // group, lax.rem(me, group)
    blocks, rows, width = tok_ref.shape
    length_all, total = blocks * rows, width // group
    heads = total // HD
    planes = [lax.rem(plane + k, slots) for k in range(1, slots)]
    members = [lax.rem(member + k, group) for k in range(1, group)]
    all_here = greet([{"blk": p * group + member} for p in planes]
                     + [{"blk": plane * group + m} for m in members])

    enter = [pltpu.make_async_copy(src, dst, enter_sems.at[i]) for i, (src, dst) in enumerate((
        (tok_hbm, tok_in), (wq_hbm, wq_ref), (wk_hbm, wk_ref), (wv_hbm, wv_ref), (cot_hbm, cot_in)))]
    for load in enter:
        load.start()
    enter[0].wait()
    low[...] = tok_in[...].astype(BF16)
    all_here()
    pending = []
    for k in range(1, slots):
        target = planes[k - 1]
        copy = send_to(low.at[target], tok_ref.at[me], send_a.at[k], recv_a.at[k],
                       {"blk": target * group + member})
        copy.start()
        pending.append(copy)
    tok_ref[me] = low[plane]

    def spread(k):
        block = lax.rem(plane + slots - k, slots) * group + member
        if k > 0:
            send_to(low.at[plane], tok_ref.at[block], send_a.at[k], recv_a.at[k],
                    {"blk": block}).wait_recv()
        for j in range(1, group):
            copy = send_to(tok_ref.at[block], tok_ref.at[block], send_b.at[k, j], recv_b.at[k, j],
                           {"blk": plane * group + members[j - 1]})
            copy.start()
            pending.append(copy)

    spread(0)
    for load in enter[1:]:
        load.wait()
    cot_low[...] = cot_in[...].astype(BF16)
    for i, ref in enumerate((wq_ref, wk_ref, wv_ref)):
        w_ref[:, i * total:(i + 1) * total] = own_columns(ref, member, total)
    bias = jnp.concatenate(
        [own_entries(qb_ref, member, total), jnp.zeros((1, total), F32),
         own_entries(vb_ref, member, total)], axis=1)
    doc_len = len_ref[plane]
    chunk = group * rows

    def project(k):
        source = lax.rem(plane + slots - k, slots)
        for j in range(1, group):
            block = source * group + lax.rem(member + group - j, group)
            send_to(tok_ref.at[block], tok_ref.at[block], send_b.at[k, j], recv_b.at[k, j],
                    {"blk": plane * group + members[j - 1]}).wait_recv()
        span = pl.ds(pl.multiple_of(source * chunk, chunk), chunk)
        qkv = mm(tok_ref[pl.ds(source * group, group)].reshape(chunk, width), w_ref[...]) + bias
        lane = lax.broadcasted_iota(jnp.int32, (chunk, LANES), 1)
        position = source * chunk + lax.broadcasted_iota(jnp.int32, (chunk, LANES), 0)
        mask = jnp.where(position < doc_len, 0.0, MASKED)
        for h in range(heads):
            def part(which):
                cols = qkv[:, which * total + h * HD:which * total + (h + 1) * HD]
                return jnp.concatenate([cols, jnp.zeros_like(cols)], axis=1)
            q_ref[h, span, :] = jnp.where(
                lane == HD, 1.0, part(0).astype(BF16).astype(F32) * (HD ** -0.5)).astype(BF16)
            k_ref[h, span, :] = jnp.where(
                lane == HD, mask, jnp.where((lane > HD) & (lane < HD + 4), 1.0, part(1))).astype(BF16)
            v_rows = jnp.where((lane >= HD) & (lane < HD + 4), 1.0, part(2)).astype(BF16)
            v_ref[h, span, :] = v_rows
            vt[h, :, span] = v_rows.T
        members_of = pl.ds(source * group, group)
        leave(tok_ref.at[members_of], tok_out.at[members_of], leave_sems.at[0, k])
        for i, (ref, out) in enumerate(((q_ref, q_out), (k_ref, k_out), (v_ref, v_out))):
            leave(ref.at[:, span], out.at[:, span], leave_sems.at[1 + i, k])

    leaving = []

    def leave(src, dst, sem):
        copy = pltpu.make_async_copy(src, dst, sem)
        copy.start()
        leaving.append(copy)

    for k in range(1, slots):
        spread(k)
        if k == slots - 1:
            for j in range(1, slots):
                target = planes[j - 1]
                copy = send_to(cot_low.at[target], cot_out.at[plane], cot_sems.at[0, j], cot_sems.at[1, j],
                               {"blk": target * group + member})
                copy.start()
                pending.append(copy)
            cot_out[plane] = cot_low[plane]
        project(k - 1)
    project(slots - 1)

    per_block = q_block // rows
    q_blocks = blocks // per_block

    def att_copy(p, g, slot, r):
        return send_to(att.at[p, g], att_in.at[slot, p], att_sems.at[0, p, r], att_sems.at[1, p, r],
                       {"blk": plane * group + g})

    def turned(step):
        return lax.rem(step + member // per_block + 1, q_blocks)

    def o_copy(step):
        span = pl.ds(pl.multiple_of(turned(step) * q_block, q_block), q_block)
        return pltpu.make_async_copy(o_ref.at[:, span], o_out.at[:, span], leave_sems.at[4, step])

    def block(step, carry):
        which = turned(step)
        span = pl.ds(pl.multiple_of(which * q_block, q_block), q_block)
        done, tops = [], []
        for h in range(heads):
            top = jnp.full((8, q_block), MASKED, F32)
            for t in range(length_all // key_tile):
                keys = slice(t * key_tile, (t + 1) * key_tile)
                part = mm_nt(k_ref[h, keys, :], q_ref[h, span, :])
                scores[h, keys, :] = part
                top = jnp.maximum(top, jnp.max(part.reshape(key_tile // 8, 8, q_block), axis=0))
            tops.append(jnp.max(top, axis=0, keepdims=True))
        for h in range(heads):
            top = tops[h]
            mixed = jnp.zeros((LANES, q_block), F32)
            for t in range(length_all // key_tile):
                keys = slice(t * key_tile, (t + 1) * key_tile)
                weights = jnp.exp(scores[h, keys, :] - top).astype(BF16)
                mixed = mixed + mm(vt[h, :, keys], weights)
            denom = mixed[HD:HD + 1, :]
            scaled = mixed * (1.0 / denom)
            sub = lax.broadcasted_iota(jnp.int32, scaled.shape, 0)
            o_rows = jnp.where(sub == HD, top + jnp.log(denom), scaled).T
            o_ref[h, span, :] = o_rows
            done.append(o_rows[:, :HD].astype(BF16))
        o_copy(step).start()
        attended = jnp.concatenate(done, axis=1)
        for u in range(per_block):
            d = which * per_block + u
            p, g = d // group, lax.rem(d, group)
            att[p, g] = attended[u * rows:(u + 1) * rows, :]

            @pl.when(g != member)
            def _():
                att_copy(p, g, member, lax.rem(g + group - member, group)).start()

            @pl.when(g == member)
            def _():
                att_in[member, p] = attended[u * rows:(u + 1) * rows, :]
        return carry

    lax.fori_loop(0, q_blocks, block, 0)
    for k in range(1, slots):
        source = lax.rem(plane + slots - k, slots)
        send_to(cot_low.at[plane], cot_out.at[source], cot_sems.at[0, k], cot_sems.at[1, k],
                {"blk": source * group + member}).wait_recv()
    for p in range(slots):
        for r in range(1, group):
            att_copy(p, member, lax.rem(member + group - r, group), r).wait_recv()
    for p in range(slots):
        for r in range(1, group):
            att_copy(p, members[r - 1], member, r).wait_send()
    for copy in pending:
        copy.wait_send()
    for copy in leaving + [o_copy(step) for step in range(q_blocks)]:
        copy.wait()


def first(tokens, cotangent, weights, biases, lengths, blocks, collective_id, q_block=1024, key_tile=512):
    slots, rows, width = tokens.shape
    group = blocks // slots
    length_all, total = blocks * rows, width // group
    heads = total // HD
    per_head = jax.ShapeDtypeStruct((heads, length_all, LANES), BF16)
    dma, vmem = pltpu.SemaphoreType.DMA, pltpu.VMEM
    return pl.pallas_call(
        functools.partial(first_kernel, slots, group, q_block, key_tile),
        out_shape=(
            jax.ShapeDtypeStruct((blocks, rows, width), BF16),
            jax.ShapeDtypeStruct((slots, rows, width), BF16),
            jax.ShapeDtypeStruct((group, slots, rows, total), BF16),
            per_head, per_head, per_head,
            jax.ShapeDtypeStruct((heads, length_all, LANES), F32),
        ),
        in_specs=[ANY] * 5 + [VMEM] * 2 + [SMEM],
        out_specs=(ANY, VMEM, VMEM) + (ANY,) * 4,
        scratch_shapes=[
            vmem(tokens.shape, F32),
            vmem(tokens.shape, F32),
            *(vmem((width, width), BF16) for _ in range(3)),
            vmem((blocks, rows, width), BF16),
            vmem(per_head.shape, BF16),
            vmem(per_head.shape, BF16),
            vmem(per_head.shape, BF16),
            vmem(per_head.shape, F32),
            vmem((slots, rows, width), BF16),
            vmem((slots, rows, width), BF16),
            vmem((heads, LANES, length_all), BF16),
            vmem((width, 3 * total), BF16),
            vmem((slots, group, rows, total), BF16),
            vmem((heads, length_all, q_block), F32),
            dma((slots,)), dma((slots,)), dma((slots, group)), dma((slots, group)), dma((2, slots)),
            dma((2, slots, group)),
            dma((5, max(slots, length_all // q_block))),
            dma((5,)),
        ],
        compiler_params=params(collective_id),
    )(tokens, cotangent, *weights, *biases, lengths)


def three(value):
    high = value.astype(BF16).astype(F32)
    mid = (value - high).astype(BF16).astype(F32)
    return high, mid, value - high - mid


def row_tile(rows):
    return next(t for t in (256, 128, 96, 64, 48, 32, 16) if rows % t == 0)


def over_rows(rows, body):
    step = row_tile(rows)

    def run(i, carry):
        body(i * step, step)
        return carry

    lax.fori_loop(0, rows // step, run, 0)


def rows_at(offset, i, step):
    return pl.ds(pl.multiple_of(offset + i, 16), step)


def rows_of(offset, n):
    return pl.ds(pl.multiple_of(offset, 16), n)


def bits_of(size):
    return [1 << i for i in range(size.bit_length() - 1)]


class Place:
    def __init__(self, docs, blocks, group):
        self.docs, self.blocks, self.group = docs, blocks, group
        self.planes = blocks // group
        self.me, self.doc = lax.axis_index("blk"), lax.axis_index("docs")
        self.plane, self.member = self.me // group, lax.rem(self.me, group)

    def pair(self, axis, bit):
        mine = self.me if axis == "blk" else self.doc
        on = lax.rem(mine // bit, 2)
        return {axis: mine + bit - 2 * bit * on}, on

    def member_peer(self, k):
        return lax.rem(self.member + k, self.group)

    def member_source(self, k):
        return lax.rem(self.member + self.group - k, self.group)

    def in_plane(self, member):
        return {"blk": self.plane * self.group + member}

    def in_line(self, plane):
        return {"blk": plane * self.group + self.member}

    def plane_peer(self, k):
        return lax.rem(self.plane + k, self.planes)

    def plane_source(self, k):
        return lax.rem(self.plane + self.planes - k, self.planes)


class Summer:
    def __init__(self, at, acc, sent, came, out, place, offset, rows, order, rest, sems, out_shift=0):
        self.at, self.acc, self.sent, self.came, self.out, self.sems = at, acc, sent, came, out, sems
        self.shift = out_shift
        self.stages = []
        for axis, bit in order:
            if axis == "planes":
                n = rows // at.planes
                self.stages.append(("planes", None, n, offset, offset + at.plane * n, place))
                offset, rows, place = offset + at.plane * n, n, place + (at.planes - 1) * n
                continue
            to, on = at.pair(axis, bit)
            n = rows // 2
            self.stages.append(("pair", to, n, offset + (1 - on) * n, offset + on * n, place))
            offset, rows, place = offset + on * n, n, place + n
        for axis, bit in rest:
            self.stages.append(("full", at.pair(axis, bit)[0], rows, offset, offset, place))
            place += rows
        self.count = len(self.stages)
        self.back = [s for s in range(self.count) if self.stages[s][0] != "full"][::-1]

    @staticmethod
    def placed(rows, order, planes, rest):
        total = 0
        for axis, _ in order:
            share = rows // planes if axis == "planes" else rows // 2
            total, rows = total + rows - share, share
        return total + rest * rows

    def copies(self, s, back=False, receive=False):
        kind, to, n, give, keep, place = self.stages[s]
        at, out = self.at, self.out
        w = 1 if back else 0
        if kind == "planes":
            found = []
            for k in range(1, at.planes):
                if back:
                    which = at.plane_source(k) if receive else at.plane
                    span = rows_of(give + which * n + self.shift, n)
                    src, dst = out.at[span], out.at[span]
                else:
                    src, dst = (ref.at[rows_of(place + (k - 1) * n, n)] for ref in (self.sent, self.came))
                to = at.in_line(at.plane_peer(k))
                found.append(send_to(src, dst, self.sems.at[w, 0, s, k], self.sems.at[w, 1, s, k], to))
            return found
        if back:
            span = rows_of((give if receive else keep) + self.shift, n)
            src, dst = out.at[span], out.at[span]
        else:
            src, dst = self.sent.at[rows_of(place, n)], self.came.at[rows_of(place, n)]
        return [send_to(src, dst, self.sems.at[w, 0, s, 0], self.sems.at[w, 1, s, 0], to)]

    def pack(self, give, place, n):
        def run(i, step):
            self.sent[rows_at(place, i, step), :] = self.acc[rows_at(give, i, step), :].astype(BF16)
        over_rows(n, run)

    def start(self, s):
        kind, to, n, give, keep, place = self.stages[s]
        if kind == "planes":
            for k in range(1, self.at.planes):
                self.pack(give + self.at.plane_peer(k) * n, place + (k - 1) * n, n)
        else:
            self.pack(give, place, n)
        for copy in self.copies(s):
            copy.start()

    def finish(self, s):
        kind, to, n, give, keep, place = self.stages[s]
        for copy in self.copies(s):
            copy.wait_recv()
        parts = self.at.planes - 1 if kind == "planes" else 1
        last = s == self.count - 1

        def run(i, step):
            total = self.acc[rows_at(keep, i, step), :]
            if kind == "full":
                total = total.astype(BF16).astype(F32)
            for k in range(parts):
                total = total + self.came[rows_at(place + k * n, i, step), :].astype(F32)
            if last:
                self.out[rows_at(keep + self.shift, i, step), :] = total.astype(BF16)
            else:
                self.acc[rows_at(keep, i, step), :] = total
        over_rows(n, run)

    def start_back(self, s):
        for copy in self.copies(s, back=True):
            copy.start()

    def finish_back(self, s):
        for copy in self.copies(s, back=True, receive=True):
            copy.wait_recv()

    def events(self, back):
        def first():
            self.start(0)

        def inward(s):
            self.finish(s)
            if s + 1 < self.count:
                self.start(s + 1)
            elif back:
                self.start_back(back[0])

        def outward(d):
            self.finish_back(back[d])
            if d + 1 < len(back):
                self.start_back(back[d + 1])

        return ([first] + [functools.partial(inward, s) for s in range(self.count)]
                + [functools.partial(outward, d) for d in range(len(back))])

    def drain(self, back):
        for s in range(self.count):
            for copy in self.copies(s):
                copy.wait_send()
        for s in back:
            for copy in self.copies(s, back=True):
                copy.wait_send()


def row_mean(value):
    return jnp.mean(value, axis=1, keepdims=True)


def col_sum(value):
    return jnp.sum(value, axis=0, keepdims=True)


def main_kernel(docs, blocks, group, cuts, k_block, q_tile,
                att_in, cot_ref, len_ref, wo_ref, ob_ref, g1_ref, s1_ref, up_hbm, ub_ref, down_hbm,
                db_ref, g2_ref, s2_ref, wq_hbm, wk_hbm, wv_hbm, q_hbm, k_hbm, v_hbm, o_hbm, tok_hbm,
                out_in, grad_in, sum_ref, qkv_ref, small_out,
                wq_ref, wk_ref, wv_ref, q_ref, k_ref, v_ref, o_ref, tok_ref, att, hid_t, gz, away, kv_in, gq_in, g_att, g_in, qx, gx, qt, gt, kv_send, gq_send,
                acc, sent, came, dwt, sent_w, came_w, bias, small_sent, small_came,
                g_sems, kv_sems, gq_sems, sum_sems, w_sems, small_sems, wide_sems, core_sems, load_sems,
                out_sems, grad_sems, enter_sems):
    at = Place(docs, blocks, group)
    me, member, plane, planes = at.me, at.member, at.plane, at.planes
    _, rows, width = tok_ref.shape
    count = planes * rows
    cols = width // group
    inner_width = up_hbm.shape[1]
    heads, length_all, _ = q_ref.shape
    parts = inner_width // width
    doc_bits = bits_of(docs)

    loads = [pltpu.make_async_copy(up_hbm.at[:, c * width:(c + 1) * width],
                                   sent.at[inner_width + c * width:inner_width + (c + 1) * width], load_sems.at[c])
             for c in range(parts)]
    loads.append(pltpu.make_async_copy(down_hbm, sent.at[:inner_width], load_sems.at[parts]))
    enter = [pltpu.make_async_copy(src, dst, enter_sems.at[i]) for i, (src, dst) in enumerate((
        (tok_hbm, tok_ref), (q_hbm, q_ref), (o_hbm, o_ref), (k_hbm, k_ref), (v_hbm, v_ref),
        (wq_hbm, wq_ref), (wk_hbm, wk_ref), (wv_hbm, wv_ref)))]
    for load in enter[:1] + loads + enter[1:]:
        load.start()

    def up_part(c):
        return sent[inner_width + c * width:inner_width + (c + 1) * width, :]

    all_here = greet([at.in_plane(at.member_peer(k)) for k in range(1, group)]
                     + [at.in_line(at.plane_peer(k)) for k in range(1, planes)]
                     + [at.pair("docs", bit)[0] for bit in doc_bits])

    rest = [("docs", bit) for bit in doc_bits[1:]]
    sums, place = [], 0
    for c, (offset, size, order) in enumerate(cuts):
        sums.append(Summer(at, acc, sent, came, sum_ref, place, offset, size, order, rest, sum_sems.at[c]))
        place = place + Summer.placed(size, order, planes, len(rest))
    chains = [s.events(s.back) for s in sums]
    at_event = [0] * len(cuts)

    def upcoming(numbers):
        found = []
        for c in numbers:
            if c < len(chains) and at_event[c] < len(chains[c]):
                found.append(chains[c][at_event[c]])
                at_event[c] += 1
        return found

    def advance(numbers):
        for event in upcoming(numbers):
            event()

    enter[0].wait()
    flat = jnp.concatenate([tok_ref[p * group + member].astype(F32) for p in range(planes)], axis=0)
    for p in range(planes):
        for g in range(group):
            att[p * rows:(p + 1) * rows, g * cols:(g + 1) * cols] = att_in[g, p]
    up_bias = row(ub_ref)
    gain1, gain2 = row(g1_ref), row(g2_ref)
    summed = flat + mm(att[...], wo_ref[...]) + row(ob_ref)
    centred = summed - row_mean(summed)
    rstd1 = lax.rsqrt(row_mean(centred * centred) + EPS)
    xhat1 = centred * rstd1
    hidden = xhat1 * gain1 + row(s1_ref)
    hidden_low = hidden.astype(BF16)
    hid_t[...] = hidden_low.T
    for load in loads:
        load.wait()
    ffn = jnp.zeros((count, width), F32)
    for c in range(parts):
        span = slice(c * width, (c + 1) * width)
        inner = mm(hidden_low, up_part(c)) + up_bias[:, span]
        square = inner * inner
        slope_in = 0.7978845608 * (1.0 + (3 * 0.044715) * square)
        tanh = jnp.tanh(inner * (0.7978845608 * (1.0 + 0.044715 * square)))
        half = 0.5 * (1.0 + tanh)
        acc[c * count:(c + 1) * count, :] = half + (0.5 * inner) * ((1.0 - tanh * tanh) * slope_in)
        low = (inner * half).astype(BF16)
        sum_ref[c * count:(c + 1) * count, :] = low
        ffn = ffn + mm(low, sent[span, :])
    summed = flat + hidden + ffn + row(db_ref)
    centred = summed - row_mean(summed)
    rstd2 = lax.rsqrt(row_mean(centred * centred) + EPS)
    xhat2 = centred * rstd2
    away[...] = (xhat2 * gain2 + row(s2_ref)).astype(BF16).reshape(planes, rows, width)

    def line_copies(dst, sems, receive=False):
        return [send_to(away.at[at.plane_peer(k)], dst.at[at.plane_source(k) if receive else plane],
                        sems.at[0, k], sems.at[1, k], at.in_line(at.plane_peer(k))) for k in range(1, planes)]

    all_here()
    for copy in line_copies(out_in, out_sems):
        copy.start()
    out_in[plane] = away[plane]
    lane_r = lax.broadcasted_iota(jnp.int32, (rows, width), 0)
    g_out = jnp.concatenate(
        [jnp.where((p * group + member) * rows + lane_r < len_ref[plane], cot_ref[p].astype(F32), 0.0)
         for p in range(planes)], axis=0)
    small_sent[0] = jnp.zeros(small_sent.shape[1:], F32)
    small_sent[0, 0:1, :] = col_sum(g_out * xhat2)
    small_sent[0, 1:2, :] = col_sum(g_out)
    scaled = g_out * gain2
    g_z2 = rstd2 * (scaled - row_mean(scaled) - xhat2 * row_mean(scaled * xhat2))
    g_ffn = g_z2.astype(BF16)
    small_sent[0, 2:3, :] = col_sum(g_ffn.astype(F32))
    g_hidden = g_z2
    for c in range(parts):
        span = slice(c * width, (c + 1) * width)
        g_inner = (mm_nt(g_ffn, sent[span, :]) * acc[c * count:(c + 1) * count, :]).astype(BF16)
        sum_ref[inner_width + c * count:inner_width + (c + 1) * count, :] = g_inner
        g_hidden = g_hidden + mm_nt(g_inner, up_part(c))
    scaled = g_hidden * gain1
    g_z1 = rstd1 * (scaled - row_mean(scaled) - xhat1 * row_mean(scaled * xhat1))
    g_branch = g_z1.astype(BF16)
    gz[...] = g_z1 + g_z2
    g_low = mm_nt(g_branch, wo_ref[...]).astype(BF16)
    for p in range(planes):
        for g in range(group):
            g_att[g, p] = g_low[p * rows:(p + 1) * rows, g * cols:(g + 1) * cols]

    def g_copy(k, receive=False):
        slot = at.member_source(k) if receive else member
        return send_to(g_att.at[at.member_peer(k)], g_in.at[:, slot], g_sems.at[0, k], g_sems.at[1, k],
                       at.in_plane(at.member_peer(k)))

    for k in range(1, group):
        g_copy(k).start()
    for p in range(planes):
        g_in[p, member] = g_att[member, p]

    for c in range(parts):
        span = slice(c * width, (c + 1) * width)
        acc[span, :] = mm_tn(sum_ref[c * count:(c + 1) * count, :], g_ffn)
    advance(POINTS[0])
    for c in range(parts):
        g_inner = sum_ref[inner_width + c * count:inner_width + (c + 1) * count, :]
        small_sent[0, 6 + c:7 + c, :] = col_sum(g_inner.astype(F32))
        acc[inner_width + c * width:inner_width + (c + 1) * width, :] = mm(hid_t[...], g_inner)
    acc[2 * inner_width:2 * inner_width + width, :] = mm_tn(att[...], g_branch)
    if acc.shape[0] > 2 * inner_width + width:
        acc[2 * inner_width + width:, :] = jnp.zeros((acc.shape[0] - 2 * inner_width - width, width), F32)
    advance(POINTS[1])
    small_sent[0, 3:4, :] = col_sum(g_hidden * xhat1)
    small_sent[0, 4:5, :] = col_sum(g_hidden)
    small_sent[0, 5:6, :] = col_sum(g_branch.astype(F32))
    chunk = group * rows
    lane = lax.broadcasted_iota(jnp.int32, (chunk, LANES), 1)

    for load in enter[1:]:
        load.wait()

    def prepare_q(step, carry):
        span = pl.ds(pl.multiple_of(step * chunk, chunk), chunk)
        for h in range(heads):
            q_rows = q_ref[h, span, :].astype(F32)
            ext = q_rows
            for i, value in enumerate(three(-o_ref[h, span, HD:HD + 1])):
                ext = jnp.where(lane == HD + 1 + i, value, ext)
            qx[h, span, :] = ext.astype(BF16)
            qt[h, :, span] = q_rows[:, :HD].T.astype(BF16)
        return carry

    lax.fori_loop(0, planes, prepare_q, 0)
    advance(POINTS[2])
    for k in range(1, group):
        g_copy(k, True).wait_recv()

    def prepare_g(step, carry):
        span = pl.ds(pl.multiple_of(step * chunk, chunk), chunk)
        g_block = g_in[step].reshape(chunk, cols)
        for h in range(heads):
            g_rows = g_block[:, h * HD:(h + 1) * HD].astype(F32)
            g_rows = jnp.concatenate([g_rows, jnp.zeros_like(g_rows)], axis=1)
            delta = jnp.sum(g_rows * o_ref[h, span, :], axis=1, keepdims=True)
            ext = g_rows
            for i, value in enumerate(three(-delta)):
                ext = jnp.where(lane == HD + i, value, ext)
            gx[h, span, :] = ext.astype(BF16)
            gt[h, :, span] = g_rows[:, :HD].T.astype(BF16)
        return carry

    lax.fori_loop(0, planes, prepare_g, 0)
    advance(POINTS[3])

    gq_acc = o_ref.at[0]
    k_blocks = length_all // k_block
    per_block = k_block // rows
    ones = jnp.ones((8, k_block), BF16)
    dwt[...] = jnp.zeros_like(dwt)
    bias[...] = jnp.zeros_like(bias)

    def kv_copy(h, p, g, slot, r):
        return send_to(kv_send.at[h, p, g], kv_in.at[slot, h, p], kv_sems.at[0, h, p, r], kv_sems.at[1, h, p, r],
                       at.in_plane(g))

    def gq_copy(h, r, receive=False):
        slot = at.member_source(r) if receive else member
        return send_to(gq_send.at[h, :, at.member_peer(r)], gq_in.at[slot, h], gq_sems.at[0, h, r],
                       gq_sems.at[1, h, r], at.in_plane(at.member_peer(r)))

    total_steps = heads * k_blocks
    timed = [(t, event) for t in range(min(total_steps, len(AT_BLOCK))) for event in upcoming(AT_BLOCK[t])]

    def block(step, carry):
        h, i = step // k_blocks, lax.rem(step, k_blocks)
        which = lax.rem(i + member // per_block + 1, k_blocks)
        span = pl.ds(pl.multiple_of(which * k_block, k_block), k_block)
        k_rows, v_rows = k_ref[h, span, :], v_ref[h, span, :]

        @pl.when(i == 0)
        def _():
            gq_acc[...] = jnp.zeros_like(gq_acc)

        gk = jnp.zeros((HD, k_block), F32)
        gv = jnp.zeros((HD, k_block), F32)
        tiles = [slice(t, t + q_tile) for t in range(0, length_all, q_tile)]

        def products(tile):
            return mm_nt(qx[h, tile, :], k_rows), mm_nt(gx[h, tile, :], v_rows)

        ahead = products(tiles[0])
        for tile, later in zip(tiles, tiles[1:] + [None]):
            scores, centred = ahead
            ahead = products(later) if later else None
            weights = jnp.exp(scores)
            g_scores = (weights * centred).astype(BF16)
            gv = gv + mm(gt[h, :, tile], weights.astype(BF16))
            gk = gk + mm(qt[h, :, tile], g_scores)
            gq_acc[tile, :] += mm(g_scores, k_rows)
        kv = jnp.concatenate([gk, gv], axis=0).astype(BF16)
        tok_rows = tok_ref[pl.ds(which * per_block, per_block)].reshape(k_block, width)
        dwt[pl.ds(pl.multiple_of(h * 2 * HD, 2 * HD), 2 * HD), :] += mm(kv, tok_rows)
        bias[h, 0] += mm_nt(ones, kv[HD:])
        for u in range(per_block):
            d = which * per_block + u
            p, g = d // group, lax.rem(d, group)
            kv_send[h, p, g] = kv[:, u * rows:(u + 1) * rows]

            @pl.when(g != member)
            def _():
                kv_copy(h, p, g, member, lax.rem(g + group - member, group)).start()

            @pl.when(g == member)
            def _():
                kv_in[member, h, p] = kv[:, u * rows:(u + 1) * rows]

        @pl.when(i == k_blocks - 1)
        def _():
            for n in range(blocks):
                gq_send[h, n // group, n % group] = (
                    gq_acc[n * rows:(n + 1) * rows, :HD] * (HD ** -0.5)).T.astype(BF16)
            for r in range(1, group):
                gq_copy(h, r).start()
            for p in range(planes):
                gq_in[member, h, p] = gq_send[h, p, member]

        for t, event in timed:
            pl.when(step == t)(event)
        return carry

    lax.fori_loop(0, total_steps, block, 0)

    q_base = heads * 2 * HD
    for h in range(heads):
        part = jnp.zeros((HD, width), F32)
        q_bias = jnp.zeros((8, HD), F32)
        for n in range(blocks):
            low = gq_send[h, n // group, n % group]
            part = part + mm(low, tok_ref[n])
            q_bias = q_bias + mm_nt(jnp.ones((8, rows), BF16), low)
        dwt[q_base + h * HD:q_base + (h + 1) * HD, :] = part
        bias[h, 1] = q_bias
    half = dwt.shape[0] // 2
    my_core = lax.rem(at.doc, 2)
    w_sum = Summer(at, dwt, sent_w, came_w, qkv_ref, 0, 0, 2 * half, W_ORDER, rest, w_sems,
                   out_shift=my_core * (half * group - half) + member * half)
    w_line = next(s for s in w_sum.back if w_sum.stages[s][0] == "planes")
    share = half // planes
    w_chain = w_sum.events([])
    lane_w = lax.broadcasted_iota(jnp.int32, (8, width), 1)
    sub = lax.broadcasted_iota(jnp.int32, (8, width), 0)
    wide = [jnp.concatenate([bias[h, i] for h in range(heads)] * group, axis=1) for i in range(2)]
    small_sent[0, 16:24, :] = jnp.where(
        (lane_w // cols) == member, jnp.where(sub == 0, wide[1], jnp.where(sub == 1, wide[0], 0.0)), 0.0)
    small_order = [("docs", 1)] + [("blk", bit) for bit in bits_of(group)]

    def small_copy(s):
        return send_to(small_sent.at[s], small_came.at[s], small_sems.at[0, s], small_sems.at[1, s],
                       at.pair(*small_order[s])[0])

    small_last = len(small_order)

    def small_line(k, receive=False):
        slot = small_last + k
        return send_to(small_sent.at[small_last], small_came.at[slot], small_sems.at[0, slot],
                       small_sems.at[1, slot], at.in_line(at.plane_peer(k)))

    def small_rest(i):
        slot = small_last + planes + i
        return send_to(small_sent.at[small_last + 1 + i], small_came.at[slot], small_sems.at[0, slot],
                       small_sems.at[1, slot], at.pair(*rest[i])[0])

    def small_step(s):
        small_copy(s).wait_recv()
        small_sent[s + 1] = small_sent[s] + small_came[s]
        if s + 1 < small_last:
            small_copy(s + 1).start()
        else:
            for k in range(1, planes):
                small_line(k).start()

    def small_end():
        for k in range(1, planes):
            small_line(k).wait_recv()
        total = jnp.zeros(small_sent.shape[1:], F32)
        for p in range(planes):
            value = small_sent[small_last]
            for k in range(1, planes):
                value = jnp.where(at.plane_source(k) == p, small_came[small_last + k], value)
            total = total + value
        for i in range(len(rest)):
            small_sent[small_last + 1 + i] = total
            small_rest(i).start()
            small_rest(i).wait_recv()
            total = total + small_came[small_last + planes + i]
        small_out[...] = total

    def slab(core, m, p=0, n=half):
        return qkv_ref.at[rows_of(core * half * group + m * half + p * share, n)]

    def wide_copy(k, j, m):
        piece = slab(my_core, m, at.plane_source(j), share)
        return send_to(piece, piece, wide_sems.at[0, k, j], wide_sems.at[1, k, j], at.in_plane(at.member_peer(k)))

    def core_copy(k, core):
        piece = slab(core, at.member_source(k))
        return send_to(piece, piece, core_sems.at[0, k], core_sems.at[1, k], at.pair("docs", 1)[0])

    def w_out():
        w_chain[-1]()
        w_sum.start_back(w_line)
        for k in range(1, group):
            wide_copy(k, 0, member).start()

    def w_forward():
        for j, copy in enumerate(w_sum.copies(w_line, back=True, receive=True)):
            copy.wait_recv()
            for k in range(1, group):
                wide_copy(k, j + 1, member).start()
        core_copy(0, my_core).start()

    def w_slabs():
        for k in range(1, group):
            for j in range(planes):
                wide_copy(k, j, at.member_source(k)).wait_recv()
            core_copy(k, my_core).start()

    def gather_part(which):
        for p in range(planes):
            for g in range(group):
                for h in range(heads):
                    low = gq_in[g, h, p] if which == 0 else kv_in[g, h, p, (which - 1) * HD:which * HD, :]
                    hid_t[g * cols + h * HD:g * cols + (h + 1) * HD, p * rows:(p + 1) * rows] = low
        return hid_t[...].T

    def key_value_rows():
        for h in range(heads):
            for p in range(planes):
                for r in range(1, group):
                    kv_copy(h, p, member, at.member_source(r), r).wait_recv()
        gz[...] += mm_nt(gather_part(1), wk_ref[...])
        gz[...] += mm_nt(gather_part(2), wv_ref[...])

    def query_rows():
        for h in range(heads):
            for r in range(1, group):
                gq_copy(h, r, True).wait_recv()
        total = gz[...] + mm_nt(gather_part(0), wq_ref[...])
        for copy in line_copies(out_in, out_sems, True):
            copy.wait_recv()
        for copy in line_copies(out_in, out_sems):
            copy.wait_send()
        away[...] = total.astype(BF16).reshape(planes, rows, width)
        for copy in line_copies(grad_in, grad_sems):
            copy.start()
        grad_in[plane] = away[plane]

    w_events = w_chain[:-1] + [w_out, w_forward, w_slabs]
    small_events = [small_copy(0).start] + [functools.partial(small_step, s) for s in range(small_last)] + [small_end]
    named = {"w": w_events, "g": [key_value_rows, query_rows], "s": small_events}
    for name in AFTER:
        if name in named:
            if named[name]:
                named[name].pop(0)()
        else:
            advance((name,))
    while any(named.values()) or any(at_event[c] < len(chains[c]) for c in range(len(cuts))):
        for work in named.values():
            if work:
                work.pop(0)()
        advance(range(len(cuts)))
    for k in range(group):
        core_copy(k, 1 - my_core).wait_recv()
    for copy in line_copies(grad_in, grad_sems, True):
        copy.wait_recv()
    for copy in line_copies(grad_in, grad_sems):
        copy.wait_send()
    for r in range(1, group):
        g_copy(r).wait_send()
        for h in range(heads):
            gq_copy(h, r).wait_send()
            for p in range(planes):
                kv_copy(h, p, at.member_peer(r), member, r).wait_send()
    for part in sums:
        part.drain(part.back)
    w_sum.drain([w_line])
    for k in range(group):
        core_copy(k, my_core).wait_send()
        for j in range(planes if k else 0):
            wide_copy(k, j, member).wait_send()
    for s in range(small_last):
        small_copy(s).wait_send()
    for k in range(1, planes):
        small_line(k).wait_send()
    for i in range(len(rest)):
        small_rest(i).wait_send()


def member_bits(group, name):
    bits = bits_of(group)
    return bits[:len(bits) // 2] if name == "x" else bits[len(bits) // 2:]


SUMS = ((2, ("xyz", "yxz")), (4, ("yxz", "zxy", "xyz", "xyz")))
W_ORDER = [("docs", 1), ("planes", 0)]
POINTS = ((0, 1,), (0, 4, 1, 2, 3, 5,), (4, 3, 5, 2, 0,), (1,))
AT_BLOCK = ((), (3, 0, 4,), (1, 5, 2, 4, 0, 3,),
            (2, 1, 5, 3,), (0,), (2, 3, 4, 1,),
            (5, 3, 0,), ())
AFTER = ("w", 4, 5, "s", "w", 2, 1, 0, 4, 3, "s", "g", "w", 5, 2, "g", "s", "w", 4, 5, 1, 1, 2, "s", 0, 5,
         "w", 2, 3, 4, "g", "w", "s",)


def main(docs, blocks, group, att_in, cotangent, lengths, weights, attention, tok_doc, collective_id,
         k_block=512, q_tile=256):
    q = attention[0]
    heads, length_all, _ = q.shape
    _, rows, width = tok_doc.shape
    planes = blocks // group
    count = planes * rows
    cols = heads * HD
    inner_width = weights[4].shape[1]
    features = -(-3 * cols // 128) * 128
    unit = 32 * blocks
    second = -(-(inner_width + width) // unit)
    cuts, offset = [], 0
    for (pieces, turns), units in zip(SUMS, (inner_width // unit, second)):
        pieces = min(pieces, units)
        for i in range(pieces):
            size = unit * (units // pieces + (1 if i >= pieces - units % pieces else 0))
            cuts.append((offset, size, [("docs", 1)] + [
                step for name in turns[i] for step in (
                    [("planes", 0)] if name == "z" else [("blk", bit) for bit in member_bits(group, name)])]))
            offset += size
    total = inner_width + second * unit
    members, rest = len(bits_of(group)), len(bits_of(docs)) - 1
    placed = sum(Summer.placed(size, order, planes, rest) for _, size, order in cuts)
    w_placed = Summer.placed(features, W_ORDER, planes, rest)
    stages = 2 + members + rest
    steps = 1 + members + planes + rest
    dma, vmem = pltpu.SemaphoreType.DMA, pltpu.VMEM
    return pl.pallas_call(
        functools.partial(main_kernel, docs, blocks, group, cuts, k_block, q_tile),
        out_shape=(
            jax.ShapeDtypeStruct((planes, rows, width), BF16),
            jax.ShapeDtypeStruct((planes, rows, width), BF16),
            jax.ShapeDtypeStruct((total, width), BF16),
            jax.ShapeDtypeStruct((features * group, width), BF16),
            jax.ShapeDtypeStruct((24, width), F32),
        ),
        in_specs=[VMEM] * 2 + [SMEM] + [VMEM] * 4 + [ANY, VMEM, ANY] + [VMEM] * 3 + [ANY] * 8,
        out_specs=(VMEM,) * 5,
        scratch_shapes=[
            *(vmem((width, width), BF16) for _ in range(3)),
            *(vmem(array.shape, array.dtype) for array in (*attention, tok_doc)),
            vmem((count, width), BF16),
            vmem((width, count), BF16),
            vmem((count, width), F32),
            vmem((planes, rows, width), BF16),
            vmem((group, heads, planes, 2 * HD, rows), BF16),
            vmem((group, heads, planes, HD, rows), BF16),
            vmem((group, planes, rows, cols), BF16),
            vmem((planes, group, rows, cols), BF16),
            vmem((heads, length_all, LANES), BF16),
            vmem((heads, length_all, LANES), BF16),
            vmem((heads, HD, length_all), BF16),
            vmem((heads, HD, length_all), BF16),
            vmem((heads, planes, group, 2 * HD, rows), BF16),
            vmem((heads, planes, group, HD, rows), BF16),
            vmem((total, width), F32),
            vmem((max(placed, 2 * inner_width), width), BF16),
            vmem((placed, width), BF16),
            vmem((features, width), F32),
            vmem((w_placed, width), BF16),
            vmem((w_placed, width), BF16),
            vmem((heads, 2, 8, HD), F32),
            vmem((steps, 24, width), F32),
            vmem((steps, 24, width), F32),
            dma((2, group)),
            dma((2, heads, planes, group)),
            dma((2, heads, group)),
            dma((len(cuts), 2, 2, stages, planes)),
            dma((2, 2, 2 + rest, planes)),
            dma((2, steps)),
            dma((2, group, planes)),
            dma((2, group)),
            dma((inner_width // width + 1,)),
            dma((2, planes)),
            dma((2, planes)),
            dma((8,)),
        ],
        compiler_params=params(collective_id),
    )(att_in, cotangent, lengths, *weights, *attention, tok_doc)


def last_kernel(group, heads, out_in, grad_in, sum_in, qkv_in, small_ref,
                out_ref, grad_ref, qw_ref, qb_ref, kw_ref, vw_ref, vb_ref, ow_ref, ob_ref, g1_ref, s1_ref,
                uw_ref, ub_ref, dw_ref, db_ref, g2_ref, s2_ref, rows_low, sums_low, qkv_low, stack, wide, come, go):
    width = ow_ref.shape[0]
    inner_width = uw_ref.shape[1]
    cols = width // group
    parts = inner_width // width
    spans = [slice(i * width, (i + 1) * width) for i in range(2 * parts + 1)]
    arrive = [pltpu.make_async_copy(sum_in.at[span], sums_low.at[span], come.at[i]) for i, span in enumerate(spans)]
    late = [pltpu.make_async_copy(qkv_in, qkv_low, come.at[len(spans)])]
    late += [pltpu.make_async_copy(src, rows_low.at[i], come.at[len(spans) + 1 + i])
             for i, src in enumerate((out_in, grad_in))]
    for copy in arrive + late:
        copy.start()
    targets = ([dw_ref.at[span] for span in spans[:parts]] + [uw_ref.at[:, span] for span in spans[:parts]] + [ow_ref])
    leaving = []

    def leave(slot, target):
        copy = pltpu.make_async_copy(wide.at[slot], target, go.at[slot])
        copy.start()
        leaving.append(copy)

    for i, span in enumerate(spans):
        arrive[i].wait()
        wide[i] = sums_low[span, :].astype(F32)
        leave(i, targets[i])
    for copy in late:
        copy.wait()
    slot = len(spans)
    planes, rows = out_ref.shape[0], out_ref.shape[1]
    for i, out in enumerate((out_ref, grad_ref)):
        for p in range(planes):
            wide[slot, p * rows:(p + 1) * rows, :] = rows_low[i, p].astype(F32)
            copy = pltpu.make_async_copy(wide.at[slot, p * rows:(p + 1) * rows], out.at[p], go.at[slot + 3 + i * planes + p])
            copy.start()
            leaving.append(copy)
        slot += 1
    half = qkv_low.shape[0] // group // 2
    unit = HD // 2
    for which, out in enumerate((qw_ref, kw_ref, vw_ref)):
        for g in range(group):
            for h in range(heads):
                first = heads * 2 * HD + h * HD if which == 0 else h * 2 * HD + (which - 1) * HD
                for u in range(2):
                    f = first + u * unit
                    at = f // half * half * group + g * half + f % half
                    to = g * cols + h * HD + u * unit
                    stack[to:to + unit, :] = qkv_low[at:at + unit, :]
        wide[slot] = stack[...].T.astype(F32)
        copy = pltpu.make_async_copy(wide.at[slot], out, go.at[len(spans) + which])
        copy.start()
        leaving.append(copy)
        slot += 1

    def vector(out, i):
        out[...] = small_ref[i:i + 1, :].reshape(out.shape)

    for i, out in ((16, qb_ref), (17, vb_ref), (0, g2_ref), (1, s2_ref), (2, db_ref), (3, g1_ref), (4, s1_ref),
                   (5, ob_ref)):
        vector(out, i)
    ub_ref[...] = jnp.concatenate([small_ref[6 + i:7 + i, :] for i in range(parts)], axis=1).reshape(ub_ref.shape)
    for copy in leaving:
        copy.wait()


def last(group, shape, inner_width, *arrays):
    slots, rows, width = shape
    heads = width // group // HD
    parts = 2 * inner_width // width + 1
    whole = jax.ShapeDtypeStruct(shape, F32)
    square = jax.ShapeDtypeStruct((width, width), F32)
    vector = jax.ShapeDtypeStruct((width,), F32)
    dma, vmem = pltpu.SemaphoreType.DMA, pltpu.VMEM
    shapes = (whole, whole, square, vector, square, square, vector, square, vector, vector, vector,
              jax.ShapeDtypeStruct((width, inner_width), F32), jax.ShapeDtypeStruct((inner_width,), F32),
              jax.ShapeDtypeStruct((inner_width, width), F32), vector, vector, vector)
    return pl.pallas_call(
        functools.partial(last_kernel, group, heads),
        out_shape=shapes,
        in_specs=[ANY] * 4 + [VMEM],
        out_specs=tuple(VMEM if len(shape.shape) == 1 else ANY for shape in shapes),
        scratch_shapes=[
            vmem((2, slots, rows, width), BF16),
            vmem((parts * width, width), BF16),
            vmem(arrays[3].shape, BF16),
            vmem((width, width), BF16),
            vmem((parts + 5, max(width, slots * rows), width), F32),
            dma((parts + 3,)),
            dma((parts + 5 + 2 * slots,)),
        ],
        compiler_params=params(),
    )(*arrays)


def device_program(docs, blocks, tokens, query_weight, query_bias, key_weight, value_weight, value_bias,
                   out_weight, out_bias, first_gain, first_shift, up_weight, up_bias, down_weight,
                   down_bias, second_gain, second_shift, cotangent, lengths):
    slots, rows, width = tokens.shape
    inner_width = up_weight.shape[1]
    group = blocks // slots
    projections = (query_weight, key_weight, value_weight)
    tok_doc, cot, att_in, q, k, v, o = first(tokens, cotangent, projections, (query_bias, value_bias), lengths,
                                             blocks, 0)
    parts = main(
        docs, blocks, group, att_in, cot, lengths,
        (out_weight, out_bias, first_gain, first_shift, up_weight, up_bias, down_weight, down_bias,
         second_gain, second_shift, *projections), (q, k, v, o), tok_doc, 1)
    return last(group, tokens.shape, inner_width, *parts)


def solution(mesh):
    split = P("docs", "blk", None)
    return jax.shard_map(
        functools.partial(device_program, mesh.shape["docs"], mesh.shape["blk"]),
        mesh=mesh,
        in_specs=(split,) + (P(),) * 15 + (split, P("docs")),
        out_specs=(split, split) + (P(),) * 15,
        check_vma=False,
    )
```
